32 devices in a mesh: blk: 4 (over z), sub: 8 (over y, x, core).
Axes of the slice: x: 2, y: 2, z: 4, core: 2. Of those that a mesh axis runs over, the one named last changes fastest.
Arguments:
- right_side: float32 [64, 8192], P(None, ('blk', 'sub')), may hold values from -8 to 8
- conductivity: float32 [8192], P(('blk', 'sub')), may hold values from 1 to 8
- material: int32 [8192], P(('blk', 'sub')), may hold values 0 or 1
- stiffness: float32 [2, 64, 64], replicated, may hold values from -0.0223 to 2.5, as said below
- trace_map: float32 [96, 64], replicated, may hold values from -0.75 to 0.75
- face_neighbour: int32 [6, 8192], P(None, ('blk', 'sub')), may hold values from 0 to 1680
- sub_sends: int32 [32, 128], P(('blk', 'sub')), may hold values from 0 to 1535
- blk_sends: int32 [32, 16], P(('blk', 'sub')), may hold values from 0 to 1535
- group_sizes: int32 [32, 64], P(('blk', 'sub')), may hold values from 1 to 8, 256 in all within a row
- coarse_conductivity: float32 [2048], P(('blk', 'sub')), may hold values from 1 to 8
- coarse_stiffness: float32 [64, 64], replicated, may hold values from -0.0223 to 2.5, as said below
- restriction: float32 [8, 64, 64], replicated, may hold values from -0.5 to 0.5
Outputs:
- solution_field: float32 [64, 8192], P(None, ('blk', 'sub'))
- residual: float32 [64, 8192], P(None, ('blk', 'sub'))
The draws below stay inside these ranges and needn't reach their ends.
Inputs may be any that keep to these rules, and one draw needn't show every extreme that they name: `group_sizes`: each row sums to 256, and some entry of each row is 8. `stiffness`: symmetric. `coarse_stiffness`: symmetric.
All inputs are finite; a program needn't handle non-finite values. No bound on the sum of `material` on one device may be relied on, other than what follows from the above.
Results may differ from the reference program's by a relative error of at most 0.0003.
Values sent between devices are 32-bit elements; how exact they have to be, the bound alone decides.
No kernel may reach another device: no remote copies, remote signals or barrier semaphores. Data moves between devices by JAX's collectives and lax.ppermute only.
A program may use at most 64 MiB of HBM per device.

```python
import math
import jax
import jax.numpy as jnp
import numpy as np
from jax import lax

M = 64
Q = 16
E_DEV = 256
CAP = 16
CAPB = 8
HEAD = 8
KF = 3
KC = 4
P_DEV = 64
ELEMS = 8192
GROUPS = 2048
TABLE = 1681
N_BLK = 4
N_SUB = 8


def dominant(key, copies, matrix_order):
    diag_key, off_key = jax.random.split(key)
    diagonal = jax.random.uniform(diag_key, (copies, matrix_order), jnp.float32, 1.5, 2.5)
    random_part = jax.random.uniform(off_key, (copies, matrix_order, matrix_order), jnp.float32, -1.0, 1.0)
    bound_off = 1.4 / (matrix_order - 1)
    off_diag = 0.5 * bound_off * (random_part + jnp.transpose(random_part, (0, 2, 1)))
    identity = jnp.eye(matrix_order, dtype=jnp.float32)
    return off_diag * (1.0 - identity) + diagonal[:, :, None] * identity


def draw_stiffness(key, part):
    key = jax.random.fold_in(key, 11)
    return dominant(key, 2, M)


def draw_coarse_stiffness(key, part):
    key = jax.random.fold_in(key, 12)
    return dominant(key, 1, M)[0]


def touch_ends(array, rng, smallest, top_value):
    index_at = [jax.random.randint(jax.random.fold_in(rng, axis), (), 0, length) for axis, length in enumerate(array.shape)]
    widest = array.shape.index(max(array.shape))
    next_to = index_at[:widest] + [(index_at[widest] + 1) % array.shape[widest]] + index_at[widest + 1:]
    return array.at[tuple(index_at)].set(smallest).at[tuple(next_to)].set(top_value)


def block_levels(stream_key, extent, cuts, low, top_value):
    def one(dim, blocks):
        steps = jax.random.uniform(jax.random.fold_in(jax.random.fold_in(stream_key, 6), dim), (blocks,), jnp.float32, low / len(cuts), top_value / len(cuts))
        return jnp.repeat(jnp.exp(steps), extent[dim] // blocks).reshape((-1,) + (1,) * (len(extent) - dim - 1))

    factor_of = one(*cuts[0])
    for cut in cuts[1:]:
        factor_of = factor_of * one(*cut)
    return factor_of


def profile(count, total, bound, lean):
    portions = [(1 << 20) // math.isqrt(standing ** lean) + 1 for standing in range(2, count + 1)]
    spare, counts = total - bound - (count - 1), [1] * (count - 1)
    while spare > 0:
        candidates = [i for i in range(count - 1) if counts[i] < bound]
        pool, budget = sum([portions[i] for i in candidates]), spare
        for i in candidates:
            more = min(bound - counts[i], max(1, budget * portions[i] // pool), spare)
            counts[i] = counts[i] + more
            spare = spare - more
    return np.array([bound] + counts)


def uneven(own_key, count, total, bound, lean):
    if count == 2:
        one = jax.random.randint(own_key, (), max(1, total - bound), min(bound, total - 1) + 1)
        return jnp.stack([one, total - one])
    lengths = jnp.asarray(profile(count, total, bound, lean), jnp.int32)
    pairs = (count - 1) // 2
    donor, sink = lengths[1:1 + 2 * pairs:2], lengths[2:2 + 2 * pairs:2]
    room = jnp.minimum(donor - 1, bound - sink)
    shifted = jax.random.randint(jax.random.fold_in(own_key, 1), (pairs,), 0, 1 << 20) % (room + 1)
    lengths = lengths.at[1:1 + 2 * pairs:2].set(donor - shifted).at[2:2 + 2 * pairs:2].set(sink + shifted)
    return lengths[jax.random.permutation(jax.random.fold_in(own_key, 2), count)]


def noise(own_key, extent, scale, reach, cuts=(), held_as=jnp.bfloat16):
    values = jax.random.normal(own_key, extent, jnp.float32) * scale
    if len(cuts) > 0:
        values = block_levels(own_key, extent, cuts, -0.22, 0.18) * values
    return jnp.clip(values, min=-reach, max=reach).astype(held_as)


def setup_inputs(seed: int = 0) -> dict:
    key_list = jax.random.split(jax.random.key(seed), 13)
    right_side = noise(key_list[0], (M, ELEMS), 1.0, 8.0, ((1, 32),), jnp.float32)
    conductivity = jnp.clip(jnp.exp(math.log(8.0) - 2.0794415 * jax.random.uniform(key_list[1], (ELEMS,), jnp.float32) ** block_levels(key_list[1], (ELEMS,), ((0, 32),), -0.2, 0.2)), 1.0, 8.0)
    material = touch_ends((jax.random.randint(key_list[2], (ELEMS,), 0, 3) < 1).astype(jnp.int32), jax.random.fold_in(key_list[2], 1), 0, 1)
    stiffness = draw_stiffness(jax.random.fold_in(key_list[12], 71), 0)
    trace_map = noise(key_list[4], (6 * Q, M), M ** -0.5, 0.75, (), jnp.float32)
    face_neighbour = touch_ends(jax.random.randint(key_list[5], (6, ELEMS), 0, TABLE), jax.random.fold_in(key_list[5], 1), 0, TABLE - 1).astype(jnp.int32)
    sub_sends = touch_ends(jax.random.randint(key_list[6], (N_BLK * N_SUB, N_SUB * CAP), 0, 6 * E_DEV), jax.random.fold_in(key_list[6], 1), 0, (6 * E_DEV) - 1).astype(jnp.int32)
    blk_sends = touch_ends(jax.random.randint(key_list[7], (N_BLK * N_SUB, 2 * CAPB), 0, 6 * E_DEV), jax.random.fold_in(key_list[7], 1), 0, (6 * E_DEV) - 1).astype(jnp.int32)
    group_sizes = jax.vmap(lambda own: uneven(own, P_DEV, E_DEV, 8, 2))(jax.random.split(key_list[8], (N_BLK * N_SUB))).reshape((N_BLK * N_SUB, P_DEV)).astype(jnp.int32)
    coarse_conductivity = jnp.clip(jnp.exp(math.log(8.0) - 2.0794415 * jax.random.uniform(key_list[9], (GROUPS,), jnp.float32) ** block_levels(key_list[9], (GROUPS,), ((0, 32),), -0.2, 0.2)), 1.0, 8.0)
    coarse_stiffness = draw_coarse_stiffness(jax.random.fold_in(key_list[12], 71), 0)
    restriction = noise(key_list[11], (8, M, M), (2 * M) ** -0.5, 0.5, (), jnp.float32)
    return {"right_side": right_side, "conductivity": conductivity, "material": material, "stiffness": stiffness, "trace_map": trace_map, "face_neighbour": face_neighbour, "sub_sends": sub_sends, "blk_sends": blk_sends, "group_sizes": group_sizes, "coarse_conductivity": coarse_conductivity, "coarse_stiffness": coarse_stiffness, "restriction": restriction}


HIGHEST = lax.Precision.HIGHEST
PENALTY = 0.3
COUPLING = 0.5
LOW_EIG = 0.4
HIGH_EIG = 2.5


def matmul(left, right):
    return jnp.dot(left, right, precision=HIGHEST)


def chebyshev(operator, diagonal, residual, sweeps):
    center_eig = 0.5 * (HIGH_EIG + LOW_EIG)
    half_width = 0.5 * (HIGH_EIG - LOW_EIG)
    sigma_ratio = center_eig / half_width
    recur_now = 1.0 / sigma_ratio
    solution = jnp.zeros_like(residual)
    direction = residual / (diagonal * center_eig)
    for iteration in range(sweeps):
        solution = solution + direction
        residual = residual - operator(direction)
        recur_next = 1.0 / (2.0 * sigma_ratio - recur_now)
        direction = recur_next * recur_now * direction + (2.0 * recur_next / half_width) * (residual / diagonal)
        recur_now = recur_next
    return solution, residual


def pick_columns(table, columns):
    return table[:, columns]


def fine_apply(field, conductivity, material, stiffness, trace_map, face_neighbour, sub_sends, blk_sends):
    devices = N_BLK * N_SUB
    picker = jax.vmap(pick_columns)
    traces = matmul(trace_map, field)
    own_table = traces.reshape(6, Q, devices, E_DEV).transpose(2, 1, 0, 3).reshape(devices, Q, 6 * E_DEV)
    outgoing = picker(own_table, sub_sends)
    incoming = outgoing.reshape(N_BLK, N_SUB, Q, N_SUB, CAP).transpose(0, 3, 2, 1, 4).reshape(devices, Q, N_SUB * CAP)
    outer = picker(own_table, blk_sends).reshape(N_BLK, N_SUB, Q, 2, CAPB)
    nothing = jnp.zeros((1, N_SUB, Q, CAPB), field.dtype)
    from_lower = jnp.concatenate([nothing, outer[:-1, :, :, 1, :]], axis=0).reshape(devices, Q, CAPB)
    from_upper = jnp.concatenate([outer[1:, :, :, 0, :], nothing], axis=0).reshape(devices, Q, CAPB)
    boundary = jnp.zeros((devices, Q, 1), field.dtype)
    table = jnp.concatenate([own_table, incoming, from_lower, from_upper, boundary], axis=2)
    columns = face_neighbour.reshape(6, devices, E_DEV).transpose(1, 0, 2).reshape(devices, 6 * E_DEV)
    seen = picker(table, columns).reshape(devices, Q, 6, E_DEV).transpose(2, 1, 0, 3).reshape(6 * Q, devices * E_DEV)
    face_term = matmul(trace_map.T, traces - seen)
    own_term = jnp.where(material[None, :] == 1, matmul(stiffness[1], field), matmul(stiffness[0], field))
    return conductivity[None, :] * own_term + PENALTY * face_term


def fine_diagonal(conductivity, material, stiffness, trace_map):
    diagonals = jnp.diagonal(stiffness, axis1=1, axis2=2)
    chosen = jnp.where(material[None, :] == 1, diagonals[1][:, None], diagonals[0][:, None])
    return conductivity[None, :] * chosen + PENALTY * jnp.sum(trace_map * trace_map, axis=0)[:, None]


def parent_layout(sizes):
    ends = jnp.cumsum(sizes).astype(jnp.int32)
    starts = ends - sizes
    position = jnp.arange(E_DEV, dtype=jnp.int32)
    parent = jnp.sum((ends[None, :] <= position[:, None]).astype(jnp.int32), axis=1).astype(jnp.int32)
    octant = position - starts[parent]
    return parent, octant


def reference(right_side, conductivity, material, stiffness, trace_map, face_neighbour, sub_sends, blk_sends, group_sizes, coarse_conductivity, coarse_stiffness, restriction):
    devices = N_BLK * N_SUB

    def operator(field):
        return fine_apply(field, conductivity, material, stiffness, trace_map, face_neighbour, sub_sends, blk_sends)

    diagonal = fine_diagonal(conductivity, material, stiffness, trace_map)
    pre_field, pre_residual = chebyshev(operator, diagonal, right_side, KF)
    parent, octant = lax.map(parent_layout, group_sizes)
    global_parent = (parent + P_DEV * jnp.arange(devices, dtype=jnp.int32)[:, None]).reshape(-1)
    octant = octant.reshape(-1)
    frame = jnp.concatenate([pre_residual[:, HEAD:], jnp.zeros((M, HEAD), pre_residual.dtype)], axis=1)
    children = jnp.zeros_like(frame)
    for octant_id in range(8):
        children = children + jnp.where(octant[None, :] == octant_id, matmul(restriction[octant_id], frame), 0.0)
    coarse_rhs = jax.ops.segment_sum(children.T, global_parent, num_segments=GROUPS).T
    coarse_diag = coarse_conductivity[None, :] * jnp.diagonal(coarse_stiffness)[:, None] + 2.0 * COUPLING

    def coarse_operator(field):
        own_term = coarse_conductivity[None, :] * matmul(coarse_stiffness, field)
        blocks = field.reshape(M, devices, P_DEV)
        padded = jnp.pad(blocks, ((0, 0), (0, 0), (1, 1)))
        laplace = 2.0 * blocks - padded[:, :, :-2] - padded[:, :, 2:]
        return own_term + COUPLING * laplace.reshape(M, GROUPS)

    coarse_field, unused = chebyshev(coarse_operator, coarse_diag, coarse_rhs, KC)
    spread = coarse_field[:, global_parent]
    fine_frame = jnp.zeros_like(frame)
    for octant_id in range(8):
        fine_frame = fine_frame + jnp.where(octant[None, :] == octant_id, matmul(restriction[octant_id].T, spread), 0.0)
    correction = jnp.concatenate([jnp.zeros((M, HEAD), frame.dtype), fine_frame[:, :ELEMS - HEAD]], axis=1)
    mid_field = pre_field + correction
    mid_residual = right_side - operator(mid_field)
    post_field, residual = chebyshev(operator, diagonal, mid_residual, KF)
    return mid_field + post_field, residual
```

```python
import functools

import jax
import jax.numpy as jnp
from jax import lax
from jax.experimental import pallas as pl
from jax.experimental.pallas import tpu as pltpu
from jax.sharding import PartitionSpec as P

HEAD = 8
KF = 3
KC = 4
FACES = 6
LANES = 128
VMEM = 4 << 20

HIGHEST = lax.Precision.HIGHEST
PENALTY = 0.3
COUPLING = 0.5
LOW_EIG = 0.4
HIGH_EIG = 2.5
CENTER = 0.5 * (HIGH_EIG + LOW_EIG)
HALF = 0.5 * (HIGH_EIG - LOW_EIG)


def steps(sweeps):
    sigma = CENTER / HALF
    rho, pairs = 1.0 / sigma, []
    for _ in range(sweeps):
        rho_next = 1.0 / (2.0 * sigma - rho)
        pairs.append((rho_next * rho, 2.0 * rho_next / HALF))
        rho = rho_next
    return pairs


def dot(left, right):
    return jnp.dot(left, right, precision=HIGHEST, preferred_element_type=jnp.float32)


def dot_t(left, right):
    return lax.dot_general(
        left, right, (((0,), (0,)), ((), ())), precision=HIGHEST, preferred_element_type=jnp.float32
    )


def take(tile, lane):
    index = jnp.broadcast_to(lane, tile.shape)
    return jnp.take_along_axis(tile, index, axis=1, mode="promise_in_bounds")


def pick(tiles, columns):
    lane = jnp.bitwise_and(columns, LANES - 1)
    at = jnp.right_shift(columns, 7)
    out = jnp.zeros(tiles[0].shape, tiles[0].dtype)
    for number, tile in enumerate(tiles):
        out = jnp.where(at == number, take(tile, lane), out)
    return out


def lanes(rows=1):
    return lax.broadcasted_iota(jnp.int32, (rows, LANES), 1)


def trace_tiles(traces):
    points = traces.shape[0] // FACES
    return [
        traces[f * points : (f + 1) * points, h : h + LANES]
        for f in range(FACES)
        for h in range(0, traces.shape[1], LANES)
    ]


def send(traces, sub_ref, blk_ref, sub_out, blk_out):
    tiles = trace_tiles(traces)
    for h in range(0, sub_ref.shape[1], LANES):
        sub_out[:, h : h + LANES] = pick(tiles, sub_ref[:, h : h + LANES])
    blk_out[...] = pick(tiles, blk_ref[...])


def start_kernel(
    b_ref, cond_ref, mat_ref, stiff_ref, map_ref, sub_ref, blk_ref, p_out, ig_out, tr_out, sub_out, blk_out
):
    modes = map_ref.shape[1]
    eye = lax.broadcasted_iota(jnp.int32, (modes, modes), 0) == lax.broadcasted_iota(
        jnp.int32, (modes, modes), 1
    )
    diagonals = [
        jnp.sum(jnp.where(eye, stiff_ref[k], 0.0), axis=1, keepdims=True) for k in range(2)
    ]
    squares = jnp.sum(map_ref[...] * map_ref[...], axis=0, keepdims=True)
    squares = jnp.sum(jnp.where(eye, squares, 0.0), axis=1, keepdims=True)
    chosen = jnp.where(mat_ref[...] == 1, diagonals[1], diagonals[0])
    inverse = 1.0 / (cond_ref[...] * chosen + PENALTY * squares)
    ig_out[...] = inverse
    p = b_ref[...] * inverse * (1.0 / CENTER)
    p_out[...] = p
    traces = dot(map_ref[...], p)
    tr_out[...] = traces
    send(traces, sub_ref, blk_ref, sub_out, blk_out)


def local_kernel(p_ref, tr_ref, x_ref, cond_ref, mat_ref, stiff_ref, map_ref, face_ref, base_out, x_out, seen):
    traces = tr_ref[...]
    tiles = trace_tiles(traces)
    points = tiles[0].shape[0]
    for f in range(FACES):
        for h in range(0, traces.shape[1], LANES):
            seen[f * points : (f + 1) * points, h : h + LANES] = pick(
                tiles, face_ref[f : f + 1, h : h + LANES]
            )
    p = p_ref[...]
    face = dot_t(map_ref[...], traces - seen[...])
    own = jnp.where(mat_ref[...] == 1, dot(stiff_ref[1], p), dot(stiff_ref[0], p))
    base_out[...] = cond_ref[...] * own + PENALTY * face
    x_out[...] = p if x_ref is None else x_ref[...] + p


def remote_residual(r_ref, base_ref, map_ref, face_ref, remote, seen):
    own = FACES * r_ref.shape[1] // LANES
    points = remote[0].shape[0]
    for f in range(FACES):
        for h in range(0, r_ref.shape[1], LANES):
            columns = face_ref[f : f + 1, h : h + LANES] - own * LANES
            seen[f * points : (f + 1) * points, h : h + LANES] = pick(remote, columns)
    return r_ref[...] - base_ref[...] + PENALTY * dot_t(map_ref[...], seen[...])


def remote_tiles(sub_refs, low_ref, high_ref, chips):
    lane = lanes()
    if chips:
        me = lax.axis_index("sub")
        slot = me * 16 + jnp.bitwise_and(lane, 15)
        owner = jnp.right_shift(lane, 4)
        tile = jnp.zeros(low_ref.shape, jnp.float32)
        for k, ref in sub_refs:
            tile = jnp.where(owner == jnp.bitwise_xor(me, k), take(ref(), slot), tile)
        tiles = [tile]
    else:
        tiles = [sub_refs[:, h : h + LANES] for h in range(0, sub_refs.shape[1], LANES)]
    other = jnp.bitwise_xor(lane, 8)
    rim = jnp.where(lane < 8, take(low_ref[...], other), take(high_ref[...], other))
    tiles.append(jnp.where(lane < 16, rim, 0.0))
    return tiles


def finish_kernel(kind, coefficients, chips, *refs):
    refs = list(refs)
    seen = refs.pop()
    r_ref, base_ref, map_ref, face_ref, low_ref, high_ref = refs[:6]
    refs = refs[6:]
    if chips:
        own_ref, two, four, six, swapped = refs[:5]
        refs = refs[5:]
        subs = [(0, lambda: own_ref[...]), (2, lambda: two[...]), (4, lambda: four[...]), (6, lambda: six[...])]
        height = own_ref.shape[0]
        for at, k in enumerate((1, 3, 5, 7)):
            subs.append((k, functools.partial(lambda a: swapped[a * height : (a + 1) * height, :], at)))
    else:
        subs = refs[0]
        refs = refs[1:]
    remote = remote_tiles(subs, low_ref, high_ref, chips)
    residual = remote_residual(r_ref, base_ref, map_ref, face_ref, remote, seen)
    if kind == "last":
        refs[0][...] = residual
        return
    if kind == "frame":
        r_out, head_out = refs
        r_out[...] = residual
        head_out[...] = residual[:, :LANES]
        return
    if kind == "step":
        p_ref = refs.pop(0)
    ig_ref, sub_ref, blk_ref, r_out, p_out, tr_out, sub_out, blk_out = refs
    r_out[...] = residual
    p = coefficients[1] * (residual * ig_ref[...])
    if kind == "step":
        p = p + coefficients[0] * p_ref[...]
    p_out[...] = p
    traces = dot(map_ref[...], p)
    tr_out[...] = traces
    send(traces, sub_ref, blk_ref, sub_out, blk_out)


def layout_kernel(sizes_ref, gather_out, place_out):
    parents = sizes_ref.shape[1]
    row = lax.broadcasted_iota(jnp.int32, (parents, parents), 0)
    col = lax.broadcasted_iota(jnp.int32, (parents, parents), 1)
    sizes = jnp.broadcast_to(sizes_ref[...], (parents, parents))
    size = jnp.sum(jnp.where(row == col, sizes, 0), axis=1, keepdims=True)
    end = jnp.sum(jnp.where(col <= row, sizes, 0), axis=1, keepdims=True)
    lane = lanes(parents)
    parent = jnp.bitwise_and(lane, parents - 1)
    group = lax.broadcasted_iota(jnp.int32, (parents, LANES), 0)
    size_row = jnp.sum(jnp.where(group == parent, size, 0), axis=0, keepdims=True)
    start_row = jnp.sum(jnp.where(group < parent, size, 0), axis=0, keepdims=True)
    half = jnp.right_shift(lanes(), parents.bit_length() - 1)
    for j in range(4):
        octant = 2 * j + half
        gather_out[j : j + 1, :] = jnp.where(octant < size_row, start_row + octant + HEAD, -1)
    for j in range(3):
        position = lane + (j * LANES - HEAD)
        before = end <= position
        place_out[2 * j : 2 * j + 1, :] = jnp.sum(before.astype(jnp.int32), axis=0, keepdims=True)
        place_out[2 * j + 1 : 2 * j + 2, :] = (
            lanes() + (j * LANES - HEAD) - jnp.sum(jnp.where(before, size, 0), axis=0, keepdims=True)
        )


def coarse_kernel(
    r_ref, arriving_ref, gather_ref, place_ref, cond_ref, stiff_ref, down_ref, up_ref, field_out, tail_out, cond
):
    modes = r_ref.shape[0]
    parents = cond_ref.shape[1]
    sources = [r_ref[:, h : h + LANES] for h in range(0, r_ref.shape[1], LANES)] + [arriving_ref[...]]
    first = second = None
    for j in range(4):
        children = pick(sources, gather_ref[j : j + 1, :])
        both = dot(down_ref[2 * j * modes : (2 * j + 2) * modes, :], children)
        one, two = both[:modes], both[modes:]
        first = one if first is None else first + one
        second = two if second is None else second + two
    lane = lanes()
    right = jnp.where(lane < parents, first + pltpu.roll(second, parents, 1), 0.0)
    cond[...] = jnp.ones(cond.shape, jnp.float32)
    cond[:, :parents] = cond_ref[...]
    scale = cond[...]
    eye = lax.broadcasted_iota(jnp.int32, (modes, modes), 0) == lax.broadcasted_iota(
        jnp.int32, (modes, modes), 1
    )
    diagonal = jnp.sum(jnp.where(eye, stiff_ref[...], 0.0), axis=1, keepdims=True)
    inverse = 1.0 / (scale * diagonal + 2.0 * COUPLING)
    p = right * inverse * (1.0 / CENTER)
    field, residual = p, right
    for before, correct in steps(KC - 1):
        left = jnp.where(lane == 0, 0.0, pltpu.roll(p, 1, 1))
        after = jnp.where(lane == parents - 1, 0.0, pltpu.roll(p, LANES - 1, 1))
        residual = residual - (
            scale * dot(stiff_ref[...], p) + COUPLING * (2.0 * p - left - after)
        )
        p = before * p + correct * (residual * inverse)
        field = field + p
    lifted = dot(up_ref[...], field)
    for j in range(3):
        parent, octant = place_ref[2 * j : 2 * j + 1, :], place_ref[2 * j + 1 : 2 * j + 2, :]
        inside = jnp.logical_and(lane + (j * LANES - HEAD) >= 0, lane + (j * LANES - HEAD) < 2 * LANES)
        parent = jnp.where(inside, parent, 0)
        out = jnp.zeros((modes, LANES), jnp.float32)
        for o in range(8):
            out = jnp.where(octant == o, take(lifted[o * modes : (o + 1) * modes], parent), out)
        out = jnp.where(inside, out, 0.0)
        if j < 2:
            field_out[:, j * LANES : (j + 1) * LANES] = out
        else:
            tail_out[...] = out


def middle_kernel(field_ref, arriving_ref, map_ref, sub_ref, blk_ref, p_out, tr_out, sub_out, blk_out):
    p_out[...] = field_ref[...]
    p_out[:, :LANES] = field_ref[:, :LANES] + jnp.where(lanes() < HEAD, arriving_ref[...], 0.0)
    traces = dot(map_ref[...], p_out[...])
    tr_out[...] = traces
    send(traces, sub_ref, blk_ref, sub_out, blk_out)


def call(kernel, outs, *args, scratch=()):
    return pl.pallas_call(
        kernel,
        out_shape=[jax.ShapeDtypeStruct(shape, kind) for shape, kind in outs],
        in_specs=[pl.BlockSpec(memory_space=pltpu.VMEM)] * len(args),
        out_specs=[pl.BlockSpec(memory_space=pltpu.VMEM)] * len(outs),
        scratch_shapes=list(scratch),
        compiler_params=pltpu.CompilerParams(vmem_limit_bytes=VMEM),
    )(*args)


def from_behind(x, axis, by):
    peers = lax.axis_size(axis)
    pairs = [(i, i + by) for i in range(peers) if 0 <= i + by < peers]
    return lax.ppermute(x, axis, pairs)


def local(
    right_side,
    conductivity,
    material,
    stiffness,
    trace_map,
    face_neighbour,
    sub_sends,
    blk_sends,
    group_sizes,
    coarse_conductivity,
    coarse_stiffness,
    restriction,
):
    f32, i32 = jnp.float32, jnp.int32
    modes, count = right_side.shape
    rows = trace_map.shape[0]
    points = rows // FACES
    peers, segments = lax.axis_size("sub"), lax.axis_size("blk")
    chips = peers == 8
    cond = conductivity.reshape(1, count)
    mat = material.reshape(1, count)
    blk_row = jnp.pad(blk_sends, ((0, 0), (0, LANES - blk_sends.shape[1])))
    block = ((modes, count), f32)
    sends = [((rows, count), f32), ((points, sub_sends.shape[1]), f32), ((points, LANES), f32)]
    seen = pltpu.VMEM((rows, count), f32)

    def exchange(sub_out, blk_out):
        ring = [(i, (i + 1) % segments) for i in range(segments)]
        low = lax.ppermute(blk_out, "blk", [(i, j) for i, j in ring if j > 0])
        high = lax.ppermute(blk_out, "blk", [(j, i) for i, j in ring if j > 0])
        if not chips:
            return [low, high, lax.all_to_all(sub_out, "sub", 1, 1, tiled=True)]
        far = [
            lax.ppermute(sub_out, "sub", [(i, i ^ k) for i in range(peers)]) for k in (2, 4, 6)
        ]
        held = jnp.concatenate([sub_out, *far], axis=0)
        swapped = lax.ppermute(held, "sub", [(i, i ^ 1) for i in range(peers)])
        return [low, high, sub_out, *far, swapped]

    def part(p, traces, x):
        args = [p, traces] + ([] if x is None else [x])
        args += [cond, mat, stiffness, trace_map, face_neighbour]
        kernel = local_kernel
        if x is None:
            def kernel(p_ref, tr_ref, *refs):
                return local_kernel(p_ref, tr_ref, None, *refs)
        return call(kernel, [block, block], *args, scratch=[seen])

    def finish(kind, coefficients, r, base, got, p=None):
        args = [r, base, trace_map, face_neighbour, *got]
        if kind == "last":
            outs = [block]
        elif kind == "frame":
            outs = [block, ((modes, LANES), f32)]
        else:
            args += ([p] if kind == "step" else []) + [inverse, sub_sends, blk_row]
            outs = [block, block, *sends]
        kernel = functools.partial(finish_kernel, kind, coefficients, chips)
        return call(kernel, outs, *args, scratch=[seen])

    gather, place = call(layout_kernel, [((4, LANES), i32), ((6, LANES), i32)], group_sizes)
    p, inverse, traces, *out = call(
        start_kernel,
        [block, block, *sends],
        right_side, cond, mat, stiffness, trace_map, sub_sends, blk_row,
    )
    r, x = right_side, None
    pairs = steps(KF)
    for step in range(KF):
        got = exchange(*out)
        base, x = part(p, traces, x)
        if step < KF - 1:
            r, p, traces, *out = finish("step", pairs[step], r, base, got, p)
    r, head = finish("frame", None, r, base, got)

    arriving = from_behind(head, ("blk", "sub"), -1)
    down = restriction.reshape(8 * modes, modes)
    up = jnp.transpose(restriction, (0, 2, 1)).reshape(8 * modes, modes)
    field, tail = call(
        coarse_kernel,
        [block, ((modes, LANES), f32)],
        r, arriving, gather, place, coarse_conductivity.reshape(1, -1), coarse_stiffness, down, up,
        scratch=[pltpu.VMEM((1, LANES), f32)],
    )
    returning = from_behind(tail, ("blk", "sub"), 1)
    p, traces, *out = call(
        middle_kernel, [block, *sends], field, returning, trace_map, sub_sends, blk_row
    )

    got = exchange(*out)
    base, x = part(p, traces, x)
    r, p, traces, *out = finish("first", (0.0, 1.0 / CENTER), r, base, got)
    for step in range(KF):
        got = exchange(*out)
        base, x = part(p, traces, x)
        if step < KF - 1:
            r, p, traces, *out = finish("step", pairs[step], r, base, got, p)
    (residual,) = finish("last", None, r, base, got)
    return x, residual


def solution(mesh):
    in_specs = (
        P(None, ("blk", "sub")),
        P(("blk", "sub")),
        P(("blk", "sub")),
        P(),
        P(),
        P(None, ("blk", "sub")),
        P(("blk", "sub"), None),
        P(("blk", "sub"), None),
        P(("blk", "sub"), None),
        P(("blk", "sub")),
        P(),
        P(),
    )
    out_specs = (P(None, ("blk", "sub")), P(None, ("blk", "sub")))
    return jax.shard_map(local, mesh=mesh, in_specs=in_specs, out_specs=out_specs, check_vma=False)
```

```python
import functools

import jax
import jax.numpy as jnp
from jax import lax
from jax.experimental import pallas as pl
from jax.experimental.pallas import tpu as pltpu
from jax.sharding import PartitionSpec as P

HEAD = 8
KF = 3
KC = 4
FACES = 6
OCTANTS = 8
LANES = 128
CORES = 2

PENALTY = 0.3
COUPLING = 0.5
LOW_EIG = 0.4
HIGH_EIG = 2.5
CENTER = 0.5 * (HIGH_EIG + LOW_EIG)
HALF = 0.5 * (HIGH_EIG - LOW_EIG)


def steps(sweeps):
    sigma = CENTER / HALF
    rho, pairs = 1.0 / sigma, []
    for _ in range(sweeps):
        rho_next = 1.0 / (2.0 * sigma - rho)
        pairs.append((rho_next * rho, 2.0 * rho_next / HALF))
        rho = rho_next
    return pairs


def halves(x):
    high = x.astype(jnp.bfloat16)
    return high, (x - high.astype(jnp.float32)).astype(jnp.bfloat16)


def product(left, x):
    high, low = halves(x)
    right = jnp.concatenate([high, low, high], axis=0)
    return jnp.dot(left, right, preferred_element_type=jnp.float32)


def store_left(out, rows, x):
    high, low = halves(x)
    width = x.shape[1]
    for place, piece in enumerate((high, high, low)):
        out[rows, place * width : (place + 1) * width] = piece


def take(tile, lane):
    index = jnp.broadcast_to(lane, tile.shape)
    return jnp.take_along_axis(tile, index, axis=1, mode="promise_in_bounds")


def pick(tiles, at, lane):
    out = jnp.zeros(tiles[0].shape, tiles[0].dtype)
    for number, tile in enumerate(tiles):
        out = jnp.where(at == number, take(tile, lane), out)
    return out


def lanes(rows=1):
    return lax.broadcasted_iota(jnp.int32, (rows, LANES), 1)


def cols(j, width, base=None):
    size, start = (width, j * width) if base is None else (LANES, j * width + base)
    return pl.ds(start if isinstance(j, int) else pl.multiple_of(start, LANES), size)


def over(blocks, body):
    if blocks <= 4:
        for j in range(blocks):
            body(j)
    else:
        lax.fori_loop(0, blocks, lambda j, carry: (body(j), carry)[1], 0)


def own_place():
    me = lax.axis_index("sub")
    return jnp.right_shift(me, 1), jnp.bitwise_and(me, 1)


def trace_tiles(traces):
    points = traces.shape[0] // FACES
    return [
        traces[f * points : (f + 1) * points, h : h + LANES]
        for f in range(FACES)
        for h in range(0, traces.shape[1], LANES)
    ]


def faces(tiles_of, shape):
    return jnp.concatenate(
        [
            jnp.concatenate([tiles_of(f, h) for h in range(0, shape, LANES)], axis=1)
            for f in range(FACES)
        ],
        axis=0,
    )


def send(j, traces, sub_ref, rim_ref, sub_out, rim_out, width, rims):
    tiles = trace_tiles(traces)
    for h in range(0, width, LANES):
        columns = sub_ref[:, cols(j, width, h)]
        sub_out[:, cols(j, width, h)] = pick(
            tiles, jnp.right_shift(columns, 7), jnp.bitwise_and(columns, LANES - 1)
        )
    group = LANES // rims
    tile = cols(j // group, LANES)
    columns = rim_ref[:, tile]
    rim = pick(tiles, jnp.right_shift(columns, 7), jnp.bitwise_and(columns, LANES - 1))
    mine = lanes() // rims == j % group
    rim_out[:, tile] = jnp.where(mine, rim, rim_out[:, tile])


def prep_kernel(map_ref, stiff_ref, t_out, tt_out, k_out):
    modes, rows = map_ref.shape
    transposed = map_ref[...]
    store_left(tt_out, slice(0, modes), transposed)
    store_left(t_out, slice(0, rows), transposed.T)
    for k in range(2):
        store_left(k_out, slice(k * modes, (k + 1) * modes), stiff_ref[k])


def prep_coarse_kernel(restriction_ref, stiff_ref, down_out, up_out, c_out):
    modes = stiff_ref.shape[0]
    store_left(c_out, slice(0, modes), stiff_ref[...])
    for o in range(OCTANTS):
        rows = slice(o * modes, (o + 1) * modes)
        store_left(down_out, rows, restriction_ref[o])
        store_left(up_out, rows, restriction_ref[o].T)


def pack_kernel(b_ref, cond_ref, mat_ref, face_ref, sub_ref, rim_ref, size_ref, coarse_ref, out):
    modes, count = b_ref.shape
    out[modes:, :] = jnp.zeros((out.shape[0] - modes, count), jnp.float32)
    out[:modes, :] = b_ref[...]
    out[modes : modes + 1, :] = cond_ref[...]
    out[modes + 1 : modes + 2, :] = mat_ref[...].astype(jnp.float32)
    out[modes + 2 : modes + 8, :] = face_ref[...].astype(jnp.float32)
    out[modes + 8 : modes + 9, : rim_ref.shape[1]] = rim_ref[...].astype(jnp.float32)
    out[modes + 9 : modes + 10, : size_ref.shape[1]] = size_ref[...].astype(jnp.float32)
    out[modes + 10 : modes + 11, : coarse_ref.shape[1]] = coarse_ref[...]
    width = sub_ref.shape[1]
    for at, h in enumerate(range(0, width, count)):
        piece = sub_ref[:, h : min(h + count, width)].astype(jnp.float32)
        out[modes + 11 + at : modes + 12 + at, : piece.shape[1]] = piece


def start_kernel(blocks, width, rims, *refs):
    gathered, refs = refs[:blocks], refs[blocks:]
    stiff_ref, map_ref, t_ref = refs[:3]
    b_out, ig_out, meta_out, lane_out, at_out, far_out, sub_out, rim_out, size_out, coarse_out = refs[3:13]
    p_out, tr_out, subs_out, rims_out, held = refs[13:]
    modes, count = map_ref.shape[0], gathered[0].shape[1]
    chip, core = own_place()
    for k, ref in enumerate(gathered):
        held[jnp.bitwise_xor(chip, k)] = ref[...]
    eye = lax.broadcasted_iota(jnp.int32, (modes, modes), 0) == lax.broadcasted_iota(
        jnp.int32, (modes, modes), 1
    )
    diagonals = [
        jnp.sum(jnp.where(eye, stiff_ref[k], 0.0), axis=1, keepdims=True) for k in range(2)
    ]
    squares = PENALTY * jnp.sum(map_ref[...] * map_ref[...], axis=1, keepdims=True)
    own_tiles = FACES * count // LANES
    sub_tiles = width // LANES
    rim_out[...] = jnp.zeros(rim_out.shape, jnp.int32)
    rims_out[...] = jnp.zeros(rims_out.shape, jnp.float32)
    peers = blocks * CORES
    slots = width // peers
    group = LANES // rims

    def body(j):
        b = held[j, :modes, :]
        cond = held[j, modes : modes + 1, :]
        mat = held[j, modes + 1 : modes + 2, :]
        b_out[:, cols(j, count)] = b
        meta_out[0:1, cols(j, count)] = cond
        meta_out[1:2, cols(j, count)] = mat
        column = held[j, modes + 2 : modes + 8, :].astype(jnp.int32)
        lane = jnp.bitwise_and(column, LANES - 1)
        at = jnp.right_shift(column, 7)
        lane_out[0:FACES, cols(j, count)] = lane
        at_out[0:FACES, cols(j, count)] = at
        remote = column - own_tiles * LANES
        other = jnp.bitwise_and(lax.div(lane, jnp.int32(slots)), 1) != core
        sub = jnp.logical_and(jnp.logical_and(at >= own_tiles, at < own_tiles + sub_tiles), other)
        rim = jnp.logical_and(at == own_tiles + sub_tiles, lane < rims)
        nothing = slots * (core + CORES)
        far_out[0:FACES, cols(j, count)] = jnp.where(
            sub, remote, jnp.where(rim, lane + slots * core, nothing)
        )
        for h in range(0, width, LANES):
            row = modes + 11 + h // count
            piece = held[j, row : row + 1, h % count : h % count + LANES]
            sub_out[:, cols(j, width, h)] = piece.astype(jnp.int32)
        row = jnp.broadcast_to(held[j, modes + 8 : modes + 9, :LANES], (8, LANES))
        row = pltpu.roll(row, (j % group) * rims, 1)[0:1].astype(jnp.int32)
        tile = cols(j // group, LANES)
        rim_out[:, tile] = jnp.where(lanes() // rims == j % group, row, rim_out[:, tile])
        size_out[pl.ds(j, 1), :] = held[j, modes + 9 : modes + 10, :LANES].astype(jnp.int32)
        coarse_out[pl.ds(j, 1), :] = held[j, modes + 10 : modes + 11, :LANES]
        inverse = 1.0 / (cond * jnp.where(mat == 1.0, diagonals[1], diagonals[0]) + squares)
        ig_out[:, cols(j, count)] = inverse
        p = b * inverse * (1.0 / CENTER)
        p_out[:, cols(j, count)] = p
        traces = product(t_ref[...], p)
        tr_out[:, cols(j, count)] = traces
        send(j, traces, sub_out, rim_out, subs_out, rims_out, width, rims)

    over(blocks, body)


def sub_tiles_of(j, sends_ref, core, width, blocks):
    slots = width // (blocks * CORES)
    pairs = LANES // slots // CORES
    lane = lanes()
    mine = lax.axis_index("sub") % CORES
    source = (CORES * (j % pairs) + mine) * slots + lane % slots
    tiles = []
    for t in range(width // LANES):
        tile = None
        for i in range(pairs):
            sent = sends_ref[:, cols(j // pairs, LANES, (pairs * t + i) * width)]
            there = take(sent, source)
            there = jnp.where(lane // slots == CORES * i + core, there, 0.0)
            tile = there if tile is None else tile + there
        tiles.append(tile)
    return tiles


def local_kernel(only_own, blocks, width, first, *refs):
    p_ref, tr_ref, subs_ref, meta_ref, lane_ref, at_ref, tt_ref, k_ref = refs[:8]
    refs = refs[8:]
    if not first:
        x_ref, refs = refs[0], refs[1:]
    base_out, x_out = refs
    modes = p_ref.shape[0]
    chip, core = own_place()
    count = x_out.shape[1]

    def body(j, out):
        traces = tr_ref[:, cols(j, count)]
        tiles = trace_tiles(traces) + sub_tiles_of(j, subs_ref, core, width, blocks)

        def tile(f, h):
            return pick(tiles, at_rows[f : f + 1, h : h + LANES], lane_rows[f : f + 1, h : h + LANES])

        at_rows, lane_rows = at_ref[:, cols(j, count)], lane_ref[:, cols(j, count)]
        seen = faces(tile, count)
        p = p_ref[:, cols(j, count)]
        both = product(k_ref[...], p)
        meta = meta_ref[:, cols(j, count)]
        own = meta[0:1] * jnp.where(meta[1:2] == 1.0, both[modes:], both[:modes])
        base_out[:, out] = own + PENALTY * product(tt_ref[...], traces - seen)

    if only_own:
        body(chip, slice(0, count))
    else:
        over(blocks, lambda j: body(j, cols(j, count)))
    p = p_ref[:, cols(chip, count)]
    x_out[...] = p if first else x_ref[...] + p


def rim_tiles(one_ref, two_ref, rims):
    segment, segments = lax.axis_index("blk"), lax.axis_size("blk")
    odd = segment % 2 == 1
    lane = lanes()
    tiles = []
    for h in range(0, one_ref.shape[1], LANES):
        one = take(one_ref[:, h : h + LANES], jnp.bitwise_xor(lane, rims // 2))
        two = take(two_ref[:, h : h + LANES], jnp.bitwise_xor(lane, rims // 2))
        low = jnp.where(segment == 0, 0.0, jnp.where(odd, one, two))
        high = jnp.where(segment == segments - 1, 0.0, jnp.where(odd, two, one))
        tiles.append(jnp.where(lane % rims < rims // 2, low, high))
    return tiles


def finish_kernel(kind, coefficients, blocks, width, rims, *refs):
    r_ref, base_ref, swapped_ref, one_ref, two_ref, far_ref, tt_ref = refs[:7]
    refs = list(refs[7:])
    modes = r_ref.shape[0]
    chip, core = own_place()
    slots = width // (blocks * CORES)
    group = LANES // rims
    lane = lanes()
    rim = rim_tiles(one_ref, two_ref, rims)
    if kind == "step":
        p_ref = refs.pop(0)
    if kind in ("step", "first"):
        ig_ref, t_ref, sub_ref, rim_ref, r_out, p_out, tr_out, subs_out, rims_out = refs
        rims_out[...] = jnp.zeros(rims_out.shape, jnp.float32)
    elif kind == "frame":
        r_out, head_out = refs
        head_out[...] = jnp.zeros(head_out.shape, jnp.float32)
    else:
        r_out = refs[0]
    count = r_out.shape[1] if kind == "last" else r_out.shape[1] // blocks

    def body(j):
        tiles = sub_tiles_of(j, swapped_ref, 1 - core, width, blocks)
        if len(rim) == 1:
            mine = rim[0]
        else:
            mine = rim[0]
            for t in range(1, len(rim)):
                mine = jnp.where(j // group == t, rim[t], mine)
        mine = pltpu.roll(mine, (slots * core - (j % group) * rims) % LANES, 1)
        tiles[0] = jnp.where(lane // slots == core, mine, tiles[0])
        far = far_ref[:, cols(j, count)]

        def tile(f, h):
            column = far[f : f + 1, h : h + LANES]
            if len(tiles) == 1:
                return take(tiles[0], column)
            return pick(tiles, jnp.right_shift(column, 7), jnp.bitwise_and(column, LANES - 1))

        here = cols(j, count)
        base = base_ref[...] if kind == "last" else base_ref[:, here]
        residual = r_ref[:, here] - base + PENALTY * product(tt_ref[...], faces(tile, count))
        if kind == "last":
            r_out[...] = residual
            return
        r_out[:, here] = residual
        if kind == "frame":
            heads = LANES // HEAD
            spot = cols(j // heads, LANES)
            moved = pltpu.roll(residual[:, :LANES], (j % heads) * HEAD, 1)
            head_out[:, spot] = jnp.where(lane // HEAD == j % heads, moved, head_out[:, spot])
            return
        p = coefficients[1] * (residual * ig_ref[:, here])
        if kind == "step":
            p = p + coefficients[0] * p_ref[:, here]
        p_out[:, here] = p
        traces = product(t_ref[...], p)
        tr_out[:, here] = traces
        send(j, traces, sub_ref, rim_ref, subs_out, rims_out, width, rims)

    if kind == "last":
        body(chip)
    else:
        over(blocks, body)


def layout_kernel(blocks, parents, size_ref, gather_out, parent_out, octant_out):
    row = lax.broadcasted_iota(jnp.int32, (parents, LANES), 0)
    lane = lanes(parents)
    pairs = LANES // parents
    group = jnp.bitwise_and(lane, parents - 1)
    half = jnp.right_shift(lanes(), parents.bit_length() - 1)
    count = parent_out.shape[1] // blocks

    def body(j):
        sizes = jnp.broadcast_to(size_ref[pl.ds(j, 1), :], (parents, LANES))
        size = jnp.sum(jnp.where(row == lane, sizes, 0), axis=1, keepdims=True)
        end = jnp.sum(jnp.where(lane <= row, sizes, 0), axis=1, keepdims=True)
        size_row = jnp.sum(jnp.where(row == group, size, 0), axis=0, keepdims=True)
        start_row = jnp.sum(jnp.where(row < group, size, 0), axis=0, keepdims=True)
        for i in range(OCTANTS // pairs):
            octant = pairs * i + half
            place = jnp.bitwise_and(start_row + octant + HEAD, count - 1)
            gather_out[i : i + 1, cols(j, LANES)] = jnp.where(octant < size_row, place, -1)
        for h in range(0, count, LANES):
            position = jnp.bitwise_and(lane + (h - HEAD), count - 1)
            before = end <= position
            parent = jnp.sum(before.astype(jnp.int32), axis=0, keepdims=True)
            start = jnp.sum(jnp.where(before, size, 0), axis=0, keepdims=True)
            parent_out[:, cols(j, count, h)] = parent + parents * (j % pairs)
            octant_out[:, cols(j, count, h)] = position[0:1] - start

    over(blocks, body)


def heads_of(j, swapped_ref, cross_ref, by, blocks):
    chip, core = own_place()
    heads = LANES // HEAD
    lane = lanes()
    apart = core if by == 1 else 1 - core
    source = j + by * apart
    inside = jnp.logical_and(source >= 0, source < blocks)
    at = jnp.clip(source, 0, blocks - 1)
    edge = 0 if by == 1 else blocks - 1
    tile = pl.ds(pl.multiple_of((at // heads) * LANES, LANES), LANES)
    near = pltpu.roll(swapped_ref[:, tile], (LANES - (at % heads) * HEAD) % LANES, 1)
    cross = cross_ref[:, (edge // heads) * LANES : (edge // heads + 1) * LANES]
    if edge % heads:
        cross = pltpu.roll(cross, LANES - (edge % heads) * HEAD, 1)
    segment, segments = lax.axis_index("blk"), lax.axis_size("blk")
    outside = segment == (segments - 1 if by == 1 else 0)
    cross = jnp.where(outside, 0.0, cross)
    return jnp.where(lane < HEAD, jnp.where(inside, near, cross), 0.0)


def coarse_kernel(
    blocks, parents, r_ref, swapped_ref, cross_ref, gather_ref, parent_ref, octant_ref, cond_ref, stiff_ref,
    down_ref, up_ref, c_ref, field_out, tail_out, right, field_ref, lifted,
):
    modes = r_ref.shape[0]
    count = r_ref.shape[1] // blocks
    lane = lanes()
    pairs = LANES // parents

    def restrict(j):
        arriving = heads_of(j, swapped_ref, cross_ref, 1, blocks)
        sources = [r_ref[:, cols(j, count, h)] for h in range(0, count, LANES)]
        sources[0] = jnp.where(lane < HEAD, arriving, sources[0])
        sums = [None] * pairs
        for i in range(OCTANTS // pairs):
            place = gather_ref[i : i + 1, cols(j, LANES)]
            children = pick(sources, jnp.right_shift(place, 7), jnp.bitwise_and(place, LANES - 1))
            both = product(down_ref[pairs * i * modes : pairs * (i + 1) * modes, :], children)
            for k in range(pairs):
                one = both[k * modes : (k + 1) * modes]
                sums[k] = one if sums[k] is None else sums[k] + one
        total = sums[0]
        for k in range(1, pairs):
            total = total + pltpu.roll(sums[k], LANES - k * parents, 1)
        tile = cols(j // pairs, LANES)
        moved = pltpu.roll(total, (j % pairs) * parents, 1)
        right[:, tile] = jnp.where(lane // parents == j % pairs, moved, right[:, tile])

    right[...] = jnp.zeros(right.shape, jnp.float32)
    over(blocks, restrict)
    eye = lax.broadcasted_iota(jnp.int32, (modes, modes), 0) == lax.broadcasted_iota(
        jnp.int32, (modes, modes), 1
    )
    diagonal = jnp.sum(jnp.where(eye, stiff_ref[...], 0.0), axis=1, keepdims=True)

    def solve(t):
        scale = jnp.zeros((1, LANES), jnp.float32)
        for k in range(pairs):
            row = jnp.broadcast_to(cond_ref[pl.ds(pairs * t + k, 1), :], (8, LANES))
            row = pltpu.roll(row, k * parents, 1)[0:1] if k else row[0:1]
            scale = jnp.where(lane // parents == k, row, scale)
        inverse = 1.0 / (scale * diagonal + 2.0 * COUPLING)
        residual = right[:, cols(t, LANES)]
        p = residual * inverse * (1.0 / CENTER)
        field = p
        for before, correct in steps(KC - 1):
            left = jnp.where(lane % parents == 0, 0.0, pltpu.roll(p, 1, 1))
            after = jnp.where(lane % parents == parents - 1, 0.0, pltpu.roll(p, LANES - 1, 1))
            residual = residual - (
                scale * product(c_ref[...], p) + COUPLING * (2.0 * p - left - after)
            )
            p = before * p + correct * (residual * inverse)
            field = field + p
        lifted[:, cols(t, LANES)] = product(up_ref[...], field)

    over(blocks // pairs, solve)
    tail_out[...] = jnp.zeros(tail_out.shape, jnp.float32)
    heads = LANES // HEAD

    def prolong(j):
        sources = [lifted[o * modes : (o + 1) * modes, cols(j // pairs, LANES)] for o in range(OCTANTS)]
        for h in range(0, count, LANES):
            parent, octant = parent_ref[:, cols(j, count, h)], octant_ref[:, cols(j, count, h)]
            out = pick(sources, octant, parent)
            field_out[:, cols(j, count, h)] = out
            if h == 0:
                spot = cols(j // heads, LANES)
                moved = pltpu.roll(out, (j % heads) * HEAD, 1)
                tail_out[:, spot] = jnp.where(lane // HEAD == j % heads, moved, tail_out[:, spot])

    over(blocks, prolong)


def middle_kernel(
    blocks, width, rims, field_ref, swapped_ref, cross_ref, t_ref, sub_ref, rim_ref, p_out, tr_out, subs_out, rims_out
):
    count = field_ref.shape[1] // blocks
    lane = lanes()
    rims_out[...] = jnp.zeros(rims_out.shape, jnp.float32)

    def body(j):
        arriving = heads_of(j, swapped_ref, cross_ref, -1, blocks)
        field = field_ref[:, cols(j, count)]
        first = jnp.where(lane < HEAD, arriving, field[:, :LANES])
        field = jnp.concatenate([first, field[:, LANES:]], axis=1)
        p_out[:, cols(j, count)] = field
        traces = product(t_ref[...], field)
        tr_out[:, cols(j, count)] = traces
        send(j, traces, sub_ref, rim_ref, subs_out, rims_out, width, rims)

    over(blocks, body)


def call(limit, kernel, outs, *args, scratch=()):
    return pl.pallas_call(
        kernel,
        out_shape=[jax.ShapeDtypeStruct(shape, kind) for shape, kind in outs],
        in_specs=[pl.BlockSpec(memory_space=pltpu.VMEM)] * len(args),
        out_specs=[pl.BlockSpec(memory_space=pltpu.VMEM)] * len(outs),
        scratch_shapes=list(scratch),
        compiler_params=pltpu.CompilerParams(vmem_limit_bytes=limit),
    )(*args)


def local(
    right_side,
    conductivity,
    material,
    stiffness,
    trace_map,
    face_neighbour,
    sub_sends,
    blk_sends,
    group_sizes,
    coarse_conductivity,
    coarse_stiffness,
    restriction,
):
    f32, i32, bf16 = jnp.float32, jnp.int32, jnp.bfloat16
    modes, count = right_side.shape
    rows = trace_map.shape[0]
    points = rows // FACES
    peers, segments = lax.axis_size("sub"), lax.axis_size("blk")
    blocks = peers // CORES
    width, rims = sub_sends.shape[1], blk_sends.shape[1]
    parents = group_sizes.shape[1]
    total = blocks * count
    limit = (4 << 20) if blocks <= 4 else (40 << 20)
    run = functools.partial(call, limit)

    def pad(size, to):
        return -(-size // to) * to

    rim_width = pad(blocks * rims, LANES)
    head_width = pad(blocks * HEAD, LANES)
    field = ((modes, total), f32)
    block = ((modes, count), f32)
    sends = [((rows, total), f32), ((points, blocks * width), f32), ((points, rim_width), f32)]

    def everywhere(partner):
        pairs = []
        for b in range(segments):
            for s in range(peers):
                other_b, other_s = partner(b, s)
                pairs.append((b * peers + s, other_b * peers + other_s))
        return pairs

    def above_or_below(first):
        def partner(b, s):
            other = b + 1 if b % 2 == first else b - 1
            return (other, s) if 0 <= other < segments else (b, s ^ 2)

        return everywhere(partner)

    def crossing(b, s):
        other = b - 1 if s % 2 == 0 else b + 1
        return (other, s ^ 1) if 0 <= other < segments else (b, s ^ 2)

    both = ("blk", "sub")
    cores = [(s, s ^ 1) for s in range(peers)]
    ones, twos, crossings = above_or_below(0), above_or_below(1), everywhere(crossing)

    def exchange(subs, rim):
        one = lax.ppermute(rim, both, ones)
        two = lax.ppermute(rim, both, twos)
        return [lax.ppermute(subs, "sub", cores), one, two]

    def shift(heads):
        return lax.ppermute(heads, "sub", cores), lax.ppermute(heads, both, crossings)

    map_t = trace_map.T
    t3, tt3, k3 = run(
        prep_kernel,
        [((rows, 3 * modes), bf16), ((modes, 3 * rows), bf16), ((2 * modes, 3 * modes), bf16)],
        map_t, stiffness,
    )
    height = pad(modes + 11 + pad(width, count) // count, 8)
    (packed,) = run(
        pack_kernel,
        [((height, count), f32)],
        right_side, conductivity.reshape(1, count), material.reshape(1, count), face_neighbour, sub_sends, blk_sends,
        group_sizes, coarse_conductivity.reshape(1, -1),
    )
    gathered = [packed] + [
        lax.ppermute(packed, "sub", [(s, s ^ (CORES * k)) for s in range(peers)]) for k in range(1, blocks)
    ]
    b, inverse, meta, lane, at, far, subs, rim, sizes, coarse_cond, p, traces, *out = run(
        functools.partial(start_kernel, blocks, width, rims),
        [
            field, field, ((8, total), f32), ((8, total), i32), ((8, total), i32), ((8, total), i32),
            ((1, blocks * width), i32), ((1, rim_width), i32), ((blocks, LANES), i32), ((blocks, LANES), f32),
            field, *sends,
        ],
        *gathered, stiffness, map_t, t3,
        scratch=[pltpu.VMEM((blocks, height, count), f32)],
    )

    def part(p, traces, subs_sent, x, only_own=False):
        args = [p, traces, subs_sent, meta, lane, at, tt3, k3] + ([] if x is None else [x])
        kernel = functools.partial(local_kernel, only_own, blocks, width, x is None)
        return run(kernel, [block if only_own else field, block], *args)

    def finish(kind, coefficients, r, base, got, p=None):
        args = [r, base, *got, far, tt3]
        if kind == "last":
            outs = [block]
        elif kind == "frame":
            outs = [field, ((modes, head_width), f32)]
        else:
            args += ([p] if kind == "step" else []) + [inverse, t3, subs, rim]
            outs = [field, field, *sends]
        return run(functools.partial(finish_kernel, kind, coefficients, blocks, width, rims), outs, *args)

    gather, parent, octant = run(
        functools.partial(layout_kernel, blocks, parents),
        [((OCTANTS * parents // LANES, blocks * LANES), i32), ((1, total), i32), ((1, total), i32)],
        sizes,
    )
    down3, up3, c3 = run(
        prep_coarse_kernel,
        [((OCTANTS * modes, 3 * modes), bf16), ((OCTANTS * modes, 3 * modes), bf16), ((modes, 3 * modes), bf16)],
        restriction, coarse_stiffness,
    )

    r, x = b, None
    pairs = steps(KF)
    for step in range(KF):
        got = exchange(*out)
        base, x = part(p, traces, out[0], x)
        if step < KF - 1:
            r, p, traces, *out = finish("step", pairs[step], r, base, got, p)
    r, heads = finish("frame", None, r, base, got)

    correction, tails = run(
        functools.partial(coarse_kernel, blocks, parents),
        [field, ((modes, head_width), f32)],
        r, *shift(heads), gather, parent, octant, coarse_cond, coarse_stiffness, down3, up3, c3,
        scratch=[
            pltpu.VMEM((modes, blocks * parents), f32),
            pltpu.VMEM((8, LANES), f32),
            pltpu.VMEM((OCTANTS * modes, blocks * parents), f32),
        ],
    )
    p, traces, *out = run(
        functools.partial(middle_kernel, blocks, width, rims), [field, *sends], correction, *shift(tails), t3, subs, rim
    )

    got = exchange(*out)
    base, x = part(p, traces, out[0], x)
    r, p, traces, *out = finish("first", (0.0, 1.0 / CENTER), r, base, got)
    for step in range(KF):
        got = exchange(*out)
        base, x = part(p, traces, out[0], x, step == KF - 1)
        if step < KF - 1:
            r, p, traces, *out = finish("step", pairs[step], r, base, got, p)
    (residual,) = finish("last", None, r, base, got)
    return x, residual


def solution(mesh):
    in_specs = (
        P(None, ("blk", "sub")),
        P(("blk", "sub")),
        P(("blk", "sub")),
        P(),
        P(),
        P(None, ("blk", "sub")),
        P(("blk", "sub"), None),
        P(("blk", "sub"), None),
        P(("blk", "sub"), None),
        P(("blk", "sub")),
        P(),
        P(),
    )
    out_specs = (P(None, ("blk", "sub")), P(None, ("blk", "sub")))
    return jax.shard_map(local, mesh=mesh, in_specs=in_specs, out_specs=out_specs, check_vma=False)
```

```python
import functools

import jax
import jax.numpy as jnp
from jax import lax
from jax.experimental import pallas as pl
from jax.experimental.pallas import tpu as pltpu
from jax.sharding import PartitionSpec as P

HEAD = 8
KF = 3
KC = 4
FACES = 6
OCTANTS = 8
LANES = 128
CORES = 2

PENALTY = 0.3
COUPLING = 0.5
LOW_EIG = 0.4
HIGH_EIG = 2.5
CENTER = 0.5 * (HIGH_EIG + LOW_EIG)
HALF = 0.5 * (HIGH_EIG - LOW_EIG)


def steps(sweeps):
    sigma = CENTER / HALF
    rho, pairs = 1.0 / sigma, []
    for _ in range(sweeps):
        rho_next = 1.0 / (2.0 * sigma - rho)
        pairs.append((rho_next * rho, 2.0 * rho_next / HALF))
        rho = rho_next
    return pairs


def halves(x):
    high = x.astype(jnp.bfloat16)
    return high, (x - high.astype(jnp.float32)).astype(jnp.bfloat16)


def product(left, x):
    high, low = halves(x)
    right = jnp.concatenate([high, low, high], axis=0)
    return jnp.dot(left, right, preferred_element_type=jnp.float32)


def store_left(out, rows, x):
    high, low = halves(x)
    width = x.shape[1]
    for place, piece in enumerate((high, high, low)):
        out[rows, place * width : (place + 1) * width] = piece


def take(tile, lane):
    index = jnp.broadcast_to(lane, tile.shape)
    return jnp.take_along_axis(tile, index, axis=1, mode="promise_in_bounds")


def pick(tiles, at, lane):
    out = jnp.zeros(tiles[0].shape, tiles[0].dtype)
    for number, tile in enumerate(tiles):
        out = jnp.where(at == number, take(tile, lane), out)
    return out


def lanes(rows=1):
    return lax.broadcasted_iota(jnp.int32, (rows, LANES), 1)


def cols(j, width, base=None):
    size, start = (width, j * width) if base is None else (LANES, j * width + base)
    return pl.ds(start if isinstance(j, int) else pl.multiple_of(start, LANES), size)


def over(blocks, body):
    if blocks <= 4:
        for j in range(blocks):
            body(j)
    else:
        lax.fori_loop(0, blocks, lambda j, carry: (body(j), carry)[1], 0)


def over_groups(blocks, body):
    size = min(blocks, 4)
    over(blocks // size, lambda g: body([g * size + i for i in range(size)], g))


def own_place():
    me = lax.axis_index("sub")
    return jnp.right_shift(me, 1), jnp.bitwise_and(me, 1)


def trace_tiles(traces):
    points = traces.shape[0] // FACES
    return [
        traces[f * points : (f + 1) * points, h : h + LANES]
        for f in range(FACES)
        for h in range(0, traces.shape[1], LANES)
    ]


def faces(tile_of, js, count):
    return jnp.concatenate(
        [
            jnp.concatenate([tile_of(j, f, h) for j in js for h in range(0, count, LANES)], axis=1)
            for f in range(FACES)
        ],
        axis=0,
    )


def of_block(x, i, count):
    return x[:, i * count : (i + 1) * count]


def send_sub(j, tiles, sub_ref, sub_out, width):
    for h in range(0, width, LANES):
        columns = sub_ref[:, cols(j, width, h)]
        sub_out[:, cols(j, width, h)] = pick(
            tiles, jnp.right_shift(columns, 7), jnp.bitwise_and(columns, LANES - 1)
        )


def send_rim(j, tiles, rim_ref, rim_out, rims):
    group = LANES // rims
    tile = cols(j // group, LANES)
    columns = rim_ref[:, tile]
    rim = pick(tiles, jnp.right_shift(columns, 7), jnp.bitwise_and(columns, LANES - 1))
    mine = lanes() // rims == j % group
    rim_out[:, tile] = jnp.where(mine, rim, rim_out[:, tile])


def prep_kernel(map_ref, stiff_ref, t_out, tt_out, k_out):
    modes, rows = map_ref.shape
    transposed = map_ref[...]
    store_left(tt_out, slice(0, modes), transposed)
    store_left(t_out, slice(0, rows), transposed.T)
    for k in range(2):
        store_left(k_out, slice(k * modes, (k + 1) * modes), stiff_ref[k])


def prep_coarse_kernel(restriction_ref, stiff_ref, down_out, up_out, c_out):
    modes = stiff_ref.shape[0]
    store_left(c_out, slice(0, modes), stiff_ref[...])
    for o in range(OCTANTS):
        rows = slice(o * modes, (o + 1) * modes)
        store_left(down_out, rows, restriction_ref[o])
        store_left(up_out, rows, restriction_ref[o].T)


def pack_kernel(
    b_ref, cond_ref, mat_ref, face_ref, sub_ref, rim_ref, size_ref, coarse_ref, out,
    b_in, cond_in, mat_in, face_in, sub_in, rim_in, size_in, coarse_in, done,
):
    sources = (b_ref, cond_ref, mat_ref, face_ref, sub_ref, rim_ref, size_ref, coarse_ref)
    places = (b_in, cond_in, mat_in, face_in, sub_in, rim_in, size_in, coarse_in)
    copies = [
        pltpu.make_async_copy(source, place, done.at[at])
        for at, (source, place) in enumerate(zip(sources, places))
    ]
    for copy in copies:
        copy.start()
    modes, count = b_in.shape
    out[modes:, :] = jnp.zeros((out.shape[0] - modes, count), jnp.float32)
    for copy in copies:
        copy.wait()
    out[:modes, :] = b_in[...]
    out[modes : modes + 1, :] = cond_in[...]
    out[modes + 1 : modes + 2, :] = mat_in[...].astype(jnp.float32)
    out[modes + 2 : modes + 8, :] = face_in[...].astype(jnp.float32)
    out[modes + 8 : modes + 9, : rim_in.shape[1]] = rim_in[...].astype(jnp.float32)
    out[modes + 9 : modes + 10, : size_in.shape[1]] = size_in[...].astype(jnp.float32)
    out[modes + 10 : modes + 11, : coarse_in.shape[1]] = coarse_in[...]
    width = sub_in.shape[1]
    for at, h in enumerate(range(0, width, count)):
        piece = sub_in[:, h : min(h + count, width)].astype(jnp.float32)
        out[modes + 11 + at : modes + 12 + at, : piece.shape[1]] = piece


def start_kernel(blocks, width, rims, *refs):
    gathered, refs = refs[:blocks], refs[blocks:]
    stiff_ref, map_ref, t_ref = refs[:3]
    b_out, ig_out, meta_out, lane_out, at_out, far_out, edge_out, sub_out, rim_out, size_out, coarse_out = refs[3:14]
    p_out, tr_out, subs_out, rims_out, held = refs[14:]
    modes, count = map_ref.shape[0], gathered[0].shape[1]
    chip, core = own_place()
    for k, ref in enumerate(gathered):
        held[jnp.bitwise_xor(chip, k)] = ref[...]
    eye = lax.broadcasted_iota(jnp.int32, (modes, modes), 0) == lax.broadcasted_iota(
        jnp.int32, (modes, modes), 1
    )
    diagonals = [
        jnp.sum(jnp.where(eye, stiff_ref[k], 0.0), axis=1, keepdims=True) for k in range(2)
    ]
    squares = PENALTY * jnp.sum(map_ref[...] * map_ref[...], axis=1, keepdims=True)
    own_tiles = FACES * count // LANES
    sub_tiles = width // LANES
    rim_out[...] = jnp.zeros(rim_out.shape, jnp.int32)
    rims_out[...] = jnp.zeros(rims_out.shape, jnp.float32)
    peers = blocks * CORES
    slots = width // peers
    group = LANES // rims

    def body(j):
        b = held[j, :modes, :]
        cond = held[j, modes : modes + 1, :]
        mat = held[j, modes + 1 : modes + 2, :]
        b_out[:, cols(j, count)] = b
        meta_out[0:1, cols(j, count)] = cond
        meta_out[1:2, cols(j, count)] = mat
        column = held[j, modes + 2 : modes + 8, :].astype(jnp.int32)
        lane = jnp.bitwise_and(column, LANES - 1)
        at = jnp.right_shift(column, 7)
        lane_out[0:FACES, cols(j, count)] = lane
        at_out[0:FACES, cols(j, count)] = at
        other = jnp.bitwise_and(lax.div(lane, jnp.int32(slots)), 1) != core
        sub = jnp.logical_and(jnp.logical_and(at >= own_tiles, at < own_tiles + sub_tiles), other)
        rim = jnp.logical_and(at == own_tiles + sub_tiles, lane < rims)
        far_out[0:FACES, cols(j, count)] = jnp.where(sub, column - own_tiles * LANES, slots * core)
        edge_out[0:FACES, cols(j, count)] = jnp.where(
            rim, jnp.bitwise_xor(lane, rims // 2) + (j % group) * rims, -1
        )
        for h in range(0, width, LANES):
            row = modes + 11 + h // count
            piece = held[j, row : row + 1, h % count : h % count + LANES]
            sub_out[:, cols(j, width, h)] = piece.astype(jnp.int32)
        row = jnp.broadcast_to(held[j, modes + 8 : modes + 9, :LANES], (8, LANES))
        row = pltpu.roll(row, (j % group) * rims, 1)[0:1].astype(jnp.int32)
        tile = cols(j // group, LANES)
        rim_out[:, tile] = jnp.where(lanes() // rims == j % group, row, rim_out[:, tile])
        size_out[pl.ds(j, 1), :] = held[j, modes + 9 : modes + 10, :LANES].astype(jnp.int32)
        coarse_out[pl.ds(j, 1), :] = held[j, modes + 10 : modes + 11, :LANES]
        inverse = 1.0 / (cond * jnp.where(mat == 1.0, diagonals[1], diagonals[0]) + squares)
        ig_out[:, cols(j, count)] = inverse
        p_out[:, cols(j, count)] = b * inverse * (1.0 / CENTER)

    def first(js, g):
        span = cols(g, len(js) * count)
        traces = product(t_ref[...], p_out[:, span])
        tr_out[:, span] = traces
        for i, j in enumerate(js):
            tiles = trace_tiles(of_block(traces, i, count))
            send_sub(j, tiles, sub_out, subs_out, width)
            send_rim(j, tiles, rim_out, rims_out, rims)

    over(blocks, body)
    over_groups(blocks, first)


def sub_tiles_of(j, sends_ref, core, width, blocks):
    slots = width // (blocks * CORES)
    pairs = LANES // slots // CORES
    lane = lanes()
    mine = lax.axis_index("sub") % CORES
    source = (CORES * (j % pairs) + mine) * slots + lane % slots
    tiles = []
    for t in range(width // LANES):
        tile = None
        for i in range(pairs):
            sent = sends_ref[:, cols(j // pairs, LANES, (pairs * t + i) * width)]
            there = take(sent, source)
            there = jnp.where(lane // slots == CORES * i + core, there, 0.0)
            tile = there if tile is None else tile + there
        tiles.append(tile)
    return tiles


def rim_kernel(blocks, rims, rim_ref, edge_ref, ig_ref, edges_out, igs_out):
    group = LANES // rims
    lane = lanes()
    edges_out[...] = jnp.full(edges_out.shape, -1, jnp.int32)
    igs_out[...] = jnp.zeros(igs_out.shape, jnp.float32)
    count = ig_ref.shape[1] // blocks

    def body(j):
        tile = cols(j // group, LANES)
        mine = lane // rims == j % group
        at, there = rim_element(rim_ref[:, tile], count)
        edges = pick([edge_ref[:, cols(j, count, h)] for h in range(0, count, LANES)], at, there)
        igs = pick([ig_ref[:, cols(j, count, h)] for h in range(0, count, LANES)], at, there)
        edges_out[:, tile] = jnp.where(mine, edges, edges_out[:, tile])
        igs_out[:, tile] = jnp.where(mine, igs, igs_out[:, tile])

    over(blocks, body)


def rim_element(columns, count):
    return jnp.bitwise_and(jnp.right_shift(columns, 7), count // LANES - 1), jnp.bitwise_and(columns, LANES - 1)


def local_kernel(only_own, blocks, width, first, *refs):
    p_ref, tr_ref, subs_ref, meta_ref, lane_ref, at_ref, k_ref = refs[:7]
    refs = refs[7:]
    if not first:
        x_ref, refs = refs[0], refs[1:]
    jump_out, own_out, x_out = refs
    modes = p_ref.shape[0]
    chip, core = own_place()
    count = x_out.shape[1]

    def body(js, span, out):
        traces = tr_ref[:, span]
        at_rows, lane_rows = at_ref[:, span], lane_ref[:, span]
        both = product(k_ref[...], p_ref[:, span])
        meta = meta_ref[:, span]
        own_out[:, out] = meta[0:1] * jnp.where(meta[1:2] == 1.0, both[modes:], both[:modes])
        tiles = [
            trace_tiles(of_block(traces, i, count)) + sub_tiles_of(j, subs_ref, core, width, blocks)
            for i, j in enumerate(js)
        ]

        def tile(i, f, h):
            row, place = slice(f, f + 1), slice(i * count + h, i * count + h + LANES)
            return pick(tiles[i], at_rows[row, place], lane_rows[row, place])

        jump_out[:, out] = traces - faces(tile, range(len(js)), count)

    if only_own:
        body([chip], cols(chip, count), slice(0, count))
    else:
        over_groups(blocks, lambda js, g: body(js, cols(g, len(js) * count), cols(g, len(js) * count)))
    p = p_ref[:, cols(chip, count)]
    x_out[...] = p if first else x_ref[...] + p


def ahead_kernel(kind, coefficients, blocks, width, rims, *refs):
    r_ref, jump_ref, own_ref, swapped_ref, far_ref, tt_ref = refs[:6]
    refs = list(refs[6:])
    chip, core = own_place()
    count = own_ref.shape[1] // (1 if kind == "last" else blocks)
    group = LANES // rims
    lane = lanes()
    p_ref = refs.pop(0) if kind == "step" else None
    if kind in ("step", "first"):
        ig_ref, rim_ref, r_out, p_out, edge_out = refs
        edge_out[...] = jnp.zeros(edge_out.shape, jnp.float32)
    else:
        r_out = refs[0]

    def body(js, span, here):
        tiles = [sub_tiles_of(j, swapped_ref, 1 - core, width, blocks) for j in js]
        far = far_ref[:, span]

        def tile(i, f, h):
            column = far[f : f + 1, i * count + h : i * count + h + LANES]
            if len(tiles[i]) == 1:
                return take(tiles[i][0], column)
            return pick(tiles[i], jnp.right_shift(column, 7), jnp.bitwise_and(column, LANES - 1))

        jump = product(tt_ref[...], jump_ref[:, here] - faces(tile, range(len(js)), count))
        residual = r_ref[:, span] - own_ref[:, here] - PENALTY * jump
        r_out[:, here] = residual
        if kind in ("frame", "last"):
            return
        p = coefficients[1] * (residual * ig_ref[:, here])
        if kind == "step":
            p = p + coefficients[0] * p_ref[:, here]
        p_out[:, here] = p
        for i, j in enumerate(js):
            spot = cols(j // group, LANES)
            at, there = rim_element(rim_ref[:, spot], count)
            mine = of_block(p, i, count)
            edge = pick([mine[:, h : h + LANES] for h in range(0, count, LANES)], at, there)
            edge_out[:, spot] = jnp.where(lane // rims == j % group, edge, edge_out[:, spot])

    if kind == "last":
        body([chip], cols(chip, count), slice(0, count))
    else:
        over_groups(blocks, lambda js, g: body(js, cols(g, len(js) * count), cols(g, len(js) * count)))


def rim_tile(one_ref, two_ref, spot, rims):
    segment, segments = lax.axis_index("blk"), lax.axis_size("blk")
    odd = segment % 2 == 1
    low = jnp.where(odd, one_ref[:, spot], two_ref[:, spot])
    high = jnp.where(odd, two_ref[:, spot], one_ref[:, spot])
    low = jnp.where(segment == 0, 0.0, low)
    high = jnp.where(segment == segments - 1, 0.0, high)
    return jnp.where(lanes() % rims < rims // 2, high, low)


def rim_seen(rim, edge, f, h):
    place = edge[f : f + 1, h : h + LANES]
    return jnp.where(place >= 0, take(rim, jnp.bitwise_and(place, LANES - 1)), 0.0)


def edge_kernel(rate, rims, one_ref, two_ref, edges_ref, igs_ref, p_ref, tt_ref, t_ref, rim_ref, rims_out):
    points = one_ref.shape[0]
    for t in range(one_ref.shape[1] // LANES):
        spot = slice(t * LANES, (t + 1) * LANES)
        rim = rim_tile(one_ref, two_ref, spot, rims)
        edge = edges_ref[:, spot]
        added = product(tt_ref[...], faces(lambda _, f, h: rim_seen(rim, edge, f, h), [0], LANES))
        p = p_ref[:, spot] + (rate * PENALTY) * (igs_ref[:, spot] * added)
        traces = product(t_ref[...], p)
        face = rim_ref[:, spot]
        out = jnp.zeros((points, LANES), jnp.float32)
        for f in range(FACES):
            out = jnp.where(face == f, traces[f * points : (f + 1) * points], out)
        rims_out[:, spot] = out


def finish_kernel(kind, rate, blocks, width, rims, *refs):
    r_ref, one_ref, two_ref, edge_ref, tt_ref = refs[:5]
    refs = list(refs[5:])
    chip, core = own_place()
    group = LANES // rims
    lane = lanes()
    if kind in ("step", "first"):
        p_ref, ig_ref, t_ref, sub_ref, _, r_out, p_out, tr_out, subs_out = refs
    elif kind == "frame":
        r_out, head_out = refs
        head_out[...] = jnp.zeros(head_out.shape, jnp.float32)
    else:
        r_out = refs[0]
    count = r_out.shape[1] // (1 if kind == "last" else blocks)

    def body(js, span, here):
        rim = [rim_tile(one_ref, two_ref, cols(j // group, LANES), rims) for j in js]
        edge = edge_ref[:, span]

        def tile(i, f, h):
            return rim_seen(rim[i], edge, f, i * count + h)

        added = PENALTY * product(tt_ref[...], faces(tile, range(len(js)), count))
        residual = r_ref[:, here] + added
        r_out[:, here] = residual
        if kind == "frame":
            heads = LANES // HEAD
            for i, j in enumerate(js):
                spot = cols(j // heads, LANES)
                moved = pltpu.roll(of_block(residual, i, count)[:, :LANES], (j % heads) * HEAD, 1)
                head_out[:, spot] = jnp.where(lane // HEAD == j % heads, moved, head_out[:, spot])
        if kind in ("frame", "last"):
            return
        p = p_ref[:, here] + rate * (ig_ref[:, here] * added)
        p_out[:, here] = p
        traces = product(t_ref[...], p)
        tr_out[:, here] = traces
        for i, j in enumerate(js):
            send_sub(j, trace_tiles(of_block(traces, i, count)), sub_ref, subs_out, width)

    if kind == "last":
        body([chip], cols(chip, count), slice(0, count))
    else:
        over_groups(blocks, lambda js, g: body(js, cols(g, len(js) * count), cols(g, len(js) * count)))


def layout_kernel(blocks, parents, size_ref, gather_out, parent_out, octant_out):
    row = lax.broadcasted_iota(jnp.int32, (parents, LANES), 0)
    lane = lanes(parents)
    pairs = LANES // parents
    group = jnp.bitwise_and(lane, parents - 1)
    half = jnp.right_shift(lanes(), parents.bit_length() - 1)
    count = parent_out.shape[1] // blocks

    def body(j):
        sizes = jnp.broadcast_to(size_ref[pl.ds(j, 1), :], (parents, LANES))
        size = jnp.sum(jnp.where(row == lane, sizes, 0), axis=1, keepdims=True)
        end = jnp.sum(jnp.where(lane <= row, sizes, 0), axis=1, keepdims=True)
        size_row = jnp.sum(jnp.where(row == group, size, 0), axis=0, keepdims=True)
        start_row = jnp.sum(jnp.where(row < group, size, 0), axis=0, keepdims=True)
        for i in range(OCTANTS // pairs):
            octant = pairs * i + half
            place = jnp.bitwise_and(start_row + octant + HEAD, count - 1)
            gather_out[i : i + 1, cols(j, LANES)] = jnp.where(octant < size_row, place, -1)
        for h in range(0, count, LANES):
            position = jnp.bitwise_and(lane + (h - HEAD), count - 1)
            before = end <= position
            parent = jnp.sum(before.astype(jnp.int32), axis=0, keepdims=True)
            start = jnp.sum(jnp.where(before, size, 0), axis=0, keepdims=True)
            parent_out[:, cols(j, count, h)] = parent + parents * (j % pairs)
            octant_out[:, cols(j, count, h)] = position[0:1] - start

    over(blocks, body)


def heads_of(j, swapped_ref, cross_ref, by, blocks):
    chip, core = own_place()
    heads = LANES // HEAD
    lane = lanes()
    apart = core if by == 1 else 1 - core
    source = j + by * apart
    inside = jnp.logical_and(source >= 0, source < blocks)
    at = jnp.clip(source, 0, blocks - 1)
    edge = 0 if by == 1 else blocks - 1
    tile = pl.ds(pl.multiple_of((at // heads) * LANES, LANES), LANES)
    near = pltpu.roll(swapped_ref[:, tile], (LANES - (at % heads) * HEAD) % LANES, 1)
    cross = cross_ref[:, (edge // heads) * LANES : (edge // heads + 1) * LANES]
    if edge % heads:
        cross = pltpu.roll(cross, LANES - (edge % heads) * HEAD, 1)
    segment, segments = lax.axis_index("blk"), lax.axis_size("blk")
    outside = segment == (segments - 1 if by == 1 else 0)
    cross = jnp.where(outside, 0.0, cross)
    return jnp.where(lane < HEAD, jnp.where(inside, near, cross), 0.0)


def coarse_kernel(
    blocks, parents, r_ref, swapped_ref, cross_ref, gather_ref, parent_ref, octant_ref, cond_ref, stiff_ref,
    down_ref, up_ref, c_ref, field_out, tail_out, right, field_ref, lifted,
):
    modes = r_ref.shape[0]
    count = r_ref.shape[1] // blocks
    lane = lanes()
    pairs = LANES // parents

    def restrict(j):
        arriving = heads_of(j, swapped_ref, cross_ref, 1, blocks)
        sources = [r_ref[:, cols(j, count, h)] for h in range(0, count, LANES)]
        sources[0] = jnp.where(lane < HEAD, arriving, sources[0])
        sums = [None] * pairs
        for i in range(OCTANTS // pairs):
            place = gather_ref[i : i + 1, cols(j, LANES)]
            children = pick(sources, jnp.right_shift(place, 7), jnp.bitwise_and(place, LANES - 1))
            both = product(down_ref[pairs * i * modes : pairs * (i + 1) * modes, :], children)
            for k in range(pairs):
                one = both[k * modes : (k + 1) * modes]
                sums[k] = one if sums[k] is None else sums[k] + one
        total = sums[0]
        for k in range(1, pairs):
            total = total + pltpu.roll(sums[k], LANES - k * parents, 1)
        tile = cols(j // pairs, LANES)
        moved = pltpu.roll(total, (j % pairs) * parents, 1)
        right[:, tile] = jnp.where(lane // parents == j % pairs, moved, right[:, tile])

    right[...] = jnp.zeros(right.shape, jnp.float32)
    over(blocks, restrict)
    eye = lax.broadcasted_iota(jnp.int32, (modes, modes), 0) == lax.broadcasted_iota(
        jnp.int32, (modes, modes), 1
    )
    diagonal = jnp.sum(jnp.where(eye, stiff_ref[...], 0.0), axis=1, keepdims=True)

    def solve(t):
        scale = jnp.zeros((1, LANES), jnp.float32)
        for k in range(pairs):
            row = jnp.broadcast_to(cond_ref[pl.ds(pairs * t + k, 1), :], (8, LANES))
            row = pltpu.roll(row, k * parents, 1)[0:1] if k else row[0:1]
            scale = jnp.where(lane // parents == k, row, scale)
        inverse = 1.0 / (scale * diagonal + 2.0 * COUPLING)
        residual = right[:, cols(t, LANES)]
        p = residual * inverse * (1.0 / CENTER)
        field = p
        for before, correct in steps(KC - 1):
            left = jnp.where(lane % parents == 0, 0.0, pltpu.roll(p, 1, 1))
            after = jnp.where(lane % parents == parents - 1, 0.0, pltpu.roll(p, LANES - 1, 1))
            residual = residual - (
                scale * product(c_ref[...], p) + COUPLING * (2.0 * p - left - after)
            )
            p = before * p + correct * (residual * inverse)
            field = field + p
        lifted[:, cols(t, LANES)] = product(up_ref[...], field)

    over(blocks // pairs, solve)
    tail_out[...] = jnp.zeros(tail_out.shape, jnp.float32)
    heads = LANES // HEAD

    def prolong(j):
        sources = [lifted[o * modes : (o + 1) * modes, cols(j // pairs, LANES)] for o in range(OCTANTS)]
        for h in range(0, count, LANES):
            parent, octant = parent_ref[:, cols(j, count, h)], octant_ref[:, cols(j, count, h)]
            out = pick(sources, octant, parent)
            field_out[:, cols(j, count, h)] = out
            if h == 0:
                spot = cols(j // heads, LANES)
                moved = pltpu.roll(out, (j % heads) * HEAD, 1)
                tail_out[:, spot] = jnp.where(lane // HEAD == j % heads, moved, tail_out[:, spot])

    over(blocks, prolong)


def middle_kernel(
    blocks, width, rims, field_ref, swapped_ref, cross_ref, t_ref, sub_ref, rim_ref, p_out, tr_out, subs_out, rims_out
):
    count = field_ref.shape[1] // blocks
    lane = lanes()
    rims_out[...] = jnp.zeros(rims_out.shape, jnp.float32)

    def body(js, g):
        span = cols(g, len(js) * count)
        for j in js:
            arriving = heads_of(j, swapped_ref, cross_ref, -1, blocks)
            p_out[:, cols(j, count)] = field_ref[:, cols(j, count)]
            first = cols(j, count, 0)
            p_out[:, first] = jnp.where(lane < HEAD, arriving, field_ref[:, first])
        traces = product(t_ref[...], p_out[:, span])
        tr_out[:, span] = traces
        for i, j in enumerate(js):
            tiles = trace_tiles(of_block(traces, i, count))
            send_sub(j, tiles, sub_ref, subs_out, width)
            send_rim(j, tiles, rim_ref, rims_out, rims)

    over_groups(blocks, body)


def call(limit, kernel, outs, *args, scratch=(), hbm=False):
    return pl.pallas_call(
        kernel,
        out_shape=[jax.ShapeDtypeStruct(shape, kind) for shape, kind in outs],
        in_specs=[pl.BlockSpec(memory_space=pltpu.HBM if hbm else pltpu.VMEM)] * len(args),
        out_specs=[pl.BlockSpec(memory_space=pltpu.VMEM)] * len(outs),
        scratch_shapes=list(scratch),
        compiler_params=pltpu.CompilerParams(vmem_limit_bytes=limit),
        cost_estimate=pl.CostEstimate(flops=10**9, bytes_accessed=1, transcendentals=0),
    )(*args)


def local(
    right_side,
    conductivity,
    material,
    stiffness,
    trace_map,
    face_neighbour,
    sub_sends,
    blk_sends,
    group_sizes,
    coarse_conductivity,
    coarse_stiffness,
    restriction,
):
    f32, i32, bf16 = jnp.float32, jnp.int32, jnp.bfloat16
    modes, count = right_side.shape
    rows = trace_map.shape[0]
    points = rows // FACES
    peers, segments = lax.axis_size("sub"), lax.axis_size("blk")
    blocks = peers // CORES
    width, rims = sub_sends.shape[1], blk_sends.shape[1]
    parents = group_sizes.shape[1]
    total = blocks * count
    limit = (4 << 20) if blocks <= 4 else (40 << 20)
    run = functools.partial(call, limit)

    def pad(size, to):
        return -(-size // to) * to

    rim_width = pad(blocks * rims, LANES)
    head_width = pad(blocks * HEAD, LANES)
    field = ((modes, total), f32)
    block = ((modes, count), f32)
    sends = [((rows, total), f32), ((points, blocks * width), f32), ((points, rim_width), f32)]

    def everywhere(partner):
        pairs = []
        for b in range(segments):
            for s in range(peers):
                other_b, other_s = partner(b, s)
                pairs.append((b * peers + s, other_b * peers + other_s))
        return pairs

    def above_or_below(first):
        def partner(b, s):
            other = b + 1 if b % 2 == first else b - 1
            return (other, s) if 0 <= other < segments else (b, s ^ 2)

        return everywhere(partner)

    def crossing(b, s):
        other = b - 1 if s % 2 == 0 else b + 1
        return (other, s ^ 1) if 0 <= other < segments else (b, s ^ 2)

    both = ("blk", "sub")
    cores = [(s, s ^ 1) for s in range(peers)]
    ones, twos, crossings = above_or_below(0), above_or_below(1), everywhere(crossing)

    def over_segments(rim):
        return lax.ppermute(rim, both, ones), lax.ppermute(rim, both, twos)

    def shift(heads):
        return lax.ppermute(heads, "sub", cores), lax.ppermute(heads, both, crossings)

    map_t = trace_map.T
    t3, tt3, k3 = run(
        prep_kernel,
        [((rows, 3 * modes), bf16), ((modes, 3 * rows), bf16), ((2 * modes, 3 * modes), bf16)],
        map_t, stiffness,
    )
    height = pad(modes + 11 + pad(width, count) // count, 8)
    inputs = [
        right_side, conductivity.reshape(1, count), material.reshape(1, count), face_neighbour, sub_sends, blk_sends,
        group_sizes, coarse_conductivity.reshape(1, -1),
    ]
    (packed,) = run(
        pack_kernel,
        [((height, count), f32)],
        *inputs,
        scratch=[pltpu.VMEM(x.shape, x.dtype) for x in inputs] + [pltpu.SemaphoreType.DMA((len(inputs),))],
        hbm=True,
    )
    gathered = [packed] + [
        lax.ppermute(packed, "sub", [(s, s ^ (CORES * k)) for s in range(peers)]) for k in range(1, blocks)
    ]
    b, inverse, meta, lane, at, far, edge, subs, rim, sizes, coarse_cond, p, traces, sub_out, rim_out = run(
        functools.partial(start_kernel, blocks, width, rims),
        [
            field, field, ((8, total), f32), *[((8, total), i32)] * 4,
            ((1, blocks * width), i32), ((1, rim_width), i32), ((blocks, LANES), i32), ((blocks, LANES), f32),
            field, *sends,
        ],
        *gathered, stiffness, map_t, t3,
        scratch=[pltpu.VMEM((blocks, height, count), f32)],
    )

    edges, igs = run(
        functools.partial(rim_kernel, blocks, rims), [((8, rim_width), i32), ((modes, rim_width), f32)], rim, edge, inverse
    )
    spot = jnp.arange(rim_width, dtype=i32)[None, :]
    rim_face = jnp.where(spot < blocks * rims, lax.div(rim, jnp.int32(count)), -1)

    def apply(kind, coefficients, r, p, traces, sub_out, rim_out, x):
        one, two = over_segments(rim_out)
        swapped = lax.ppermute(sub_out, "sub", cores)
        only_own = kind == "last"
        size = count if only_own else total
        part, col = ((modes, size), f32), ((rows, size), f32)
        jump, own, x = run(
            functools.partial(local_kernel, only_own, blocks, width, x is None),
            [col, part, block],
            p, traces, sub_out, meta, lane, at, k3, *([] if x is None else [x]),
        )
        goes_on = kind in ("step", "first")
        kernel = functools.partial(ahead_kernel, kind, coefficients, blocks, width, rims)
        args = [r, jump, own, swapped, far, tt3] + ([p] if kind == "step" else [])
        if not goes_on:
            (r,) = run(kernel, [part], *args)
            outs = [block] if only_own else [field, ((modes, head_width), f32)]
            kernel = functools.partial(finish_kernel, kind, None, blocks, width, rims)
            return *run(kernel, outs, r, one, two, edge, tt3), x
        r, p, p_edge = run(kernel, [field, field, ((modes, rim_width), f32)], *args, inverse, rim)
        rate = coefficients[1]
        (rim_out,) = run(
            functools.partial(edge_kernel, rate, rims), [((points, rim_width), f32)],
            one, two, edges, igs, p_edge, tt3, t3, rim_face,
        )
        r, p, traces, sub_out = run(
            functools.partial(finish_kernel, kind, rate, blocks, width, rims),
            [field, field, ((rows, total), f32), ((points, blocks * width), f32)],
            r, one, two, edge, tt3, p, inverse, t3, subs, rim_out,
        )
        return r, p, traces, sub_out, rim_out, x

    gather, parent, octant = run(
        functools.partial(layout_kernel, blocks, parents),
        [((OCTANTS * parents // LANES, blocks * LANES), i32), ((1, total), i32), ((1, total), i32)],
        sizes,
    )
    down3, up3, c3 = run(
        prep_coarse_kernel,
        [((OCTANTS * modes, 3 * modes), bf16), ((OCTANTS * modes, 3 * modes), bf16), ((modes, 3 * modes), bf16)],
        restriction, coarse_stiffness,
    )

    x = None
    r = b
    pairs = steps(KF)
    for step in range(KF - 1):
        r, p, traces, sub_out, rim_out, x = apply("step", pairs[step], r, p, traces, sub_out, rim_out, x)
    r, heads, x = apply("frame", None, r, p, traces, sub_out, rim_out, x)

    correction, tails = run(
        functools.partial(coarse_kernel, blocks, parents),
        [field, ((modes, head_width), f32)],
        r, *shift(heads), gather, parent, octant, coarse_cond, coarse_stiffness, down3, up3, c3,
        scratch=[
            pltpu.VMEM((modes, blocks * parents), f32),
            pltpu.VMEM((8, LANES), f32),
            pltpu.VMEM((OCTANTS * modes, blocks * parents), f32),
        ],
    )
    p, traces, sub_out, rim_out = run(
        functools.partial(middle_kernel, blocks, width, rims), [field, *sends], correction, *shift(tails), t3, subs, rim
    )
    r, p, traces, sub_out, rim_out, x = apply("first", (0.0, 1.0 / CENTER), r, p, traces, sub_out, rim_out, x)
    for step in range(KF - 1):
        r, p, traces, sub_out, rim_out, x = apply("step", pairs[step], r, p, traces, sub_out, rim_out, x)
    residual, x = apply("last", None, r, p, traces, sub_out, rim_out, x)
    return x, residual


def solution(mesh):
    in_specs = (
        P(None, ("blk", "sub")),
        P(("blk", "sub")),
        P(("blk", "sub")),
        P(),
        P(),
        P(None, ("blk", "sub")),
        P(("blk", "sub"), None),
        P(("blk", "sub"), None),
        P(("blk", "sub"), None),
        P(("blk", "sub")),
        P(),
        P(),
    )
    out_specs = (P(None, ("blk", "sub")), P(None, ("blk", "sub")))
    return jax.shard_map(local, mesh=mesh, in_specs=in_specs, out_specs=out_specs, check_vma=False)
```

```python
import functools

import jax
import jax.numpy as jnp
from jax import lax
from jax.experimental import pallas as pl
from jax.experimental.pallas import tpu as pltpu
from jax.sharding import PartitionSpec as P

HEAD = 8
KF = 3
KC = 4
FACES = 6
OCTANTS = 8
LANES = 128
CORES = 2

PENALTY = 0.3
COUPLING = 0.5
LOW_EIG = 0.4
HIGH_EIG = 2.5
CENTER = 0.5 * (HIGH_EIG + LOW_EIG)
HALF = 0.5 * (HIGH_EIG - LOW_EIG)


def steps(sweeps):
    sigma = CENTER / HALF
    rho, pairs = 1.0 / sigma, []
    for _ in range(sweeps):
        rho_next = 1.0 / (2.0 * sigma - rho)
        pairs.append((rho_next * rho, 2.0 * rho_next / HALF))
        rho = rho_next
    return pairs


def halves(x):
    high = x.astype(jnp.bfloat16)
    return high, (x - high.astype(jnp.float32)).astype(jnp.bfloat16)


def product(left, x):
    high, low = halves(x)
    right = jnp.concatenate([high, low, high], axis=0)
    return jnp.dot(left, right, preferred_element_type=jnp.float32)


def store_left(out, rows, x, base=0):
    high, low = halves(x)
    width = x.shape[1]
    for place, piece in enumerate((high, high, low)):
        out[rows, base + place * width : base + (place + 1) * width] = piece


def take(tile, lane):
    index = jnp.broadcast_to(lane, tile.shape)
    return jnp.take_along_axis(tile, index, axis=1, mode="promise_in_bounds")


def pick(tiles, at, lane):
    out = jnp.zeros(tiles[0].shape, tiles[0].dtype)
    for number, tile in enumerate(tiles):
        out = jnp.where(at == number, take(tile, lane), out)
    return out


def lanes(rows=1):
    return lax.broadcasted_iota(jnp.int32, (rows, LANES), 1)


def cols(j, width, base=None):
    size, start = (width, j * width) if base is None else (LANES, j * width + base)
    return pl.ds(start if isinstance(j, int) else pl.multiple_of(start, LANES), size)


def over(blocks, body):
    if blocks <= 4:
        for j in range(blocks):
            body(j)
    else:
        lax.fori_loop(0, blocks, lambda j, carry: (body(j), carry)[1], 0)


def over_groups(blocks, body):
    size = min(blocks, 4)
    over(blocks // size, lambda g: body([g * size + i for i in range(size)], g))


def own_place():
    me = lax.axis_index("sub")
    return jnp.right_shift(me, 1), jnp.bitwise_and(me, 1)


def trace_tiles(traces):
    points = traces.shape[0] // FACES
    return [
        traces[f * points : (f + 1) * points, h : h + LANES]
        for f in range(FACES)
        for h in range(0, traces.shape[1], LANES)
    ]


def faces(tile_of, js, count):
    return jnp.concatenate(
        [
            jnp.concatenate([tile_of(j, f, h) for j in js for h in range(0, count, LANES)], axis=1)
            for f in range(FACES)
        ],
        axis=0,
    )


def of_block(x, i, count):
    return x[:, i * count : (i + 1) * count]


def send_sub(j, tiles, sub_ref, sub_out, width):
    for h in range(0, width, LANES):
        columns = sub_ref[:, cols(j, width, h)]
        sub_out[:, cols(j, width, h)] = pick(
            tiles, jnp.right_shift(columns, 7), jnp.bitwise_and(columns, LANES - 1)
        )


def send_rim(j, tiles, rim_ref, rim_out, rims):
    group = LANES // rims
    tile = cols(j // group, LANES)
    columns = rim_ref[:, tile]
    rim = pick(tiles, jnp.right_shift(columns, 7), jnp.bitwise_and(columns, LANES - 1))
    mine = lanes() // rims == j % group
    rim_out[:, tile] = jnp.where(mine, rim, rim_out[:, tile])


def prep_kernel(map_ref, stiff_ref, t_out, tt_out, k_out):
    modes, rows = map_ref.shape
    transposed = map_ref[...]
    store_left(tt_out, slice(0, modes), transposed)
    store_left(t_out, slice(0, rows), transposed.T)
    for k in range(2):
        store_left(k_out, slice(k * modes, (k + 1) * modes), stiff_ref[k])


def prep_coarse_kernel(restriction_ref, stiff_ref, down_out, up_out, c_out):
    modes = stiff_ref.shape[0]
    store_left(c_out, slice(0, modes), stiff_ref[...])
    pairs = down_out.shape[0] // modes
    for o in range(OCTANTS):
        rows = slice(o % pairs * modes, (o % pairs + 1) * modes)
        store_left(down_out, rows, restriction_ref[o], o // pairs * 3 * modes)
        store_left(up_out, slice(0, modes), restriction_ref[o].T, o * 3 * modes)


def pack_kernel(
    b_ref, cond_ref, mat_ref, face_ref, sub_ref, rim_ref, size_ref, coarse_ref, out,
    b_in, cond_in, mat_in, face_in, sub_in, rim_in, size_in, coarse_in, done,
):
    sources = (b_ref, cond_ref, mat_ref, face_ref, sub_ref, rim_ref, size_ref, coarse_ref)
    places = (b_in, cond_in, mat_in, face_in, sub_in, rim_in, size_in, coarse_in)
    copies = [
        pltpu.make_async_copy(source, place, done.at[at])
        for at, (source, place) in enumerate(zip(sources, places))
    ]
    for copy in copies:
        copy.start()
    modes, count = b_in.shape
    out[modes:, :] = jnp.zeros((out.shape[0] - modes, count), jnp.float32)
    for copy in copies:
        copy.wait()
    out[:modes, :] = b_in[...]
    out[modes : modes + 1, :] = cond_in[...]
    out[modes + 1 : modes + 2, :] = mat_in[...].astype(jnp.float32)
    out[modes + 2 : modes + 8, :] = face_in[...].astype(jnp.float32)
    out[modes + 8 : modes + 9, : rim_in.shape[1]] = rim_in[...].astype(jnp.float32)
    out[modes + 9 : modes + 10, : size_in.shape[1]] = size_in[...].astype(jnp.float32)
    out[modes + 10 : modes + 11, : coarse_in.shape[1]] = coarse_in[...]
    width = sub_in.shape[1]
    for at, h in enumerate(range(0, width, count)):
        piece = sub_in[:, h : min(h + count, width)].astype(jnp.float32)
        out[modes + 11 + at : modes + 12 + at, : piece.shape[1]] = piece


def start_kernel(blocks, width, rims, *refs):
    gathered, refs = refs[:blocks], refs[blocks:]
    stiff_ref, map_ref, t_ref, _ = refs[:4]
    b_out, ig_out, meta_out, lane_out, at_out, far_out, edge_out, sub_out, rim_out, size_out, coarse_out = refs[4:15]
    p_out, tr_out, subs_out, rims_out, held = refs[15:]
    modes, count = map_ref.shape[0], gathered[0].shape[1]
    chip, core = own_place()
    for k, ref in enumerate(gathered):
        held[jnp.bitwise_xor(chip, k)] = ref[...]
    eye = lax.broadcasted_iota(jnp.int32, (modes, modes), 0) == lax.broadcasted_iota(
        jnp.int32, (modes, modes), 1
    )
    diagonals = [
        jnp.sum(jnp.where(eye, stiff_ref[k], 0.0), axis=1, keepdims=True) for k in range(2)
    ]
    squares = PENALTY * jnp.sum(map_ref[...] * map_ref[...], axis=1, keepdims=True)
    own_tiles = FACES * count // LANES
    sub_tiles = width // LANES
    rim_out[...] = jnp.zeros(rim_out.shape, jnp.int32)
    rims_out[...] = jnp.zeros(rims_out.shape, jnp.float32)
    peers = blocks * CORES
    slots = width // peers
    group = LANES // rims

    def body(j):
        b = held[j, :modes, :]
        cond = held[j, modes : modes + 1, :]
        mat = held[j, modes + 1 : modes + 2, :]
        b_out[:, cols(j, count)] = b
        meta_out[0:1, cols(j, count)] = cond
        meta_out[1:2, cols(j, count)] = mat
        column = held[j, modes + 2 : modes + 8, :].astype(jnp.int32)
        lane = jnp.bitwise_and(column, LANES - 1)
        at = jnp.right_shift(column, 7)
        lane_out[0:FACES, cols(j, count)] = lane
        at_out[0:FACES, cols(j, count)] = at
        other = jnp.bitwise_and(lax.div(lane, jnp.int32(slots)), 1) != core
        sub = jnp.logical_and(jnp.logical_and(at >= own_tiles, at < own_tiles + sub_tiles), other)
        rim = jnp.logical_and(at == own_tiles + sub_tiles, lane < rims)
        far_out[0:FACES, cols(j, count)] = jnp.where(sub, column - own_tiles * LANES, slots * core)
        edge_out[0:FACES, cols(j, count)] = jnp.where(
            rim, jnp.bitwise_xor(lane, rims // 2) + (j % group) * rims, -1
        )
        for h in range(0, width, LANES):
            row = modes + 11 + h // count
            piece = held[j, row : row + 1, h % count : h % count + LANES]
            sub_out[:, cols(j, width, h)] = piece.astype(jnp.int32)
        row = jnp.broadcast_to(held[j, modes + 8 : modes + 9, :LANES], (8, LANES))
        row = pltpu.roll(row, (j % group) * rims, 1)[0:1].astype(jnp.int32)
        tile = cols(j // group, LANES)
        rim_out[:, tile] = jnp.where(lanes() // rims == j % group, row, rim_out[:, tile])
        size_out[pl.ds(j, 1), :] = held[j, modes + 9 : modes + 10, :LANES].astype(jnp.int32)
        coarse_out[pl.ds(j, 1), :] = held[j, modes + 10 : modes + 11, :LANES]
        inverse = 1.0 / (cond * jnp.where(mat == 1.0, diagonals[1], diagonals[0]) + squares)
        ig_out[:, cols(j, count)] = inverse
        p_out[:, cols(j, count)] = b * inverse * (1.0 / CENTER)

    def first(js, g):
        span = cols(g, len(js) * count)
        traces = product(t_ref[...], p_out[:, span])
        tr_out[:, span] = traces
        for i, j in enumerate(js):
            tiles = trace_tiles(of_block(traces, i, count))
            send_sub(j, tiles, sub_out, subs_out, width)
            send_rim(j, tiles, rim_out, rims_out, rims)

    over(blocks, body)
    over_groups(blocks, first)


def sub_tiles_of(j, sends_ref, core, width, blocks):
    slots = width // (blocks * CORES)
    pairs = LANES // slots // CORES
    lane = lanes()
    mine = lax.axis_index("sub") % CORES
    source = (CORES * (j % pairs) + mine) * slots + lane % slots
    tiles = []
    for t in range(width // LANES):
        tile = None
        for i in range(pairs):
            sent = sends_ref[:, cols(j // pairs, LANES, (pairs * t + i) * width)]
            there = take(sent, source)
            there = jnp.where(lane // slots == CORES * i + core, there, 0.0)
            tile = there if tile is None else tile + there
        tiles.append(tile)
    return tiles


def rim_element(columns, count):
    return jnp.bitwise_and(jnp.right_shift(columns, 7), count // LANES - 1), jnp.bitwise_and(columns, LANES - 1)


def local_kernel(only_own, blocks, width, first, *refs):
    p_ref, tr_ref, subs_ref, meta_ref, lane_ref, at_ref, k_ref = refs[:7]
    refs = refs[7:]
    if not first:
        x_ref, refs = refs[0], refs[1:]
    jump_out, own_out, x_out = refs
    modes = p_ref.shape[0]
    chip, core = own_place()
    count = x_out.shape[1]

    def body(js, span, out):
        traces = tr_ref[:, span]
        at_rows, lane_rows = at_ref[:, span], lane_ref[:, span]
        both = product(k_ref[...], p_ref[:, span])
        meta = meta_ref[:, span]
        own_out[:, out] = meta[0:1] * jnp.where(meta[1:2] == 1.0, both[modes:], both[:modes])
        tiles = [
            trace_tiles(of_block(traces, i, count)) + sub_tiles_of(j, subs_ref, core, width, blocks)
            for i, j in enumerate(js)
        ]

        def tile(i, f, h):
            row, place = slice(f, f + 1), slice(i * count + h, i * count + h + LANES)
            return pick(tiles[i], at_rows[row, place], lane_rows[row, place])

        jump_out[:, out] = traces - faces(tile, range(len(js)), count)

    if only_own:
        body([chip], cols(chip, count), slice(0, count))
    else:
        over_groups(blocks, lambda js, g: body(js, cols(g, len(js) * count), cols(g, len(js) * count)))
    p = p_ref[:, cols(chip, count)]
    x_out[...] = p if first else x_ref[...] + p


def ahead_kernel(kind, coefficients, blocks, width, rims, *refs):
    r_ref, jump_ref, own_ref, swapped_ref, far_ref, tt_ref = refs[:6]
    refs = list(refs[6:])
    chip, core = own_place()
    count = own_ref.shape[1] // (1 if kind == "last" else blocks)
    group = LANES // rims
    lane = lanes()
    p_ref = refs.pop(0) if kind == "step" else None
    if kind in ("step", "first"):
        ig_ref, rim_ref, r_out, p_out, edge_out = refs
        edge_out[...] = jnp.zeros(edge_out.shape, jnp.float32)
    else:
        r_out = refs[0]

    def body(js, span, here):
        tiles = [sub_tiles_of(j, swapped_ref, 1 - core, width, blocks) for j in js]
        far = far_ref[:, span]

        def tile(i, f, h):
            column = far[f : f + 1, i * count + h : i * count + h + LANES]
            if len(tiles[i]) == 1:
                return take(tiles[i][0], column)
            return pick(tiles[i], jnp.right_shift(column, 7), jnp.bitwise_and(column, LANES - 1))

        jump = product(tt_ref[...], jump_ref[:, here] - faces(tile, range(len(js)), count))
        residual = r_ref[:, span] - own_ref[:, here] - PENALTY * jump
        r_out[:, here] = residual
        if kind in ("frame", "last"):
            return
        p = coefficients[1] * (residual * ig_ref[:, here])
        if kind == "step":
            p = p + coefficients[0] * p_ref[:, here]
        p_out[:, here] = p
        for i, j in enumerate(js):
            keep_edge(j, of_block(p, i, count), rim_ref, edge_out, rims)

    if kind == "last":
        body([chip], cols(chip, count), slice(0, count))
    else:
        over_groups(blocks, lambda js, g: body(js, cols(g, len(js) * count), cols(g, len(js) * count)))


def rim_tile(one_ref, two_ref, spot, rims):
    segment, segments = lax.axis_index("blk"), lax.axis_size("blk")
    odd = segment % 2 == 1
    low = jnp.where(odd, one_ref[:, spot], two_ref[:, spot])
    high = jnp.where(odd, two_ref[:, spot], one_ref[:, spot])
    low = jnp.where(segment == 0, 0.0, low)
    high = jnp.where(segment == segments - 1, 0.0, high)
    return jnp.where(lanes() % rims < rims // 2, high, low)


def rim_seen(rim, edge, f, h):
    place = edge[f : f + 1, h : h + LANES]
    return jnp.where(place >= 0, take(rim, jnp.bitwise_and(place, LANES - 1)), 0.0)


def keep_edge(j, p, rim_ref, edge_out, rims):
    group = LANES // rims
    spot = cols(j // group, LANES)
    count = p.shape[1]
    at, there = rim_element(rim_ref[:, spot], count)
    edge = pick([p[:, h : h + LANES] for h in range(0, count, LANES)], at, there)
    edge_out[:, spot] = jnp.where(lanes() // rims == j % group, edge, edge_out[:, spot])


def rim_traces(t_ref, p, face):
    traces = product(t_ref[...], p)
    points = traces.shape[0] // FACES
    out = jnp.zeros((points, p.shape[1]), jnp.float32)
    for f in range(FACES):
        out = jnp.where(face == f, traces[f * points : (f + 1) * points], out)
    return out


def edge_kernel(rate, rims, one_ref, two_ref, edges_ref, igs_ref, p_ref, tt_ref, t_ref, face_ref, rims_out):
    for t in range(one_ref.shape[1] // LANES):
        spot = slice(t * LANES, (t + 1) * LANES)
        rim = rim_tile(one_ref, two_ref, spot, rims)
        edge = edges_ref[:, spot]
        added = product(tt_ref[...], faces(lambda _, f, h: rim_seen(rim, edge, f, h), [0], LANES))
        p = p_ref[:, spot] + (rate * PENALTY) * (igs_ref[:, spot] * added)
        rims_out[:, spot] = rim_traces(t_ref, p, face_ref[:, spot])


def cross_kernel(blocks, rims, r_ref, one_ref, two_ref, edge_ref, tt_ref, size_ref, cond_ref, cross_out):
    modes = r_ref.shape[0]
    count = r_ref.shape[1] // blocks
    group = LANES // rims
    chip, core = own_place()
    last = blocks - 1
    first_tile, last_tile = cols(0, count, 0), cols(last, count, count - LANES)
    rim = jnp.where(
        core == 0,
        rim_tile(one_ref, two_ref, cols(0, LANES), rims),
        rim_tile(one_ref, two_ref, cols(last // group, LANES), rims),
    )
    edge = jnp.where(core == 0, edge_ref[:, first_tile], edge_ref[:, last_tile])
    seen = faces(lambda _, f, h: rim_seen(rim, edge, f, h), [0], LANES)
    residual = jnp.where(core == 0, r_ref[:, first_tile], r_ref[:, last_tile])
    cross_out[modes:, :] = jnp.zeros((cross_out.shape[0] - modes, LANES), jnp.float32)
    cross_out[:modes, :] = residual + PENALTY * product(tt_ref[...], seen)
    cross_out[modes : modes + 1, :] = size_ref[last : last + 1, :].astype(jnp.float32)
    cross_out[modes + 1 : modes + 2, :] = cond_ref[last : last + 1, :]


def finish_kernel(kind, rate, blocks, width, rims, *refs):
    r_ref, one_ref, two_ref, edge_ref, tt_ref = refs[:5]
    refs = list(refs[5:])
    chip, core = own_place()
    group = LANES // rims
    lane = lanes()
    if kind in ("step", "first"):
        p_ref, ig_ref, t_ref, sub_ref, _, r_out, p_out, tr_out, subs_out = refs
    elif kind == "frame":
        size_ref, cond_ref, _, r_out, near_out = refs
        near_out[...] = jnp.zeros(near_out.shape, jnp.float32)
    else:
        r_out = refs[0]
    count = r_out.shape[1] // (1 if kind == "last" else blocks)
    modes = r_ref.shape[0]

    def body(js, span, here):
        rim = [rim_tile(one_ref, two_ref, cols(j // group, LANES), rims) for j in js]
        edge = edge_ref[:, span]

        def tile(i, f, h):
            return rim_seen(rim[i], edge, f, i * count + h)

        added = PENALTY * product(tt_ref[...], faces(tile, range(len(js)), count))
        residual = r_ref[:, here] + added
        r_out[:, here] = residual
        if kind == "frame":
            heads = LANES // HEAD
            for i, j in enumerate(js):
                spot = cols(j // heads, LANES)
                mine = of_block(residual, i, count)
                moved = pltpu.roll(mine[:, :LANES], (j % heads) * HEAD, 1)
                near_out[:modes, spot] = jnp.where(lane // HEAD == j % heads, moved, near_out[:modes, spot])
                tail = cols(j, LANES, near_out.shape[1] - blocks * LANES)
                near_out[:modes, tail] = mine[:, count - LANES :]
                near_out[modes : modes + 1, tail] = size_ref[pl.ds(j, 1), :].astype(jnp.float32)
                near_out[modes + 1 : modes + 2, tail] = cond_ref[pl.ds(j, 1), :]
        if kind in ("frame", "last"):
            return
        p = p_ref[:, here] + rate * (ig_ref[:, here] * added)
        p_out[:, here] = p
        traces = product(t_ref[...], p)
        tr_out[:, here] = traces
        for i, j in enumerate(js):
            send_sub(j, trace_tiles(of_block(traces, i, count)), sub_ref, subs_out, width)

    if kind == "last":
        body([chip], cols(chip, count), slice(0, count))
    else:
        over_groups(blocks, lambda js, g: body(js, cols(g, len(js) * count), cols(g, len(js) * count)))


def layout_kernel(blocks, parents, size_ref, gather_out, parent_out, octant_out):
    lane = lanes()
    pairs = LANES // parents
    half = jnp.right_shift(lane, parents.bit_length() - 1)
    count = parent_out.shape[1] // blocks

    def body(j):
        each, end, size, start = children(size_ref[pl.ds(j, 1), :], parents, jnp.bitwise_and(lanes(parents), parents - 1))
        for i in range(OCTANTS // pairs):
            octant = pairs * i + half
            place = jnp.bitwise_and(start + octant + HEAD, count - 1)
            gather_out[i : i + 1, cols(j, LANES)] = jnp.where(octant < size, place, -1)
        for h in range(0, count, LANES):
            position = jnp.bitwise_and(lanes(parents) + (h - HEAD), count - 1)
            parent, octant = owner(each, end, position)
            parent_out[:, cols(j, count, h)] = parent + parents * (j % pairs)
            octant_out[:, cols(j, count, h)] = octant

    over(blocks, body)


def rim_kernel(blocks, rims, rim_ref, edge_ref, ig_ref, edges_out, igs_out):
    group = LANES // rims
    edges_out[...] = jnp.full(edges_out.shape, -1, jnp.int32)
    igs_out[...] = jnp.zeros(igs_out.shape, jnp.float32)
    count = ig_ref.shape[1] // blocks

    def body(j):
        tile = cols(j // group, LANES)
        mine = lanes() // rims == j % group
        at, there = rim_element(rim_ref[:, tile], count)
        edges = pick([edge_ref[:, cols(j, count, h)] for h in range(0, count, LANES)], at, there)
        igs = pick([ig_ref[:, cols(j, count, h)] for h in range(0, count, LANES)], at, there)
        edges_out[:, tile] = jnp.where(mine, edges, edges_out[:, tile])
        igs_out[:, tile] = jnp.where(mine, igs, igs_out[:, tile])

    over(blocks, body)


def children(sizes, parents, wanted):
    row = lax.broadcasted_iota(jnp.int32, (parents, LANES), 0)
    lane = lanes(parents)
    sizes = jnp.broadcast_to(sizes, (parents, LANES))
    each = jnp.sum(jnp.where(row == lane, sizes, 0), axis=1, keepdims=True)
    end = jnp.sum(jnp.where(lane <= row, sizes, 0), axis=1, keepdims=True)
    size = jnp.sum(jnp.where(row == wanted, each, 0), axis=0, keepdims=True)
    start = jnp.sum(jnp.where(row < wanted, each, 0), axis=0, keepdims=True)
    return each, end, size, start


def owner(each, end, position):
    passed = end <= position
    parent = jnp.sum(passed.astype(jnp.int32), axis=0, keepdims=True)
    return parent, position[0:1] - jnp.sum(jnp.where(passed, each, 0), axis=0, keepdims=True)


def restrict(sources, at, lane_of, down_ref):
    parts = []
    for i in range(len(at[0])):
        picked = [pick(*one) for one in zip(sources, [row[i] for row in at], [row[i] for row in lane_of])]
        high, low = halves(jnp.concatenate(picked, axis=1))
        parts += [high, low, high]
    both = jnp.dot(down_ref[...], jnp.concatenate(parts, axis=0), preferred_element_type=jnp.float32)
    modes = sources[0][0].shape[0]
    pairs = both.shape[0] // modes
    width = LANES // pairs
    totals = []
    for b in range(len(sources)):
        mine = both[:, b * LANES : (b + 1) * LANES]
        total = mine[:modes]
        for k in range(1, pairs):
            total = total + pltpu.roll(mine[k * modes : (k + 1) * modes], LANES - k * width, 1)
        totals.append(jnp.where(lanes() < width, total, 0.0))
    return totals


def last_parents(tail, modes, parents, extra):
    wanted = parents - extra + jnp.bitwise_and(lanes(parents), extra - 1)
    each, end, size, start = children(tail[modes : modes + 1].astype(jnp.int32), parents, wanted)
    rows = jnp.broadcast_to(tail[modes + 1 : modes + 2], (8, LANES))
    conds = take(rows, wanted[0:1])[0:1]
    total = jnp.sum(each, axis=0, keepdims=True)
    position = total - HEAD + jnp.bitwise_and(lanes(parents), HEAD - 1)
    parent, octant = owner(each, end, position)
    return size, start, conds, parent - (parents - extra), octant


def restrict_kernel(
    blocks, parents, r_ref, near_ref, gather_ref, cond_ref, down_ref, right_out, scale_out, front_out
):
    modes = r_ref.shape[0]
    count = r_ref.shape[1] // blocks
    lane = lanes()
    pairs = LANES // parents
    heads = LANES // HEAD
    extra = LANES // OCTANTS
    packed = parents // extra
    chip, core = own_place()
    own_tiles = blocks // pairs
    tails = near_ref.shape[1] - blocks * LANES
    right_out[...] = jnp.zeros(right_out.shape, jnp.float32)
    scale_out[...] = jnp.ones(scale_out.shape, jnp.float32)

    def body(js, g):
        sources, at, there = [], [], []
        for j in js:
            source = j + core
            tile = pl.ds(pl.multiple_of((jnp.minimum(source, blocks - 1) // heads) * LANES, LANES), LANES)
            arriving = pltpu.roll(near_ref[:modes, tile], (LANES - (source % heads) * HEAD) % LANES, 1)
            arriving = jnp.where(source < blocks, arriving, 0.0)
            own = [r_ref[:, cols(j, count, h)] for h in range(0, count, LANES)]
            sources.append([jnp.where(lane < HEAD, arriving, own[0])] + own[1:])
            places = [gather_ref[i : i + 1, cols(j, LANES)] for i in range(OCTANTS // pairs)]
            at.append([jnp.right_shift(place, 7) for place in places])
            there.append([jnp.bitwise_and(place, LANES - 1) for place in places])
            mine = jnp.broadcast_to(cond_ref[pl.ds(j, 1), :], (8, LANES))
            mine = pltpu.roll(mine, (j % pairs) * parents, 1)[0:1]
            spot = cols(j // pairs, LANES)
            scale_out[:, spot] = jnp.where(lane // parents == j % pairs, mine, scale_out[:, spot])
        before(js[0] // packed, sources, at, there)
        totals = restrict(sources, at, there, down_ref)
        for j, total in zip(js, totals):
            spot = cols(j // pairs, LANES)
            right_out[:, spot] = right_out[:, spot] + pltpu.roll(total, (j % pairs) * parents, 1)
        v = js[0] // packed
        spot = cols(v // pairs, LANES, own_tiles * LANES)
        right_out[:, spot] = right_out[:, spot] + pltpu.roll(totals[-1], (v % pairs) * parents, 1)

    def before(v, all_sources, all_at, all_there):
        group = jnp.bitwise_and(lane // extra, packed - 1)
        sources = []
        start = size = head_parent = head_octant = jnp.zeros((1, LANES), jnp.int32)
        conds = jnp.ones((1, LANES), jnp.float32)
        for i in range(packed):
            j = packed * v + i
            at = j - (1 - core)
            tail = near_ref[:, pl.ds(pl.multiple_of(tails + jnp.maximum(at, 0) * LANES, LANES), LANES)]
            sources.append(jnp.where(lane < HEAD, r_ref[:, cols(j, count, 0)], tail[:modes]))
            one_size, one_start, one_cond, parent, octant = last_parents(tail, modes, parents, extra)
            mine = group == i
            size = jnp.where(jnp.logical_and(mine, at >= 0), one_size, size)
            start = jnp.where(mine, one_start, start)
            conds = jnp.where(jnp.logical_and(mine, lane < parents), one_cond, conds)
            here = lane // HEAD == j % heads
            head_parent = jnp.where(here, parent + (v % pairs) * parents + i * extra, head_parent)
            head_octant = jnp.where(here, octant, head_octant)
        octants = [pairs * i + lane // parents for i in range(OCTANTS // pairs)]
        all_sources.append(sources)
        all_at.append([jnp.where(octant < size, group, -1) for octant in octants])
        all_there.append([jnp.bitwise_and(start + octant + HEAD, LANES - 1) for octant in octants])
        spot = cols(v // pairs, LANES, own_tiles * LANES)
        conds = pltpu.roll(jnp.broadcast_to(conds, (8, LANES)), (v % pairs) * parents, 1)[0:1]
        scale_out[:, spot] = jnp.where(lane // parents == v % pairs, conds, scale_out[:, spot])
        front_out[v, 0:1, :LANES] = head_parent
        front_out[v, 0:1, LANES:] = head_octant

    over_groups(blocks, body)


def coarse_kernel(
    blocks, parents, rims, right_ref, scale_ref, front_ref, r_ref, cross_ref, gather_ref, parent_ref, octant_ref,
    stiff_ref, down_ref, up_ref, c_ref, t_ref, rim_ref, face_ref, p_out, rims_out, right, scale, front, edge,
):
    modes = r_ref.shape[0]
    count = r_ref.shape[1] // blocks
    lane = lanes()
    pairs = LANES // parents
    heads = LANES // HEAD
    extra = LANES // OCTANTS
    packed = parents // extra
    chip, core = own_place()
    segment, segments = lax.axis_index("blk"), lax.axis_size("blk")
    own_tiles = blocks // pairs
    edge[...] = jnp.zeros(edge.shape, jnp.float32)
    right[...] = right_ref[...]
    scale[...] = scale_ref[...]
    front[...] = front_ref[...]

    cross = cross_ref[...]
    size, start, conds, parent, octant = last_parents(cross, modes, parents, extra)
    above = jnp.where(jnp.logical_and(lane < HEAD, segment < segments - 1), cross[:modes], 0.0)
    below = jnp.where(lane < HEAD, r_ref[:, :LANES], cross[:modes])
    below = jnp.where(segment == 0, 0.0, below)
    at, there = [], []
    for i in range(OCTANTS // pairs):
        place = gather_ref[i : i + 1, cols(blocks - 1, LANES)]
        one = pairs * i + lane // parents
        inside = jnp.logical_and(place >= 0, place < HEAD)
        mine = jnp.logical_and(jnp.bitwise_and(lane, parents - 1) < extra, one < size)
        at.append(jnp.where(core == 1, jnp.where(inside, 0, -1), jnp.where(mine, 0, -1)))
        there.append(jnp.bitwise_and(jnp.where(core == 1, place, start + one + HEAD), LANES - 1))
    (added,) = restrict([[jnp.where(core == 1, above, below)]], [at], [there], down_ref)
    spot = cols((blocks - 1) // pairs, LANES)
    moved = pltpu.roll(added, ((blocks - 1) % pairs) * parents, 1)
    right[:, spot] = right[:, spot] + jnp.where(core == 1, moved, 0.0)
    spot = cols(0, LANES, own_tiles * LANES)
    right[:, spot] = right[:, spot] + jnp.where(core == 0, added, 0.0)
    scale[:, spot] = jnp.where(jnp.logical_and(core == 0, lane < extra), conds, scale[:, spot])
    first = jnp.logical_and(core == 0, lane < HEAD)
    front[0, 0:1, :LANES] = jnp.where(first, parent, front[0, 0:1, :LANES])
    front[0, 0:1, LANES:] = jnp.where(first, octant, front[0, 0:1, LANES:])

    eye = lax.broadcasted_iota(jnp.int32, (modes, modes), 0) == lax.broadcasted_iota(
        jnp.int32, (modes, modes), 1
    )
    diagonal = jnp.sum(jnp.where(eye, stiff_ref[...], 0.0), axis=1, keepdims=True)
    tiles = right.shape[1] // LANES
    inverse = 1.0 / (scale[...] * diagonal + 2.0 * COUPLING)
    residual = right[...]
    p = residual * inverse * (1.0 / CENTER)
    field = p
    for ahead, correct in steps(KC - 1):
        pieces = []
        for t in range(tiles):
            here = p[:, t * LANES : (t + 1) * LANES]
            last = (parents if t < own_tiles else extra) - 1
            left = jnp.where(jnp.bitwise_and(lane, last) == 0, 0.0, pltpu.roll(here, 1, 1))
            after = jnp.where(jnp.bitwise_and(lane, last) == last, 0.0, pltpu.roll(here, LANES - 1, 1))
            pieces.append(left + after)
        sides = jnp.concatenate(pieces, axis=1)
        residual = residual - (scale[...] * product(c_ref[...], p) + COUPLING * (2.0 * p - sides))
        p = ahead * p + correct * (residual * inverse)
        field = field + p
    right[...] = field

    def prolong(js, g):
        span = cols(g, len(js) * count)
        v = js[0] // packed
        leading = take(right[:, cols(own_tiles + v // pairs, LANES)], front[v, 0:1, :LANES])
        leading_octant = jnp.broadcast_to(front[v, 0:1, LANES:], (8, LANES))
        spread, octants = [], []
        for j in js:
            parent = right[:, cols(j // pairs, LANES)]
            back = (LANES - (j % heads) * HEAD) % LANES
            for h in range(0, count, LANES):
                spot = cols(j, count, h)
                one, octant = take(parent, parent_ref[:, spot]), octant_ref[:, spot]
                if h == 0:
                    one = jnp.where(lane < HEAD, pltpu.roll(leading, back, 1), one)
                    octant = jnp.where(lane < HEAD, pltpu.roll(leading_octant, back, 1)[0:1], octant)
                spread.append(one)
                octants.append(octant)
        high, low = halves(jnp.concatenate(spread, axis=1))
        octant = jnp.concatenate(octants, axis=1)
        parts = []
        for o in range(OCTANTS):
            mine = (octant == o).astype(jnp.float32).astype(jnp.bfloat16)
            parts += [high * mine, low * mine, high * mine]
        p = jnp.dot(up_ref[...], jnp.concatenate(parts, axis=0), preferred_element_type=jnp.float32)
        p_out[:, span] = p
        for i, j in enumerate(js):
            keep_edge(j, of_block(p, i, count), rim_ref, edge, rims)

    over_groups(blocks, prolong)
    for t in range(edge.shape[1] // LANES):
        spot = slice(t * LANES, (t + 1) * LANES)
        rims_out[:, spot] = rim_traces(t_ref, edge[:, spot], face_ref[:, spot])


def spread_kernel(blocks, width, p_ref, t_ref, sub_ref, _, tr_out, subs_out):
    count = p_ref.shape[1] // blocks

    def body(js, g):
        span = cols(g, len(js) * count)
        traces = product(t_ref[...], p_ref[:, span])
        tr_out[:, span] = traces
        for i, j in enumerate(js):
            send_sub(j, trace_tiles(of_block(traces, i, count)), sub_ref, subs_out, width)

    over_groups(blocks, body)


def call(limit, kernel, outs, *args, scratch=(), hbm=False, flops=3 * 10**9):
    limit = (60 << 20) if hbm else limit
    return pl.pallas_call(
        kernel,
        out_shape=[jax.ShapeDtypeStruct(shape, kind) for shape, kind in outs],
        in_specs=[pl.BlockSpec(memory_space=pltpu.HBM if hbm else pltpu.VMEM)] * len(args),
        out_specs=[pl.BlockSpec(memory_space=pltpu.VMEM)] * len(outs),
        scratch_shapes=list(scratch),
        compiler_params=pltpu.CompilerParams(vmem_limit_bytes=limit),
        cost_estimate=pl.CostEstimate(flops=flops, bytes_accessed=1, transcendentals=0),
    )(*args)


def local(
    right_side,
    conductivity,
    material,
    stiffness,
    trace_map,
    face_neighbour,
    sub_sends,
    blk_sends,
    group_sizes,
    coarse_conductivity,
    coarse_stiffness,
    restriction,
):
    f32, i32, bf16 = jnp.float32, jnp.int32, jnp.bfloat16
    modes, count = right_side.shape
    rows = trace_map.shape[0]
    points = rows // FACES
    peers, segments = lax.axis_size("sub"), lax.axis_size("blk")
    blocks = peers // CORES
    parents = group_sizes.shape[1]
    width, rims = sub_sends.shape[1], blk_sends.shape[1]
    total = blocks * count
    limit = (4 << 20) if blocks <= 4 else (40 << 20)
    run = functools.partial(call, limit)

    def pad(size, to):
        return -(-size // to) * to

    rim_width = pad(blocks * rims, LANES)
    near_width = pad(blocks * HEAD, LANES) + blocks * LANES
    field = ((modes, total), f32)
    block = ((modes, count), f32)
    sends = [((rows, total), f32), ((points, blocks * width), f32), ((points, rim_width), f32)]

    def everywhere(partner):
        pairs = []
        for b in range(segments):
            for s in range(peers):
                other_b, other_s = partner(b, s)
                pairs.append((b * peers + s, other_b * peers + other_s))
        return pairs

    def above_or_below(first):
        def partner(b, s):
            other = b + 1 if b % 2 == first else b - 1
            return (other, s) if 0 <= other < segments else (b, s ^ 2)

        return everywhere(partner)

    def crossing(b, s):
        other = b - 1 if s % 2 == 0 else b + 1
        return (other, s ^ 1) if 0 <= other < segments else (b, s ^ 2)

    both = ("blk", "sub")
    cores = [(s, s ^ 1) for s in range(peers)]
    ones, twos, crossings = above_or_below(0), above_or_below(1), everywhere(crossing)

    def over_segments(rim):
        return lax.ppermute(rim, both, ones), lax.ppermute(rim, both, twos)

    map_t = trace_map.T
    t3, tt3, k3 = run(
        prep_kernel,
        [((rows, 3 * modes), bf16), ((modes, 3 * rows), bf16), ((2 * modes, 3 * modes), bf16)],
        map_t, stiffness,
    )
    down3, up3, c3 = run(
        prep_coarse_kernel,
        [((LANES // parents * modes, OCTANTS * parents // LANES * 3 * modes), bf16), ((modes, OCTANTS * 3 * modes), bf16), ((modes, 3 * modes), bf16)],
        restriction, coarse_stiffness,
    )

    height = pad(modes + 11 + pad(width, count) // count, 8)
    inputs = [
        right_side, conductivity.reshape(1, count), material.reshape(1, count), face_neighbour, sub_sends, blk_sends,
        group_sizes, coarse_conductivity.reshape(1, -1),
    ]
    (packed,) = run(
        pack_kernel,
        [((height, count), f32)],
        *inputs,
        scratch=[pltpu.VMEM(x.shape, x.dtype) for x in inputs] + [pltpu.SemaphoreType.DMA((len(inputs),))],
        hbm=True,
    )
    gathered = [packed] + [
        lax.ppermute(packed, "sub", [(s, s ^ (CORES * k)) for s in range(peers)]) for k in range(1, blocks)
    ]
    b, inverse, meta, lane, at, far, edge, subs, rim, sizes, coarse_cond, p, traces, sub_out, rim_out = run(
        functools.partial(start_kernel, blocks, width, rims),
        [
            field, field, ((8, total), f32), *[((8, total), i32)] * 4,
            ((1, blocks * width), i32), ((1, rim_width), i32), ((blocks, LANES), i32), ((blocks, LANES), f32),
            field, *sends,
        ],
        *gathered, stiffness, map_t, t3, c3,
        scratch=[pltpu.VMEM((blocks, height, count), f32)],
    )

    edges, igs = run(
        functools.partial(rim_kernel, blocks, rims), [((8, rim_width), i32), ((modes, rim_width), f32)], rim, edge, inverse
    )
    gather, parent, octant = run(
        functools.partial(layout_kernel, blocks, parents),
        [((OCTANTS * parents // LANES, blocks * LANES), i32), ((1, total), i32), ((1, total), i32)],
        sizes,
        flops=3 * 10**10,
    )
    spot = jnp.arange(rim_width, dtype=i32)[None, :]
    rim_face = jnp.where(spot < blocks * rims, lax.div(rim, jnp.int32(count)), -1)

    def apply(kind, coefficients, r, p, traces, sub_out, rim_out, x):
        one, two = over_segments(rim_out)
        swapped = lax.ppermute(sub_out, "sub", cores)
        only_own = kind == "last"
        size = count if only_own else total
        part, col = ((modes, size), f32), ((rows, size), f32)
        jump, own, x = run(
            functools.partial(local_kernel, only_own, blocks, width, x is None),
            [col, part, block],
            p, traces, sub_out, meta, lane, at, k3, *([] if x is None else [x]),
        )
        goes_on = kind in ("step", "first")
        kernel = functools.partial(ahead_kernel, kind, coefficients, blocks, width, rims)
        args = [r, jump, own, swapped, far, tt3] + ([p] if kind == "step" else [])
        if not goes_on:
            (r,) = run(kernel, [part], *args)
            finish = functools.partial(finish_kernel, kind, None, blocks, width, rims)
            args = [r, one, two, edge, tt3]
            if only_own:
                return *run(finish, [block], *args), x
            args += [sizes, coarse_cond]
            (cross,) = run(functools.partial(cross_kernel, blocks, rims), [((modes + 8, LANES), f32)], *args)
            return *run(finish, [field, ((modes + 8, near_width), f32)], *args, cross), cross, x
        r, p, p_edge = run(kernel, [field, field, ((modes, rim_width), f32)], *args, inverse, rim)
        rate = coefficients[1]
        (rim_out,) = run(
            functools.partial(edge_kernel, rate, rims), [((points, rim_width), f32)],
            one, two, edges, igs, p_edge, tt3, t3, rim_face,
        )
        r, p, traces, sub_out = run(
            functools.partial(finish_kernel, kind, rate, blocks, width, rims),
            [field, field, ((rows, total), f32), ((points, blocks * width), f32)],
            r, one, two, edge, tt3, p, inverse, t3, subs, rim_out,
        )
        return r, p, traces, sub_out, rim_out, x

    x = None
    r = b
    pairs = steps(KF)
    for step in range(KF - 1):
        r, p, traces, sub_out, rim_out, x = apply("step", pairs[step], r, p, traces, sub_out, rim_out, x)
    r, near, cross, x = apply("frame", None, r, p, traces, sub_out, rim_out, x)

    cross = lax.ppermute(cross, both, crossings)
    near = lax.ppermute(near, "sub", cores)
    coarse_width = blocks * parents + pad(blocks * LANES // OCTANTS, LANES)
    front = ((blocks * LANES // OCTANTS // parents, 8, 2 * LANES), i32)
    right, scale, leading = run(
        functools.partial(restrict_kernel, blocks, parents),
        [((modes, coarse_width), f32), ((1, coarse_width), f32), front],
        r, near, gather, coarse_cond, down3,
        flops=10**8,
    )
    p, rim_out = run(
        functools.partial(coarse_kernel, blocks, parents, rims),
        [field, sends[2]],
        right, scale, leading, r, cross, gather, parent, octant, coarse_stiffness, down3, up3, c3, t3, rim, rim_face,
        scratch=[
            pltpu.VMEM((modes, coarse_width), f32),
            pltpu.VMEM((1, coarse_width), f32),
            pltpu.VMEM(*front),
            pltpu.VMEM((modes, rim_width), f32),
        ],
    )
    traces, sub_out = run(functools.partial(spread_kernel, blocks, width), sends[:2], p, t3, subs, rim_out)
    r, p, traces, sub_out, rim_out, x = apply("first", (0.0, 1.0 / CENTER), r, p, traces, sub_out, rim_out, x)
    for step in range(KF - 1):
        r, p, traces, sub_out, rim_out, x = apply("step", pairs[step], r, p, traces, sub_out, rim_out, x)
    residual, x = apply("last", None, r, p, traces, sub_out, rim_out, x)
    return x, residual


def solution(mesh):
    in_specs = (
        P(None, ("blk", "sub")),
        P(("blk", "sub")),
        P(("blk", "sub")),
        P(),
        P(),
        P(None, ("blk", "sub")),
        P(("blk", "sub"), None),
        P(("blk", "sub"), None),
        P(("blk", "sub"), None),
        P(("blk", "sub")),
        P(),
        P(),
    )
    out_specs = (P(None, ("blk", "sub")), P(None, ("blk", "sub")))
    return jax.shard_map(local, mesh=mesh, in_specs=in_specs, out_specs=out_specs, check_vma=False)
```

```python
import functools

import jax
import jax.numpy as jnp
from jax import lax
from jax.experimental import pallas as pl
from jax.experimental.pallas import tpu as pltpu
from jax.sharding import PartitionSpec as P

HEAD = 8
KF = 3
KC = 4
FACES = 6
OCTANTS = 8
LANES = 128
CORES = 2

PENALTY = 0.3
COUPLING = 0.5
LOW_EIG = 0.4
HIGH_EIG = 2.5
CENTER = 0.5 * (HIGH_EIG + LOW_EIG)
HALF = 0.5 * (HIGH_EIG - LOW_EIG)


def steps(sweeps):
    sigma = CENTER / HALF
    rho, pairs = 1.0 / sigma, []
    for _ in range(sweeps):
        rho_next = 1.0 / (2.0 * sigma - rho)
        pairs.append((rho_next * rho, 2.0 * rho_next / HALF))
        rho = rho_next
    return pairs


def halves(x):
    high = x.astype(jnp.bfloat16)
    return high, (x - high.astype(jnp.float32)).astype(jnp.bfloat16)


def product(left, x):
    high, low = halves(x)
    right = jnp.concatenate([high, low, high], axis=0)
    return jnp.dot(left, right, preferred_element_type=jnp.float32)


def store_left(out, rows, x, base=0):
    high, low = halves(x)
    width = x.shape[1]
    for place, piece in enumerate((high, high, low)):
        out[rows, base + place * width : base + (place + 1) * width] = piece


def take(tile, lane):
    index = jnp.broadcast_to(lane, tile.shape)
    return jnp.take_along_axis(tile, index, axis=1, mode="promise_in_bounds")


def pick(tiles, at, lane):
    out = jnp.zeros(tiles[0].shape, tiles[0].dtype)
    for number, tile in enumerate(tiles):
        out = jnp.where(at == number, take(tile, lane), out)
    return out


def lanes(rows=1):
    return lax.broadcasted_iota(jnp.int32, (rows, LANES), 1)


def cols(j, width, base=None):
    size, start = (width, j * width) if base is None else (LANES, j * width + base)
    return pl.ds(start if isinstance(j, int) else pl.multiple_of(start, LANES), size)


def over(blocks, body):
    if blocks <= 4:
        for j in range(blocks):
            body(j)
    else:
        lax.fori_loop(0, blocks, lambda j, carry: (body(j), carry)[1], 0)


def over_groups(blocks, body):
    size = min(blocks, 4)
    over(blocks // size, lambda g: body([g * size + i for i in range(size)], g))


def own_place():
    me = lax.axis_index("sub")
    return jnp.right_shift(me, 1), jnp.bitwise_and(me, 1)


def trace_tiles(traces):
    points = traces.shape[0] // FACES
    return [
        traces[f * points : (f + 1) * points, h : h + LANES]
        for f in range(FACES)
        for h in range(0, traces.shape[1], LANES)
    ]


def faces(tile_of, js, count):
    return jnp.concatenate(
        [
            jnp.concatenate([tile_of(j, f, h) for j in js for h in range(0, count, LANES)], axis=1)
            for f in range(FACES)
        ],
        axis=0,
    )


def of_block(x, i, count):
    return x[:, i * count : (i + 1) * count]


def send_sub(j, tiles, sub_ref, sub_out, width):
    for h in range(0, width, LANES):
        columns = sub_ref[:, cols(j, width, h)]
        sub_out[:, cols(j, width, h)] = pick(
            tiles, jnp.right_shift(columns, 7), jnp.bitwise_and(columns, LANES - 1)
        )


def send_rim(j, tiles, rim_ref, rim_out, rims):
    group = LANES // rims
    tile = cols(j // group, LANES)
    columns = rim_ref[:, tile]
    rim = pick(tiles, jnp.right_shift(columns, 7), jnp.bitwise_and(columns, LANES - 1))
    mine = lanes() // rims == j % group
    rim_out[:, tile] = jnp.where(mine, rim, rim_out[:, tile])


def prep_kernel(map_ref, stiff_ref, t_out, tt_out, k_out):
    modes, rows = map_ref.shape
    transposed = map_ref[...]
    store_left(tt_out, slice(0, modes), transposed)
    store_left(t_out, slice(0, rows), transposed.T)
    for k in range(2):
        store_left(k_out, slice(k * modes, (k + 1) * modes), stiff_ref[k])


def prep_coarse_kernel(restriction_ref, stiff_ref, down_out, up_out, c_out):
    modes = stiff_ref.shape[0]
    store_left(c_out, slice(0, modes), stiff_ref[...])
    pairs = down_out.shape[0] // modes
    for o in range(OCTANTS):
        rows = slice(o % pairs * modes, (o % pairs + 1) * modes)
        store_left(down_out, rows, restriction_ref[o], o // pairs * 3 * modes)
        store_left(up_out, slice(0, modes), restriction_ref[o].T, o * 3 * modes)


def pack_kernel(
    b_ref, cond_ref, mat_ref, face_ref, sub_ref, rim_ref, size_ref, coarse_ref, out,
    b_in, cond_in, mat_in, face_in, sub_in, rim_in, size_in, coarse_in, done,
):
    sources = (b_ref, cond_ref, mat_ref, face_ref, sub_ref, rim_ref, size_ref, coarse_ref)
    places = (b_in, cond_in, mat_in, face_in, sub_in, rim_in, size_in, coarse_in)
    copies = [
        pltpu.make_async_copy(source, place, done.at[at])
        for at, (source, place) in enumerate(zip(sources, places))
    ]
    for copy in copies:
        copy.start()
    modes, count = b_in.shape
    out[modes:, :] = jnp.zeros((out.shape[0] - modes, count), jnp.float32)
    for copy in copies:
        copy.wait()
    out[:modes, :] = b_in[...]
    out[modes : modes + 1, :] = cond_in[...]
    out[modes + 1 : modes + 2, :] = mat_in[...].astype(jnp.float32)
    out[modes + 2 : modes + 8, :] = face_in[...].astype(jnp.float32)
    out[modes + 8 : modes + 9, : rim_in.shape[1]] = rim_in[...].astype(jnp.float32)
    out[modes + 9 : modes + 10, : size_in.shape[1]] = size_in[...].astype(jnp.float32)
    out[modes + 10 : modes + 11, : coarse_in.shape[1]] = coarse_in[...]
    width = sub_in.shape[1]
    for at, h in enumerate(range(0, width, count)):
        piece = sub_in[:, h : min(h + count, width)].astype(jnp.float32)
        out[modes + 11 + at : modes + 12 + at, : piece.shape[1]] = piece


def start_kernel(blocks, width, rims, *refs):
    gathered, refs = refs[:blocks], refs[blocks:]
    stiff_ref, map_ref, t_ref, _ = refs[:4]
    b_out, ig_out, meta_out, lane_out, at_out, far_out, edge_out, sub_out, rim_out, size_out, coarse_out = refs[4:15]
    face_out, p_out, rims_out, held, edge = refs[15:]
    modes, count = map_ref.shape[0], gathered[0].shape[1]
    chip, core = own_place()
    for k, ref in enumerate(gathered):
        held[jnp.bitwise_xor(chip, k)] = ref[...]
    eye = lax.broadcasted_iota(jnp.int32, (modes, modes), 0) == lax.broadcasted_iota(
        jnp.int32, (modes, modes), 1
    )
    diagonals = [
        jnp.sum(jnp.where(eye, stiff_ref[k], 0.0), axis=1, keepdims=True) for k in range(2)
    ]
    squares = PENALTY * jnp.sum(map_ref[...] * map_ref[...], axis=1, keepdims=True)
    own_tiles = FACES * count // LANES
    sub_tiles = width // LANES
    rim_out[...] = jnp.zeros(rim_out.shape, jnp.int32)
    group = LANES // rims

    def body(j):
        b = held[j, :modes, :]
        cond = held[j, modes : modes + 1, :]
        mat = held[j, modes + 1 : modes + 2, :]
        b_out[:, cols(j, count)] = b
        meta_out[0:1, cols(j, count)] = cond
        meta_out[1:2, cols(j, count)] = mat
        column = held[j, modes + 2 : modes + 8, :].astype(jnp.int32)
        lane = jnp.bitwise_and(column, LANES - 1)
        at = jnp.right_shift(column, 7)
        lane_out[0:FACES, cols(j, count)] = lane
        at_out[0:FACES, cols(j, count)] = at
        rim = jnp.logical_and(at == own_tiles + sub_tiles, lane < rims)
        sub = jnp.logical_and(at >= own_tiles, at < own_tiles + sub_tiles)
        far_out[0:FACES, cols(j, count)] = jnp.where(sub, column - own_tiles * LANES, -1)
        edge_out[0:FACES, cols(j, count)] = jnp.where(
            rim, jnp.bitwise_xor(lane, rims // 2) + (j % group) * rims, -1
        )
        for h in range(0, width, LANES):
            row = modes + 11 + h // count
            piece = held[j, row : row + 1, h % count : h % count + LANES]
            sub_out[:, cols(j, width, h)] = piece.astype(jnp.int32)
        row = jnp.broadcast_to(held[j, modes + 8 : modes + 9, :LANES], (8, LANES))
        row = pltpu.roll(row, (j % group) * rims, 1)[0:1].astype(jnp.int32)
        tile = cols(j // group, LANES)
        rim_out[:, tile] = jnp.where(lanes() // rims == j % group, row, rim_out[:, tile])
        size_out[pl.ds(j, 1), :] = held[j, modes + 9 : modes + 10, :LANES].astype(jnp.int32)
        coarse_out[pl.ds(j, 1), :] = held[j, modes + 10 : modes + 11, :LANES]
        inverse = 1.0 / (cond * jnp.where(mat == 1.0, diagonals[1], diagonals[0]) + squares)
        ig_out[:, cols(j, count)] = inverse
        p_out[:, cols(j, count)] = b * inverse * (1.0 / CENTER)

    over(blocks, body)
    spot = lax.broadcasted_iota(jnp.int32, rim_out.shape, 1)
    face_out[...] = jnp.where(spot < blocks * rims, lax.div(rim_out[...], jnp.int32(count)), -1)
    edge[...] = jnp.zeros(edge.shape, jnp.float32)
    over(blocks, lambda j: keep_edge(j, p_out[:, cols(j, count)], rim_out, edge, rims))
    rims_out[...] = rim_traces(t_ref, edge[...], face_out[...])


def sub_tiles_of(j, sends_refs, core, width, blocks):
    slots = width // (blocks * CORES)
    pairs = LANES // slots // CORES
    lane = lanes()
    mine = lax.axis_index("sub") % CORES
    source = (CORES * (j % pairs) + mine) * slots + lane % slots
    tiles = []
    for t in range(width // LANES):
        tile = None
        for i in range(pairs):
            for ref, sender in zip(sends_refs, (core, 1 - core)):
                there = take(ref[:, cols(j // pairs, LANES, (pairs * t + i) * width)], source)
                tile = there if tile is None else jnp.where(lane // slots == CORES * i + sender, there, tile)
        tiles.append(tile)
    return tiles


def rim_element(columns, count):
    return jnp.bitwise_and(jnp.right_shift(columns, 7), count // LANES - 1), jnp.bitwise_and(columns, LANES - 1)


def local_kernel(only_own, blocks, width, first, *refs):
    p_ref, tr_ref, meta_ref, lane_ref, at_ref, k_ref = refs[:6]
    refs = refs[6:]
    if not first:
        x_ref, refs = refs[0], refs[1:]
    jump_out, own_out, x_out = refs
    modes = p_ref.shape[0]
    chip, core = own_place()
    count = x_out.shape[1]

    def body(js, span, out):
        traces = tr_ref[:, span]
        at_rows, lane_rows = at_ref[:, span], lane_ref[:, span]
        tiles = [
            trace_tiles(of_block(traces, i, count)) for i in range(len(js))
        ]

        def tile(i, f, h):
            row, place = slice(f, f + 1), slice(i * count + h, i * count + h + LANES)
            return pick(tiles[i], at_rows[row, place], lane_rows[row, place])

        jump_out[:, out] = traces - faces(tile, range(len(js)), count)
        both = product(k_ref[...], p_ref[:, span])
        meta = meta_ref[:, span]
        own_out[:, out] = meta[0:1] * jnp.where(meta[1:2] == 1.0, both[modes:], both[:modes])

    if only_own:
        body([chip], cols(chip, count), slice(0, count))
    else:
        over_groups(blocks, lambda js, g: body(js, cols(g, len(js) * count), cols(g, len(js) * count)))
    p = p_ref[:, cols(chip, count)]
    x_out[...] = p if first else x_ref[...] + p


def ahead_kernel(kind, coefficients, blocks, width, rims, *refs):
    r_ref, jump_ref, own_ref, subs_ref, swapped_ref, far_ref, tt_ref = refs[:7]
    refs = list(refs[7:])
    chip, core = own_place()
    count = own_ref.shape[1] // (1 if kind == "last" else blocks)
    group = LANES // rims
    lane = lanes()
    p_ref = refs.pop(0) if kind == "step" else None
    if kind in ("step", "first"):
        ig_ref, rim_ref, r_out, p_out, edge_out = refs
        edge_out[...] = jnp.zeros(edge_out.shape, jnp.float32)
    else:
        r_out = refs[0]

    def body(js, span, here):
        tiles = [sub_tiles_of(j, (subs_ref, swapped_ref), core, width, blocks) for j in js]
        far = far_ref[:, span]

        def tile(i, f, h):
            column = far[f : f + 1, i * count + h : i * count + h + LANES]
            return pick(tiles[i], jnp.right_shift(column, 7), jnp.bitwise_and(column, LANES - 1))

        jump = product(tt_ref[...], jump_ref[:, here] - faces(tile, range(len(js)), count))
        residual = r_ref[:, span] - own_ref[:, here] - PENALTY * jump
        r_out[:, here] = residual
        if kind in ("frame", "last"):
            return
        p = coefficients[1] * (residual * ig_ref[:, here])
        if kind == "step":
            p = p + coefficients[0] * p_ref[:, here]
        p_out[:, here] = p
        for i, j in enumerate(js):
            keep_edge(j, of_block(p, i, count), rim_ref, edge_out, rims)

    if kind == "last":
        body([chip], cols(chip, count), slice(0, count))
    else:
        over_groups(blocks, lambda js, g: body(js, cols(g, len(js) * count), cols(g, len(js) * count)))


def rim_tile(one_ref, two_ref, spot, rims):
    segment, segments = lax.axis_index("blk"), lax.axis_size("blk")
    odd = segment % 2 == 1
    low = jnp.where(odd, one_ref[:, spot], two_ref[:, spot])
    high = jnp.where(odd, two_ref[:, spot], one_ref[:, spot])
    low = jnp.where(segment == 0, 0.0, low)
    high = jnp.where(segment == segments - 1, 0.0, high)
    return jnp.where(lanes() % rims < rims // 2, high, low)


def rim_seen(rim, edge, f, h):
    place = edge[f : f + 1, h : h + LANES]
    return jnp.where(place >= 0, take(rim, jnp.bitwise_and(place, LANES - 1)), 0.0)


def keep_edge(j, p, rim_ref, edge_out, rims):
    group = LANES // rims
    spot = cols(j // group, LANES)
    count = p.shape[1]
    at, there = rim_element(rim_ref[:, spot], count)
    edge = pick([p[:, h : h + LANES] for h in range(0, count, LANES)], at, there)
    edge_out[:, spot] = jnp.where(lanes() // rims == j % group, edge, edge_out[:, spot])


def rim_traces(t_ref, p, face):
    traces = product(t_ref[...], p)
    points = traces.shape[0] // FACES
    out = jnp.zeros((points, p.shape[1]), jnp.float32)
    for f in range(FACES):
        out = jnp.where(face == f, traces[f * points : (f + 1) * points], out)
    return out


def edge_kernel(rate, rims, one_ref, two_ref, edges_ref, igs_ref, p_ref, tt_ref, t_ref, face_ref, rims_out):
    for t in range(one_ref.shape[1] // LANES):
        spot = slice(t * LANES, (t + 1) * LANES)
        rim = rim_tile(one_ref, two_ref, spot, rims)
        edge = edges_ref[:, spot]
        added = product(tt_ref[...], faces(lambda _, f, h: rim_seen(rim, edge, f, h), [0], LANES))
        p = p_ref[:, spot] + (rate * PENALTY) * (igs_ref[:, spot] * added)
        rims_out[:, spot] = rim_traces(t_ref, p, face_ref[:, spot])


def cross_kernel(blocks, rims, r_ref, one_ref, two_ref, edge_ref, tt_ref, size_ref, cond_ref, cross_out):
    modes = r_ref.shape[0]
    count = r_ref.shape[1] // blocks
    group = LANES // rims
    chip, core = own_place()
    last = blocks - 1
    first_tile, last_tile = cols(0, count, 0), cols(last, count, count - LANES)
    rim = jnp.where(
        core == 0,
        rim_tile(one_ref, two_ref, cols(0, LANES), rims),
        rim_tile(one_ref, two_ref, cols(last // group, LANES), rims),
    )
    edge = jnp.where(core == 0, edge_ref[:, first_tile], edge_ref[:, last_tile])
    seen = faces(lambda _, f, h: rim_seen(rim, edge, f, h), [0], LANES)
    residual = jnp.where(core == 0, r_ref[:, first_tile], r_ref[:, last_tile])
    cross_out[modes:, :] = jnp.zeros((cross_out.shape[0] - modes, LANES), jnp.float32)
    cross_out[:modes, :] = residual + PENALTY * product(tt_ref[...], seen)
    cross_out[modes : modes + 1, :] = size_ref[last : last + 1, :].astype(jnp.float32)
    cross_out[modes + 1 : modes + 2, :] = cond_ref[last : last + 1, :]


def finish_kernel(kind, rate, blocks, width, rims, *refs):
    r_ref, one_ref, two_ref, edge_ref, tt_ref = refs[:5]
    refs = list(refs[5:])
    chip, core = own_place()
    group = LANES // rims
    lane = lanes()
    if kind in ("step", "first"):
        p_ref, ig_ref, t_ref, sub_ref, _, r_out, p_out, tr_out, subs_out = refs
    elif kind == "frame":
        size_ref, cond_ref, _, r_out, near_out = refs
        near_out[...] = jnp.zeros(near_out.shape, jnp.float32)
    else:
        r_out = refs[0]
    count = r_out.shape[1] // (1 if kind == "last" else blocks)
    modes = r_ref.shape[0]

    def body(js, span, here):
        rim = [rim_tile(one_ref, two_ref, cols(j // group, LANES), rims) for j in js]
        edge = edge_ref[:, span]

        def tile(i, f, h):
            return rim_seen(rim[i], edge, f, i * count + h)

        added = PENALTY * product(tt_ref[...], faces(tile, range(len(js)), count))
        residual = r_ref[:, here] + added
        r_out[:, here] = residual
        if kind == "frame":
            heads = LANES // HEAD
            for i, j in enumerate(js):
                spot = cols(j // heads, LANES)
                mine = of_block(residual, i, count)
                moved = pltpu.roll(mine[:, :LANES], (j % heads) * HEAD, 1)
                near_out[:modes, spot] = jnp.where(lane // HEAD == j % heads, moved, near_out[:modes, spot])
                tail = cols(j, LANES, near_out.shape[1] - blocks * LANES)
                near_out[:modes, tail] = mine[:, count - LANES :]
                near_out[modes : modes + 1, tail] = size_ref[pl.ds(j, 1), :].astype(jnp.float32)
                near_out[modes + 1 : modes + 2, tail] = cond_ref[pl.ds(j, 1), :]
        if kind in ("frame", "last"):
            return
        p = p_ref[:, here] + rate * (ig_ref[:, here] * added)
        p_out[:, here] = p
        traces = product(t_ref[...], p)
        tr_out[:, here] = traces
        for i, j in enumerate(js):
            send_sub(j, trace_tiles(of_block(traces, i, count)), sub_ref, subs_out, width)

    if kind == "last":
        body([chip], cols(chip, count), slice(0, count))
    else:
        over_groups(blocks, lambda js, g: body(js, cols(g, len(js) * count), cols(g, len(js) * count)))


def layout_kernel(blocks, parents, size_ref, gather_out, parent_out, octant_out):
    lane = lanes()
    pairs = LANES // parents
    half = jnp.right_shift(lane, parents.bit_length() - 1)
    count = parent_out.shape[1] // blocks

    def body(j):
        each, end, size, start = children(size_ref[pl.ds(j, 1), :], parents, jnp.bitwise_and(lanes(parents), parents - 1))
        for i in range(OCTANTS // pairs):
            octant = pairs * i + half
            place = jnp.bitwise_and(start + octant + HEAD, count - 1)
            gather_out[i : i + 1, cols(j, LANES)] = jnp.where(octant < size, place, -1)
        for h in range(0, count, LANES):
            position = jnp.bitwise_and(lanes(parents) + (h - HEAD), count - 1)
            parent, octant = owner(each, end, position)
            parent_out[:, cols(j, count, h)] = parent + parents * (j % pairs)
            octant_out[:, cols(j, count, h)] = octant

    over(blocks, body)


def rim_kernel(blocks, rims, rim_ref, edge_ref, ig_ref, edges_out, igs_out):
    group = LANES // rims
    edges_out[...] = jnp.full(edges_out.shape, -1, jnp.int32)
    igs_out[...] = jnp.zeros(igs_out.shape, jnp.float32)
    count = ig_ref.shape[1] // blocks

    def body(j):
        tile = cols(j // group, LANES)
        mine = lanes() // rims == j % group
        at, there = rim_element(rim_ref[:, tile], count)
        edges = pick([edge_ref[:, cols(j, count, h)] for h in range(0, count, LANES)], at, there)
        igs = pick([ig_ref[:, cols(j, count, h)] for h in range(0, count, LANES)], at, there)
        edges_out[:, tile] = jnp.where(mine, edges, edges_out[:, tile])
        igs_out[:, tile] = jnp.where(mine, igs, igs_out[:, tile])

    over(blocks, body)


def children(sizes, parents, wanted):
    row = lax.broadcasted_iota(jnp.int32, (parents, LANES), 0)
    lane = lanes(parents)
    sizes = jnp.broadcast_to(sizes, (parents, LANES))
    each = jnp.sum(jnp.where(row == lane, sizes, 0), axis=1, keepdims=True)
    end = jnp.sum(jnp.where(lane <= row, sizes, 0), axis=1, keepdims=True)
    size = jnp.sum(jnp.where(row == wanted, each, 0), axis=0, keepdims=True)
    start = jnp.sum(jnp.where(row < wanted, each, 0), axis=0, keepdims=True)
    return each, end, size, start


def owner(each, end, position):
    passed = end <= position
    parent = jnp.sum(passed.astype(jnp.int32), axis=0, keepdims=True)
    return parent, position[0:1] - jnp.sum(jnp.where(passed, each, 0), axis=0, keepdims=True)


def restrict(sources, at, lane_of, down_ref):
    parts = []
    for i in range(len(at[0])):
        picked = [pick(*one) for one in zip(sources, [row[i] for row in at], [row[i] for row in lane_of])]
        high, low = halves(jnp.concatenate(picked, axis=1))
        parts += [high, low, high]
    both = jnp.dot(down_ref[...], jnp.concatenate(parts, axis=0), preferred_element_type=jnp.float32)
    modes = sources[0][0].shape[0]
    pairs = both.shape[0] // modes
    width = LANES // pairs
    totals = []
    for b in range(len(sources)):
        mine = both[:, b * LANES : (b + 1) * LANES]
        total = mine[:modes]
        for k in range(1, pairs):
            total = total + pltpu.roll(mine[k * modes : (k + 1) * modes], LANES - k * width, 1)
        totals.append(jnp.where(lanes() < width, total, 0.0))
    return totals


def last_parents(tail, modes, parents, extra):
    wanted = parents - extra + jnp.bitwise_and(lanes(parents), extra - 1)
    each, end, size, start = children(tail[modes : modes + 1].astype(jnp.int32), parents, wanted)
    rows = jnp.broadcast_to(tail[modes + 1 : modes + 2], (8, LANES))
    conds = take(rows, wanted[0:1])[0:1]
    total = jnp.sum(each, axis=0, keepdims=True)
    position = total - HEAD + jnp.bitwise_and(lanes(parents), HEAD - 1)
    parent, octant = owner(each, end, position)
    return size, start, conds, parent - (parents - extra), octant


def restrict_kernel(
    blocks, parents, r_ref, near_ref, gather_ref, cond_ref, down_ref, right_out, scale_out, front_out
):
    modes = r_ref.shape[0]
    count = r_ref.shape[1] // blocks
    lane = lanes()
    pairs = LANES // parents
    heads = LANES // HEAD
    extra = LANES // OCTANTS
    packed = parents // extra
    chip, core = own_place()
    own_tiles = blocks // pairs
    tails = near_ref.shape[1] - blocks * LANES
    right_out[...] = jnp.zeros(right_out.shape, jnp.float32)
    scale_out[...] = jnp.ones(scale_out.shape, jnp.float32)

    def body(js, g):
        sources, at, there = [], [], []
        for j in js:
            source = j + core
            tile = pl.ds(pl.multiple_of((jnp.minimum(source, blocks - 1) // heads) * LANES, LANES), LANES)
            arriving = pltpu.roll(near_ref[:modes, tile], (LANES - (source % heads) * HEAD) % LANES, 1)
            arriving = jnp.where(source < blocks, arriving, 0.0)
            own = [r_ref[:, cols(j, count, h)] for h in range(0, count, LANES)]
            sources.append([jnp.where(lane < HEAD, arriving, own[0])] + own[1:])
            places = [gather_ref[i : i + 1, cols(j, LANES)] for i in range(OCTANTS // pairs)]
            at.append([jnp.right_shift(place, 7) for place in places])
            there.append([jnp.bitwise_and(place, LANES - 1) for place in places])
            mine = jnp.broadcast_to(cond_ref[pl.ds(j, 1), :], (8, LANES))
            mine = pltpu.roll(mine, (j % pairs) * parents, 1)[0:1]
            spot = cols(j // pairs, LANES)
            scale_out[:, spot] = jnp.where(lane // parents == j % pairs, mine, scale_out[:, spot])
        before(js[0] // packed, sources, at, there)
        totals = restrict(sources, at, there, down_ref)
        for j, total in zip(js, totals):
            spot = cols(j // pairs, LANES)
            right_out[:, spot] = right_out[:, spot] + pltpu.roll(total, (j % pairs) * parents, 1)
        v = js[0] // packed
        spot = cols(v // pairs, LANES, own_tiles * LANES)
        right_out[:, spot] = right_out[:, spot] + pltpu.roll(totals[-1], (v % pairs) * parents, 1)

    def before(v, all_sources, all_at, all_there):
        group = jnp.bitwise_and(lane // extra, packed - 1)
        sources = []
        start = size = head_parent = head_octant = jnp.zeros((1, LANES), jnp.int32)
        conds = jnp.ones((1, LANES), jnp.float32)
        for i in range(packed):
            j = packed * v + i
            at = j - (1 - core)
            tail = near_ref[:, pl.ds(pl.multiple_of(tails + jnp.maximum(at, 0) * LANES, LANES), LANES)]
            sources.append(jnp.where(lane < HEAD, r_ref[:, cols(j, count, 0)], tail[:modes]))
            one_size, one_start, one_cond, parent, octant = last_parents(tail, modes, parents, extra)
            mine = group == i
            size = jnp.where(jnp.logical_and(mine, at >= 0), one_size, size)
            start = jnp.where(mine, one_start, start)
            conds = jnp.where(jnp.logical_and(mine, lane < parents), one_cond, conds)
            here = lane // HEAD == j % heads
            head_parent = jnp.where(here, parent + (v % pairs) * parents + i * extra, head_parent)
            head_octant = jnp.where(here, octant, head_octant)
        octants = [pairs * i + lane // parents for i in range(OCTANTS // pairs)]
        all_sources.append(sources)
        all_at.append([jnp.where(octant < size, group, -1) for octant in octants])
        all_there.append([jnp.bitwise_and(start + octant + HEAD, LANES - 1) for octant in octants])
        spot = cols(v // pairs, LANES, own_tiles * LANES)
        conds = pltpu.roll(jnp.broadcast_to(conds, (8, LANES)), (v % pairs) * parents, 1)[0:1]
        scale_out[:, spot] = jnp.where(lane // parents == v % pairs, conds, scale_out[:, spot])
        front_out[v, 0:1, :LANES] = head_parent
        front_out[v, 0:1, LANES:] = head_octant

    over_groups(blocks, body)


def coarse_kernel(
    blocks, parents, rims, right_ref, scale_ref, front_ref, r_ref, cross_ref, gather_ref, parent_ref, octant_ref,
    stiff_ref, down_ref, up_ref, c_ref, t_ref, rim_ref, face_ref, p_out, rims_out, right, scale, front, edge,
):
    modes = r_ref.shape[0]
    count = r_ref.shape[1] // blocks
    lane = lanes()
    pairs = LANES // parents
    heads = LANES // HEAD
    extra = LANES // OCTANTS
    packed = parents // extra
    chip, core = own_place()
    segment, segments = lax.axis_index("blk"), lax.axis_size("blk")
    own_tiles = blocks // pairs
    edge[...] = jnp.zeros(edge.shape, jnp.float32)
    right[...] = right_ref[...]
    scale[...] = scale_ref[...]
    front[...] = front_ref[...]

    cross = cross_ref[...]
    size, start, conds, parent, octant = last_parents(cross, modes, parents, extra)
    above = jnp.where(jnp.logical_and(lane < HEAD, segment < segments - 1), cross[:modes], 0.0)
    below = jnp.where(lane < HEAD, r_ref[:, :LANES], cross[:modes])
    below = jnp.where(segment == 0, 0.0, below)
    at, there = [], []
    for i in range(OCTANTS // pairs):
        place = gather_ref[i : i + 1, cols(blocks - 1, LANES)]
        one = pairs * i + lane // parents
        inside = jnp.logical_and(place >= 0, place < HEAD)
        mine = jnp.logical_and(jnp.bitwise_and(lane, parents - 1) < extra, one < size)
        at.append(jnp.where(core == 1, jnp.where(inside, 0, -1), jnp.where(mine, 0, -1)))
        there.append(jnp.bitwise_and(jnp.where(core == 1, place, start + one + HEAD), LANES - 1))
    (added,) = restrict([[jnp.where(core == 1, above, below)]], [at], [there], down_ref)
    spot = cols((blocks - 1) // pairs, LANES)
    moved = pltpu.roll(added, ((blocks - 1) % pairs) * parents, 1)
    right[:, spot] = right[:, spot] + jnp.where(core == 1, moved, 0.0)
    spot = cols(0, LANES, own_tiles * LANES)
    right[:, spot] = right[:, spot] + jnp.where(core == 0, added, 0.0)
    scale[:, spot] = jnp.where(jnp.logical_and(core == 0, lane < extra), conds, scale[:, spot])
    first = jnp.logical_and(core == 0, lane < HEAD)
    front[0, 0:1, :LANES] = jnp.where(first, parent, front[0, 0:1, :LANES])
    front[0, 0:1, LANES:] = jnp.where(first, octant, front[0, 0:1, LANES:])

    eye = lax.broadcasted_iota(jnp.int32, (modes, modes), 0) == lax.broadcasted_iota(
        jnp.int32, (modes, modes), 1
    )
    diagonal = jnp.sum(jnp.where(eye, stiff_ref[...], 0.0), axis=1, keepdims=True)
    tiles = right.shape[1] // LANES
    inverse = 1.0 / (scale[...] * diagonal + 2.0 * COUPLING)
    residual = right[...]
    p = residual * inverse * (1.0 / CENTER)
    field = p
    for ahead, correct in steps(KC - 1):
        pieces = []
        for t in range(tiles):
            here = p[:, t * LANES : (t + 1) * LANES]
            last = (parents if t < own_tiles else extra) - 1
            left = jnp.where(jnp.bitwise_and(lane, last) == 0, 0.0, pltpu.roll(here, 1, 1))
            after = jnp.where(jnp.bitwise_and(lane, last) == last, 0.0, pltpu.roll(here, LANES - 1, 1))
            pieces.append(left + after)
        sides = jnp.concatenate(pieces, axis=1)
        residual = residual - (scale[...] * product(c_ref[...], p) + COUPLING * (2.0 * p - sides))
        p = ahead * p + correct * (residual * inverse)
        field = field + p
    right[...] = field

    def prolong(js, g):
        span = cols(g, len(js) * count)
        v = js[0] // packed
        leading = take(right[:, cols(own_tiles + v // pairs, LANES)], front[v, 0:1, :LANES])
        leading_octant = jnp.broadcast_to(front[v, 0:1, LANES:], (8, LANES))
        spread, octants = [], []
        for j in js:
            parent = right[:, cols(j // pairs, LANES)]
            back = (LANES - (j % heads) * HEAD) % LANES
            for h in range(0, count, LANES):
                spot = cols(j, count, h)
                one, octant = take(parent, parent_ref[:, spot]), octant_ref[:, spot]
                if h == 0:
                    one = jnp.where(lane < HEAD, pltpu.roll(leading, back, 1), one)
                    octant = jnp.where(lane < HEAD, pltpu.roll(leading_octant, back, 1)[0:1], octant)
                spread.append(one)
                octants.append(octant)
        high, low = halves(jnp.concatenate(spread, axis=1))
        octant = jnp.concatenate(octants, axis=1)
        parts = []
        for o in range(OCTANTS):
            mine = (octant == o).astype(jnp.float32).astype(jnp.bfloat16)
            parts += [high * mine, low * mine, high * mine]
        p = jnp.dot(up_ref[...], jnp.concatenate(parts, axis=0), preferred_element_type=jnp.float32)
        p_out[:, span] = p
        for i, j in enumerate(js):
            keep_edge(j, of_block(p, i, count), rim_ref, edge, rims)

    over_groups(blocks, prolong)
    for t in range(edge.shape[1] // LANES):
        spot = slice(t * LANES, (t + 1) * LANES)
        rims_out[:, spot] = rim_traces(t_ref, edge[:, spot], face_ref[:, spot])


def spread_kernel(blocks, width, p_ref, t_ref, sub_ref, _, tr_out, subs_out):
    count = p_ref.shape[1] // blocks

    def body(js, g):
        span = cols(g, len(js) * count)
        traces = product(t_ref[...], p_ref[:, span])
        tr_out[:, span] = traces
        for i, j in enumerate(js):
            send_sub(j, trace_tiles(of_block(traces, i, count)), sub_ref, subs_out, width)

    over_groups(blocks, body)


def call(limit, kernel, outs, *args, scratch=(), hbm=False, flops=3 * 10**9):
    limit = (60 << 20) if hbm else limit
    return pl.pallas_call(
        kernel,
        out_shape=[jax.ShapeDtypeStruct(shape, kind) for shape, kind in outs],
        in_specs=[pl.BlockSpec(memory_space=pltpu.HBM if hbm else pltpu.VMEM)] * len(args),
        out_specs=[pl.BlockSpec(memory_space=pltpu.VMEM)] * len(outs),
        scratch_shapes=list(scratch),
        compiler_params=pltpu.CompilerParams(vmem_limit_bytes=limit),
        cost_estimate=pl.CostEstimate(flops=flops, bytes_accessed=1, transcendentals=0),
    )(*args)


def local(
    right_side,
    conductivity,
    material,
    stiffness,
    trace_map,
    face_neighbour,
    sub_sends,
    blk_sends,
    group_sizes,
    coarse_conductivity,
    coarse_stiffness,
    restriction,
):
    f32, i32, bf16 = jnp.float32, jnp.int32, jnp.bfloat16
    modes, count = right_side.shape
    rows = trace_map.shape[0]
    points = rows // FACES
    peers, segments = lax.axis_size("sub"), lax.axis_size("blk")
    blocks = peers // CORES
    parents = group_sizes.shape[1]
    width, rims = sub_sends.shape[1], blk_sends.shape[1]
    total = blocks * count
    limit = (4 << 20) if blocks <= 4 else (40 << 20)
    run = functools.partial(call, limit)

    def pad(size, to):
        return -(-size // to) * to

    rim_width = pad(blocks * rims, LANES)
    near_width = pad(blocks * HEAD, LANES) + blocks * LANES
    field = ((modes, total), f32)
    block = ((modes, count), f32)
    sends = [((rows, total), f32), ((points, blocks * width), f32), ((points, rim_width), f32)]

    def everywhere(partner):
        pairs = []
        for b in range(segments):
            for s in range(peers):
                other_b, other_s = partner(b, s)
                pairs.append((b * peers + s, other_b * peers + other_s))
        return pairs

    def above_or_below(first):
        def partner(b, s):
            other = b + 1 if b % 2 == first else b - 1
            return (other, s) if 0 <= other < segments else (b, s ^ 1)

        return everywhere(partner)

    def crossing(b, s):
        other = b - 1 if s % 2 == 0 else b + 1
        return (other, s ^ 1) if 0 <= other < segments else (b, s ^ 2)

    both = ("blk", "sub")
    cores = [(s, s ^ 1) for s in range(peers)]
    ones, twos, crossings = above_or_below(0), above_or_below(1), everywhere(crossing)

    def over_segments(rim):
        return lax.ppermute(rim, both, ones), lax.ppermute(rim, both, twos)

    map_t = trace_map.T
    t3, tt3, k3 = run(
        prep_kernel,
        [((rows, 3 * modes), bf16), ((modes, 3 * rows), bf16), ((2 * modes, 3 * modes), bf16)],
        map_t, stiffness,
    )
    down3, up3, c3 = run(
        prep_coarse_kernel,
        [((LANES // parents * modes, OCTANTS * parents // LANES * 3 * modes), bf16), ((modes, OCTANTS * 3 * modes), bf16), ((modes, 3 * modes), bf16)],
        restriction, coarse_stiffness,
    )

    height = pad(modes + 11 + pad(width, count) // count, 8)
    inputs = [
        right_side, conductivity.reshape(1, count), material.reshape(1, count), face_neighbour, sub_sends, blk_sends,
        group_sizes, coarse_conductivity.reshape(1, -1),
    ]
    (packed,) = run(
        pack_kernel,
        [((height, count), f32)],
        *inputs,
        scratch=[pltpu.VMEM(x.shape, x.dtype) for x in inputs] + [pltpu.SemaphoreType.DMA((len(inputs),))],
        hbm=True,
    )
    gathered = [packed] + [
        lax.ppermute(packed, "sub", [(s, s ^ (CORES * k)) for s in range(peers)]) for k in range(1, blocks)
    ]
    b, inverse, meta, lane, at, far, edge, subs, rim, sizes, coarse_cond, rim_face, p, rim_out = run(
        functools.partial(start_kernel, blocks, width, rims),
        [
            field, field, ((8, total), f32), *[((8, total), i32)] * 4,
            ((1, blocks * width), i32), ((1, rim_width), i32), ((blocks, LANES), i32), ((blocks, LANES), f32),
            ((1, rim_width), i32), field, sends[2],
        ],
        *gathered, stiffness, map_t, t3, c3,
        scratch=[pltpu.VMEM((blocks, height, count), f32), pltpu.VMEM((modes, rim_width), f32)],
    )
    traces, sub_out = run(functools.partial(spread_kernel, blocks, width), sends[:2], p, t3, subs, rim_out)

    edges, igs = run(
        functools.partial(rim_kernel, blocks, rims), [((8, rim_width), i32), ((modes, rim_width), f32)], rim, edge, inverse
    )
    gather, parent, octant = run(
        functools.partial(layout_kernel, blocks, parents),
        [((OCTANTS * parents // LANES, blocks * LANES), i32), ((1, total), i32), ((1, total), i32)],
        sizes,
        flops=3 * 10**10,
    )
    def apply(kind, coefficients, r, p, traces, sub_out, rim_out, x):
        one, two = over_segments(rim_out)
        swapped = lax.ppermute(sub_out, "sub", cores)
        only_own = kind == "last"
        size = count if only_own else total
        part, col = ((modes, size), f32), ((rows, size), f32)
        jump, own, x = run(
            functools.partial(local_kernel, only_own, blocks, width, x is None),
            [col, part, block],
            p, traces, meta, lane, at, k3, *([] if x is None else [x]),
        )
        goes_on = kind in ("step", "first")
        kernel = functools.partial(ahead_kernel, kind, coefficients, blocks, width, rims)
        args = [r, jump, own, sub_out, swapped, far, tt3] + ([p] if kind == "step" else [])
        if not goes_on:
            (r,) = run(kernel, [part], *args)
            finish = functools.partial(finish_kernel, kind, None, blocks, width, rims)
            args = [r, one, two, edge, tt3]
            if only_own:
                return *run(finish, [block], *args), x
            args += [sizes, coarse_cond]
            (cross,) = run(functools.partial(cross_kernel, blocks, rims), [((modes + 8, LANES), f32)], *args)
            return *run(finish, [field, ((modes + 8, near_width), f32)], *args, cross), cross, x
        r, p, p_edge = run(kernel, [field, field, ((modes, rim_width), f32)], *args, inverse, rim)
        rate = coefficients[1]
        (rim_out,) = run(
            functools.partial(edge_kernel, rate, rims), [((points, rim_width), f32)],
            one, two, edges, igs, p_edge, tt3, t3, rim_face,
        )
        r, p, traces, sub_out = run(
            functools.partial(finish_kernel, kind, rate, blocks, width, rims),
            [field, field, ((rows, total), f32), ((points, blocks * width), f32)],
            r, one, two, edge, tt3, p, inverse, t3, subs, rim_out,
        )
        return r, p, traces, sub_out, rim_out, x

    x = None
    r = b
    pairs = steps(KF)
    for step in range(KF - 1):
        r, p, traces, sub_out, rim_out, x = apply("step", pairs[step], r, p, traces, sub_out, rim_out, x)
    r, near, cross, x = apply("frame", None, r, p, traces, sub_out, rim_out, x)

    cross = lax.ppermute(cross, both, crossings)
    near = lax.ppermute(near, "sub", cores)
    coarse_width = blocks * parents + pad(blocks * LANES // OCTANTS, LANES)
    front = ((blocks * LANES // OCTANTS // parents, 8, 2 * LANES), i32)
    right, scale, leading = run(
        functools.partial(restrict_kernel, blocks, parents),
        [((modes, coarse_width), f32), ((1, coarse_width), f32), front],
        r, near, gather, coarse_cond, down3,
        flops=10**8,
    )
    p, rim_out = run(
        functools.partial(coarse_kernel, blocks, parents, rims),
        [field, sends[2]],
        right, scale, leading, r, cross, gather, parent, octant, coarse_stiffness, down3, up3, c3, t3, rim, rim_face,
        scratch=[
            pltpu.VMEM((modes, coarse_width), f32),
            pltpu.VMEM((1, coarse_width), f32),
            pltpu.VMEM(*front),
            pltpu.VMEM((modes, rim_width), f32),
        ],
    )
    traces, sub_out = run(functools.partial(spread_kernel, blocks, width), sends[:2], p, t3, subs, rim_out)
    r, p, traces, sub_out, rim_out, x = apply("first", (0.0, 1.0 / CENTER), r, p, traces, sub_out, rim_out, x)
    for step in range(KF - 1):
        r, p, traces, sub_out, rim_out, x = apply("step", pairs[step], r, p, traces, sub_out, rim_out, x)
    residual, x = apply("last", None, r, p, traces, sub_out, rim_out, x)
    return x, residual


def solution(mesh):
    in_specs = (
        P(None, ("blk", "sub")),
        P(("blk", "sub")),
        P(("blk", "sub")),
        P(),
        P(),
        P(None, ("blk", "sub")),
        P(("blk", "sub"), None),
        P(("blk", "sub"), None),
        P(("blk", "sub"), None),
        P(("blk", "sub")),
        P(),
        P(),
    )
    out_specs = (P(None, ("blk", "sub")), P(None, ("blk", "sub")))
    return jax.shard_map(local, mesh=mesh, in_specs=in_specs, out_specs=out_specs, check_vma=False)
```

```python
import functools

import jax
import jax.numpy as jnp
from jax import lax
from jax.experimental import pallas as pl
from jax.experimental.pallas import tpu as pltpu
from jax.sharding import PartitionSpec as P

HEAD = 8
KF = 3
KC = 4
FACES = 6
OCTANTS = 8
LANES = 128
CORES = 2

PENALTY = 0.3
COUPLING = 0.5
LOW_EIG = 0.4
HIGH_EIG = 2.5
CENTER = 0.5 * (HIGH_EIG + LOW_EIG)
HALF = 0.5 * (HIGH_EIG - LOW_EIG)


def steps(sweeps):
    sigma = CENTER / HALF
    rho, pairs = 1.0 / sigma, []
    for _ in range(sweeps):
        rho_next = 1.0 / (2.0 * sigma - rho)
        pairs.append((rho_next * rho, 2.0 * rho_next / HALF))
        rho = rho_next
    return pairs


def halves(x):
    high = x.astype(jnp.bfloat16)
    return high, (x - high.astype(jnp.float32)).astype(jnp.bfloat16)


def product(left, x):
    high, low = halves(x)
    right = jnp.concatenate([high, low, high], axis=0)
    return jnp.dot(left, right, preferred_element_type=jnp.float32)


def store_left(out, rows, x, base=0):
    high, low = halves(x)
    width = x.shape[1]
    for place, piece in enumerate((high, high, low)):
        out[rows, base + place * width : base + (place + 1) * width] = piece


def take(tile, lane):
    index = jnp.broadcast_to(lane, tile.shape)
    return jnp.take_along_axis(tile, index, axis=1, mode="promise_in_bounds")


def pick(tiles, at, lane):
    out = jnp.zeros(tiles[0].shape, tiles[0].dtype)
    for number, tile in enumerate(tiles):
        out = jnp.where(at == number, take(tile, lane), out)
    return out


def lanes(rows=1):
    return lax.broadcasted_iota(jnp.int32, (rows, LANES), 1)


def cols(j, width, base=None):
    size, start = (width, j * width) if base is None else (LANES, j * width + base)
    return pl.ds(start if isinstance(j, int) else pl.multiple_of(start, LANES), size)


def over(blocks, body):
    if blocks <= 4:
        for j in range(blocks):
            body(j)
    else:
        lax.fori_loop(0, blocks, lambda j, carry: (body(j), carry)[1], 0)


def over_groups(blocks, body):
    size = min(blocks, 4)
    over(blocks // size, lambda g: body([g * size + i for i in range(size)], g))


def own_place():
    me = lax.axis_index("sub")
    return jnp.right_shift(me, 1), jnp.bitwise_and(me, 1)


def trace_tiles(traces):
    points = traces.shape[0] // FACES
    return [
        traces[f * points : (f + 1) * points, h : h + LANES]
        for f in range(FACES)
        for h in range(0, traces.shape[1], LANES)
    ]


def faces(tile_of, js, count):
    return jnp.concatenate(
        [
            jnp.concatenate([tile_of(j, f, h) for j in js for h in range(0, count, LANES)], axis=1)
            for f in range(FACES)
        ],
        axis=0,
    )


def of_block(x, i, count):
    return x[:, i * count : (i + 1) * count]


def send_sub(j, tiles, sub_ref, sub_out, width):
    for h in range(0, width, LANES):
        columns = sub_ref[:, cols(j, width, h)]
        sub_out[:, cols(j, width, h)] = pick(
            tiles, jnp.right_shift(columns, 7), jnp.bitwise_and(columns, LANES - 1)
        )


def send_rim(j, tiles, rim_ref, rim_out, rims):
    group = LANES // rims
    tile = cols(j // group, LANES)
    columns = rim_ref[:, tile]
    rim = pick(tiles, jnp.right_shift(columns, 7), jnp.bitwise_and(columns, LANES - 1))
    mine = lanes() // rims == j % group
    rim_out[:, tile] = jnp.where(mine, rim, rim_out[:, tile])


def prep_kernel(map_ref, stiff_ref, t_out, tt_out, k_out):
    modes, rows = map_ref.shape
    transposed = map_ref[...]
    store_left(tt_out, slice(0, modes), transposed)
    store_left(t_out, slice(0, rows), transposed.T)
    for k in range(2):
        store_left(k_out, slice(k * modes, (k + 1) * modes), stiff_ref[k])


def prep_coarse_kernel(restriction_ref, stiff_ref, down_out, up_out, c_out):
    modes = stiff_ref.shape[0]
    store_left(c_out, slice(0, modes), stiff_ref[...])
    pairs = down_out.shape[0] // modes
    for o in range(OCTANTS):
        rows = slice(o % pairs * modes, (o % pairs + 1) * modes)
        store_left(down_out, rows, restriction_ref[o], o // pairs * 3 * modes)
        store_left(up_out, slice(0, modes), restriction_ref[o].T, o * 3 * modes)


def pack_kernel(
    b_ref, cond_ref, mat_ref, face_ref, sub_ref, rim_ref, size_ref, coarse_ref, out,
    b_in, cond_in, mat_in, face_in, sub_in, rim_in, size_in, coarse_in, done,
):
    sources = (b_ref, cond_ref, mat_ref, face_ref, sub_ref, rim_ref, size_ref, coarse_ref)
    places = (b_in, cond_in, mat_in, face_in, sub_in, rim_in, size_in, coarse_in)
    copies = [
        pltpu.make_async_copy(source, place, done.at[at])
        for at, (source, place) in enumerate(zip(sources, places))
    ]
    for copy in copies:
        copy.start()
    modes, count = b_in.shape
    out[modes:, :] = jnp.zeros((out.shape[0] - modes, count), jnp.float32)
    for copy in copies:
        copy.wait()
    out[:modes, :] = b_in[...]
    out[modes : modes + 1, :] = cond_in[...]
    out[modes + 1 : modes + 2, :] = mat_in[...].astype(jnp.float32)
    out[modes + 2 : modes + 8, :] = face_in[...].astype(jnp.float32)
    out[modes + 8 : modes + 9, : rim_in.shape[1]] = rim_in[...].astype(jnp.float32)
    out[modes + 9 : modes + 10, : size_in.shape[1]] = size_in[...].astype(jnp.float32)
    out[modes + 10 : modes + 11, : coarse_in.shape[1]] = coarse_in[...]
    width = sub_in.shape[1]
    for at, h in enumerate(range(0, width, count)):
        piece = sub_in[:, h : min(h + count, width)].astype(jnp.float32)
        out[modes + 11 + at : modes + 12 + at, : piece.shape[1]] = piece


def start_kernel(blocks, width, rims, *refs):
    gathered, refs = refs[:blocks], refs[blocks:]
    stiff_ref, map_ref, t_ref, _ = refs[:4]
    b_out, ig_out, meta_out, lane_out, at_out, far_out, edge_out, sub_out, rim_out, size_out, coarse_out = refs[4:15]
    face_out, p_out, rims_out, held, edge = refs[15:]
    modes, count = map_ref.shape[0], gathered[0].shape[1]
    chip, core = own_place()
    for k, ref in enumerate(gathered):
        held[jnp.bitwise_xor(chip, k)] = ref[...]
    eye = lax.broadcasted_iota(jnp.int32, (modes, modes), 0) == lax.broadcasted_iota(
        jnp.int32, (modes, modes), 1
    )
    diagonals = [
        jnp.sum(jnp.where(eye, stiff_ref[k], 0.0), axis=1, keepdims=True) for k in range(2)
    ]
    squares = PENALTY * jnp.sum(map_ref[...] * map_ref[...], axis=1, keepdims=True)
    own_tiles = FACES * count // LANES
    sub_tiles = width // LANES
    rim_out[...] = jnp.zeros(rim_out.shape, jnp.int32)
    group = LANES // rims

    def body(j):
        b = held[j, :modes, :]
        cond = held[j, modes : modes + 1, :]
        mat = held[j, modes + 1 : modes + 2, :]
        b_out[:, cols(j, count)] = b
        meta_out[0:1, cols(j, count)] = cond
        meta_out[1:2, cols(j, count)] = mat
        column = held[j, modes + 2 : modes + 8, :].astype(jnp.int32)
        lane = jnp.bitwise_and(column, LANES - 1)
        at = jnp.right_shift(column, 7)
        lane_out[0:FACES, cols(j, count)] = lane
        at_out[0:FACES, cols(j, count)] = at
        rim = jnp.logical_and(at == own_tiles + sub_tiles, lane < rims)
        sub = jnp.logical_and(at >= own_tiles, at < own_tiles + sub_tiles)
        far_out[0:FACES, cols(j, count)] = jnp.where(sub, column - own_tiles * LANES, -1)
        edge_out[0:FACES, cols(j, count)] = jnp.where(
            rim, jnp.bitwise_xor(lane, rims // 2) + (j % group) * rims, -1
        )
        for h in range(0, width, LANES):
            row = modes + 11 + h // count
            piece = held[j, row : row + 1, h % count : h % count + LANES]
            sub_out[:, cols(j, width, h)] = piece.astype(jnp.int32)
        row = jnp.broadcast_to(held[j, modes + 8 : modes + 9, :LANES], (8, LANES))
        row = pltpu.roll(row, (j % group) * rims, 1)[0:1].astype(jnp.int32)
        tile = cols(j // group, LANES)
        rim_out[:, tile] = jnp.where(lanes() // rims == j % group, row, rim_out[:, tile])
        size_out[pl.ds(j, 1), :] = held[j, modes + 9 : modes + 10, :LANES].astype(jnp.int32)
        coarse_out[pl.ds(j, 1), :] = held[j, modes + 10 : modes + 11, :LANES]
        inverse = 1.0 / (cond * jnp.where(mat == 1.0, diagonals[1], diagonals[0]) + squares)
        ig_out[:, cols(j, count)] = inverse
        p_out[:, cols(j, count)] = b * inverse * (1.0 / CENTER)

    over(blocks, body)
    spot = lax.broadcasted_iota(jnp.int32, rim_out.shape, 1)
    face_out[...] = jnp.where(spot < blocks * rims, lax.div(rim_out[...], jnp.int32(count)), -1)
    edge[...] = jnp.zeros(edge.shape, jnp.float32)
    over(blocks, lambda j: keep_edge(j, p_out[:, cols(j, count)], rim_out, edge, rims))
    rims_out[...] = rim_traces(t_ref, edge[...], face_out[...])


def sub_tiles_of(j, sends_refs, core, width, blocks):
    slots = width // (blocks * CORES)
    pairs = LANES // slots // CORES
    lane = lanes()
    mine = lax.axis_index("sub") % CORES
    source = (CORES * (j % pairs) + mine) * slots + lane % slots
    tiles = []
    for t in range(width // LANES):
        tile = None
        for i in range(pairs):
            for ref, sender in zip(sends_refs, (core, 1 - core)):
                there = take(ref[:, cols(j // pairs, LANES, (pairs * t + i) * width)], source)
                tile = there if tile is None else jnp.where(lane // slots == CORES * i + sender, there, tile)
        tiles.append(tile)
    return tiles


def rim_element(columns, count):
    return jnp.bitwise_and(jnp.right_shift(columns, 7), count // LANES - 1), jnp.bitwise_and(columns, LANES - 1)


def local_kernel(only_own, blocks, width, first, *refs):
    p_ref, tr_ref, meta_ref, lane_ref, at_ref, k_ref = refs[:6]
    refs = refs[6:]
    if not first:
        x_ref, refs = refs[0], refs[1:]
    jump_out, own_out, x_out = refs
    modes = p_ref.shape[0]
    chip, core = own_place()
    count = x_out.shape[1]

    def body(js, span, out):
        traces = tr_ref[:, span]
        at_rows, lane_rows = at_ref[:, span], lane_ref[:, span]
        tiles = [
            trace_tiles(of_block(traces, i, count)) for i in range(len(js))
        ]

        def tile(i, f, h):
            row, place = slice(f, f + 1), slice(i * count + h, i * count + h + LANES)
            return pick(tiles[i], at_rows[row, place], lane_rows[row, place])

        jump_out[:, out] = traces - faces(tile, range(len(js)), count)
        both = product(k_ref[...], p_ref[:, span])
        meta = meta_ref[:, span]
        own_out[:, out] = meta[0:1] * jnp.where(meta[1:2] == 1.0, both[modes:], both[:modes])

    if only_own:
        body([chip], cols(chip, count), slice(0, count))
    else:
        over_groups(blocks, lambda js, g: body(js, cols(g, len(js) * count), cols(g, len(js) * count)))
    p = p_ref[:, cols(chip, count)]
    x_out[...] = p if first else x_ref[...] + p


def ahead_kernel(kind, coefficients, blocks, width, rims, *refs):
    r_ref, jump_ref, own_ref, subs_ref, swapped_ref, far_ref, tt_ref = refs[:7]
    refs = list(refs[7:])
    chip, core = own_place()
    count = own_ref.shape[1] // (1 if kind == "last" else blocks)
    group = LANES // rims
    lane = lanes()
    p_ref = refs.pop(0) if kind == "step" else None
    if kind in ("step", "first"):
        ig_ref, rim_ref, r_out, p_out, edge_out = refs
        edge_out[...] = jnp.zeros(edge_out.shape, jnp.float32)
    else:
        r_out = refs[0]

    def body(js, span, here):
        tiles = [sub_tiles_of(j, (subs_ref, swapped_ref), core, width, blocks) for j in js]
        far = far_ref[:, span]

        def tile(i, f, h):
            column = far[f : f + 1, i * count + h : i * count + h + LANES]
            return pick(tiles[i], jnp.right_shift(column, 7), jnp.bitwise_and(column, LANES - 1))

        jump = product(tt_ref[...], jump_ref[:, here] - faces(tile, range(len(js)), count))
        residual = r_ref[:, span] - own_ref[:, here] - PENALTY * jump
        r_out[:, here] = residual
        if kind in ("frame", "last"):
            return
        p = coefficients[1] * (residual * ig_ref[:, here])
        if kind == "step":
            p = p + coefficients[0] * p_ref[:, here]
        p_out[:, here] = p
        for i, j in enumerate(js):
            keep_edge(j, of_block(p, i, count), rim_ref, edge_out, rims)

    if kind == "last":
        body([chip], cols(chip, count), slice(0, count))
    else:
        over_groups(blocks, lambda js, g: body(js, cols(g, len(js) * count), cols(g, len(js) * count)))


def rim_tile(one_ref, two_ref, spot, rims):
    segment, segments = lax.axis_index("blk"), lax.axis_size("blk")
    odd = segment % 2 == 1
    low = jnp.where(odd, one_ref[:, spot], two_ref[:, spot])
    high = jnp.where(odd, two_ref[:, spot], one_ref[:, spot])
    low = jnp.where(segment == 0, 0.0, low)
    high = jnp.where(segment == segments - 1, 0.0, high)
    return jnp.where(lanes() % rims < rims // 2, high, low)


def rim_seen(rim, edge, f, h):
    place = edge[f : f + 1, h : h + LANES]
    return jnp.where(place >= 0, take(rim, jnp.bitwise_and(place, LANES - 1)), 0.0)


def keep_edge(j, p, rim_ref, edge_out, rims):
    group = LANES // rims
    spot = cols(j // group, LANES)
    count = p.shape[1]
    at, there = rim_element(rim_ref[:, spot], count)
    edge = pick([p[:, h : h + LANES] for h in range(0, count, LANES)], at, there)
    edge_out[:, spot] = jnp.where(lanes() // rims == j % group, edge, edge_out[:, spot])


def rim_traces(t_ref, p, face):
    traces = product(t_ref[...], p)
    points = traces.shape[0] // FACES
    out = jnp.zeros((points, p.shape[1]), jnp.float32)
    for f in range(FACES):
        out = jnp.where(face == f, traces[f * points : (f + 1) * points], out)
    return out


def edge_kernel(rate, rims, one_ref, two_ref, edges_ref, igs_ref, p_ref, tt_ref, t_ref, face_ref, rims_out):
    for t in range(one_ref.shape[1] // LANES):
        spot = slice(t * LANES, (t + 1) * LANES)
        rim = rim_tile(one_ref, two_ref, spot, rims)
        edge = edges_ref[:, spot]
        added = product(tt_ref[...], faces(lambda _, f, h: rim_seen(rim, edge, f, h), [0], LANES))
        p = p_ref[:, spot] + (rate * PENALTY) * (igs_ref[:, spot] * added)
        rims_out[:, spot] = rim_traces(t_ref, p, face_ref[:, spot])


def cross_kernel(blocks, rims, r_ref, one_ref, two_ref, edge_ref, tt_ref, size_ref, cond_ref, cross_out):
    modes = r_ref.shape[0]
    count = r_ref.shape[1] // blocks
    group = LANES // rims
    chip, core = own_place()
    last = blocks - 1
    first_tile, last_tile = cols(0, count, 0), cols(last, count, count - LANES)
    rim = jnp.where(
        core == 0,
        rim_tile(one_ref, two_ref, cols(0, LANES), rims),
        rim_tile(one_ref, two_ref, cols(last // group, LANES), rims),
    )
    edge = jnp.where(core == 0, edge_ref[:, first_tile], edge_ref[:, last_tile])
    seen = faces(lambda _, f, h: rim_seen(rim, edge, f, h), [0], LANES)
    residual = jnp.where(core == 0, r_ref[:, first_tile], r_ref[:, last_tile])
    cross_out[modes:, :] = jnp.zeros((cross_out.shape[0] - modes, LANES), jnp.float32)
    cross_out[:modes, :] = residual + PENALTY * product(tt_ref[...], seen)
    cross_out[modes : modes + 1, :] = size_ref[last : last + 1, :].astype(jnp.float32)
    cross_out[modes + 1 : modes + 2, :] = cond_ref[last : last + 1, :]


def finish_kernel(kind, rate, blocks, width, rims, *refs):
    r_ref, one_ref, two_ref, edge_ref, tt_ref = refs[:5]
    refs = list(refs[5:])
    chip, core = own_place()
    group = LANES // rims
    lane = lanes()
    if kind in ("step", "first"):
        p_ref, ig_ref, t_ref, sub_ref, _, r_out, p_out, tr_out, subs_out = refs
    elif kind == "frame":
        size_ref, cond_ref, _, r_out, near_out = refs
        near_out[...] = jnp.zeros(near_out.shape, jnp.float32)
    else:
        r_out = refs[0]
    count = r_out.shape[1] // (1 if kind == "last" else blocks)
    modes = r_ref.shape[0]

    def body(js, span, here):
        rim = [rim_tile(one_ref, two_ref, cols(j // group, LANES), rims) for j in js]
        edge = edge_ref[:, span]

        def tile(i, f, h):
            return rim_seen(rim[i], edge, f, i * count + h)

        added = PENALTY * product(tt_ref[...], faces(tile, range(len(js)), count))
        residual = r_ref[:, here] + added
        r_out[:, here] = residual
        if kind == "frame":
            heads = LANES // HEAD
            for i, j in enumerate(js):
                spot = cols(j // heads, LANES)
                mine = of_block(residual, i, count)
                moved = pltpu.roll(mine[:, :LANES], (j % heads) * HEAD, 1)
                near_out[:modes, spot] = jnp.where(lane // HEAD == j % heads, moved, near_out[:modes, spot])
                tail = cols(j, LANES, near_out.shape[1] - blocks * LANES)
                near_out[:modes, tail] = mine[:, count - LANES :]
                near_out[modes : modes + 1, tail] = size_ref[pl.ds(j, 1), :].astype(jnp.float32)
                near_out[modes + 1 : modes + 2, tail] = cond_ref[pl.ds(j, 1), :]
        if kind in ("frame", "last"):
            return
        p = p_ref[:, here] + rate * (ig_ref[:, here] * added)
        p_out[:, here] = p
        traces = product(t_ref[...], p)
        tr_out[:, here] = traces
        for i, j in enumerate(js):
            send_sub(j, trace_tiles(of_block(traces, i, count)), sub_ref, subs_out, width)

    if kind == "last":
        body([chip], cols(chip, count), slice(0, count))
    else:
        over_groups(blocks, lambda js, g: body(js, cols(g, len(js) * count), cols(g, len(js) * count)))


def layout_kernel(blocks, parents, size_ref, gather_out, parent_out, octant_out):
    lane = lanes()
    pairs = LANES // parents
    half = jnp.right_shift(lane, parents.bit_length() - 1)
    count = parent_out.shape[1] // blocks

    def body(j):
        each, end, size, start = children(size_ref[pl.ds(j, 1), :], parents, jnp.bitwise_and(lanes(parents), parents - 1))
        for i in range(OCTANTS // pairs):
            octant = pairs * i + half
            place = jnp.bitwise_and(start + octant + HEAD, count - 1)
            gather_out[i : i + 1, cols(j, LANES)] = jnp.where(octant < size, place, -1)
        for h in range(0, count, LANES):
            position = jnp.bitwise_and(lanes(parents) + (h - HEAD), count - 1)
            parent, octant = owner(each, end, position)
            parent_out[:, cols(j, count, h)] = parent + parents * (j % pairs)
            octant_out[:, cols(j, count, h)] = octant

    over(blocks, body)


def rim_kernel(blocks, rims, rim_ref, edge_ref, ig_ref, edges_out, igs_out):
    group = LANES // rims
    edges_out[...] = jnp.full(edges_out.shape, -1, jnp.int32)
    igs_out[...] = jnp.zeros(igs_out.shape, jnp.float32)
    count = ig_ref.shape[1] // blocks

    def body(j):
        tile = cols(j // group, LANES)
        mine = lanes() // rims == j % group
        at, there = rim_element(rim_ref[:, tile], count)
        edges = pick([edge_ref[:, cols(j, count, h)] for h in range(0, count, LANES)], at, there)
        igs = pick([ig_ref[:, cols(j, count, h)] for h in range(0, count, LANES)], at, there)
        edges_out[:, tile] = jnp.where(mine, edges, edges_out[:, tile])
        igs_out[:, tile] = jnp.where(mine, igs, igs_out[:, tile])

    over(blocks, body)


def children(sizes, parents, wanted):
    row = lax.broadcasted_iota(jnp.int32, (parents, LANES), 0)
    lane = lanes(parents)
    sizes = jnp.broadcast_to(sizes, (parents, LANES))
    each = jnp.sum(jnp.where(row == lane, sizes, 0), axis=1, keepdims=True)
    end = jnp.sum(jnp.where(lane <= row, sizes, 0), axis=1, keepdims=True)
    size = jnp.sum(jnp.where(row == wanted, each, 0), axis=0, keepdims=True)
    start = jnp.sum(jnp.where(row < wanted, each, 0), axis=0, keepdims=True)
    return each, end, size, start


def owner(each, end, position):
    passed = end <= position
    parent = jnp.sum(passed.astype(jnp.int32), axis=0, keepdims=True)
    return parent, position[0:1] - jnp.sum(jnp.where(passed, each, 0), axis=0, keepdims=True)


def restrict(sources, at, lane_of, down_ref):
    parts = []
    for i in range(len(at[0])):
        picked = [pick(*one) for one in zip(sources, [row[i] for row in at], [row[i] for row in lane_of])]
        high, low = halves(jnp.concatenate(picked, axis=1))
        parts += [high, low, high]
    both = jnp.dot(down_ref[...], jnp.concatenate(parts, axis=0), preferred_element_type=jnp.float32)
    modes = sources[0][0].shape[0]
    pairs = both.shape[0] // modes
    width = LANES // pairs
    totals = []
    for b in range(len(sources)):
        mine = both[:, b * LANES : (b + 1) * LANES]
        total = mine[:modes]
        for k in range(1, pairs):
            total = total + pltpu.roll(mine[k * modes : (k + 1) * modes], LANES - k * width, 1)
        totals.append(jnp.where(lanes() < width, total, 0.0))
    return totals


def last_parents(tail, modes, parents, extra):
    wanted = parents - extra + jnp.bitwise_and(lanes(parents), extra - 1)
    each, end, size, start = children(tail[modes : modes + 1].astype(jnp.int32), parents, wanted)
    rows = jnp.broadcast_to(tail[modes + 1 : modes + 2], (8, LANES))
    conds = take(rows, wanted[0:1])[0:1]
    total = jnp.sum(each, axis=0, keepdims=True)
    position = total - HEAD + jnp.bitwise_and(lanes(parents), HEAD - 1)
    parent, octant = owner(each, end, position)
    return size, start, conds, parent - (parents - extra), octant


def restrict_kernel(
    blocks, parents, r_ref, near_ref, gather_ref, cond_ref, down_ref, right_out, scale_out, front_out
):
    modes = r_ref.shape[0]
    count = r_ref.shape[1] // blocks
    lane = lanes()
    pairs = LANES // parents
    heads = LANES // HEAD
    extra = LANES // OCTANTS
    packed = parents // extra
    chip, core = own_place()
    own_tiles = blocks // pairs
    tails = near_ref.shape[1] - blocks * LANES
    right_out[...] = jnp.zeros(right_out.shape, jnp.float32)
    scale_out[...] = jnp.ones(scale_out.shape, jnp.float32)

    def body(js, g):
        sources, at, there = [], [], []
        for j in js:
            source = j + core
            tile = pl.ds(pl.multiple_of((jnp.minimum(source, blocks - 1) // heads) * LANES, LANES), LANES)
            arriving = pltpu.roll(near_ref[:modes, tile], (LANES - (source % heads) * HEAD) % LANES, 1)
            arriving = jnp.where(source < blocks, arriving, 0.0)
            own = [r_ref[:, cols(j, count, h)] for h in range(0, count, LANES)]
            sources.append([jnp.where(lane < HEAD, arriving, own[0])] + own[1:])
            places = [gather_ref[i : i + 1, cols(j, LANES)] for i in range(OCTANTS // pairs)]
            at.append([jnp.right_shift(place, 7) for place in places])
            there.append([jnp.bitwise_and(place, LANES - 1) for place in places])
            mine = jnp.broadcast_to(cond_ref[pl.ds(j, 1), :], (8, LANES))
            mine = pltpu.roll(mine, (j % pairs) * parents, 1)[0:1]
            spot = cols(j // pairs, LANES)
            scale_out[:, spot] = jnp.where(lane // parents == j % pairs, mine, scale_out[:, spot])
        before(js[0] // packed, sources, at, there)
        totals = restrict(sources, at, there, down_ref)
        for j, total in zip(js, totals):
            spot = cols(j // pairs, LANES)
            right_out[:, spot] = right_out[:, spot] + pltpu.roll(total, (j % pairs) * parents, 1)
        v = js[0] // packed
        spot = cols(v // pairs, LANES, own_tiles * LANES)
        right_out[:, spot] = right_out[:, spot] + pltpu.roll(totals[-1], (v % pairs) * parents, 1)

    def before(v, all_sources, all_at, all_there):
        group = jnp.bitwise_and(lane // extra, packed - 1)
        sources = []
        start = size = head_parent = head_octant = jnp.zeros((1, LANES), jnp.int32)
        conds = jnp.ones((1, LANES), jnp.float32)
        for i in range(packed):
            j = packed * v + i
            at = j - (1 - core)
            tail = near_ref[:, pl.ds(pl.multiple_of(tails + jnp.maximum(at, 0) * LANES, LANES), LANES)]
            sources.append(jnp.where(lane < HEAD, r_ref[:, cols(j, count, 0)], tail[:modes]))
            one_size, one_start, one_cond, parent, octant = last_parents(tail, modes, parents, extra)
            mine = group == i
            size = jnp.where(jnp.logical_and(mine, at >= 0), one_size, size)
            start = jnp.where(mine, one_start, start)
            conds = jnp.where(jnp.logical_and(mine, lane < parents), one_cond, conds)
            here = lane // HEAD == j % heads
            head_parent = jnp.where(here, parent + (v % pairs) * parents + i * extra, head_parent)
            head_octant = jnp.where(here, octant, head_octant)
        octants = [pairs * i + lane // parents for i in range(OCTANTS // pairs)]
        all_sources.append(sources)
        all_at.append([jnp.where(octant < size, group, -1) for octant in octants])
        all_there.append([jnp.bitwise_and(start + octant + HEAD, LANES - 1) for octant in octants])
        spot = cols(v // pairs, LANES, own_tiles * LANES)
        conds = pltpu.roll(jnp.broadcast_to(conds, (8, LANES)), (v % pairs) * parents, 1)[0:1]
        scale_out[:, spot] = jnp.where(lane // parents == v % pairs, conds, scale_out[:, spot])
        front_out[v, 0:1, :LANES] = head_parent
        front_out[v, 0:1, LANES:] = head_octant

    over_groups(blocks, body)


def coarse_kernel(
    blocks, parents, rims, right_ref, scale_ref, front_ref, r_ref, cross_ref, gather_ref, parent_ref, octant_ref,
    stiff_ref, down_ref, up_ref, c_ref, t_ref, rim_ref, face_ref, p_out, rims_out, right, scale, front, edge,
):
    modes = r_ref.shape[0]
    count = r_ref.shape[1] // blocks
    lane = lanes()
    pairs = LANES // parents
    heads = LANES // HEAD
    extra = LANES // OCTANTS
    packed = parents // extra
    chip, core = own_place()
    segment, segments = lax.axis_index("blk"), lax.axis_size("blk")
    own_tiles = blocks // pairs
    edge[...] = jnp.zeros(edge.shape, jnp.float32)
    right[...] = right_ref[...]
    scale[...] = scale_ref[...]
    front[...] = front_ref[...]

    cross = cross_ref[...]
    size, start, conds, parent, octant = last_parents(cross, modes, parents, extra)
    above = jnp.where(jnp.logical_and(lane < HEAD, segment < segments - 1), cross[:modes], 0.0)
    below = jnp.where(lane < HEAD, r_ref[:, :LANES], cross[:modes])
    below = jnp.where(segment == 0, 0.0, below)
    at, there = [], []
    for i in range(OCTANTS // pairs):
        place = gather_ref[i : i + 1, cols(blocks - 1, LANES)]
        one = pairs * i + lane // parents
        inside = jnp.logical_and(place >= 0, place < HEAD)
        mine = jnp.logical_and(jnp.bitwise_and(lane, parents - 1) < extra, one < size)
        at.append(jnp.where(core == 1, jnp.where(inside, 0, -1), jnp.where(mine, 0, -1)))
        there.append(jnp.bitwise_and(jnp.where(core == 1, place, start + one + HEAD), LANES - 1))
    (added,) = restrict([[jnp.where(core == 1, above, below)]], [at], [there], down_ref)
    spot = cols((blocks - 1) // pairs, LANES)
    moved = pltpu.roll(added, ((blocks - 1) % pairs) * parents, 1)
    right[:, spot] = right[:, spot] + jnp.where(core == 1, moved, 0.0)
    spot = cols(0, LANES, own_tiles * LANES)
    right[:, spot] = right[:, spot] + jnp.where(core == 0, added, 0.0)
    scale[:, spot] = jnp.where(jnp.logical_and(core == 0, lane < extra), conds, scale[:, spot])
    first = jnp.logical_and(core == 0, lane < HEAD)
    front[0, 0:1, :LANES] = jnp.where(first, parent, front[0, 0:1, :LANES])
    front[0, 0:1, LANES:] = jnp.where(first, octant, front[0, 0:1, LANES:])

    eye = lax.broadcasted_iota(jnp.int32, (modes, modes), 0) == lax.broadcasted_iota(
        jnp.int32, (modes, modes), 1
    )
    diagonal = jnp.sum(jnp.where(eye, stiff_ref[...], 0.0), axis=1, keepdims=True)
    tiles = right.shape[1] // LANES
    inverse = 1.0 / (scale[...] * diagonal + 2.0 * COUPLING)
    residual = right[...]
    p = residual * inverse * (1.0 / CENTER)
    field = p
    for ahead, correct in steps(KC - 1):
        pieces = []
        for t in range(tiles):
            here = p[:, t * LANES : (t + 1) * LANES]
            last = (parents if t < own_tiles else extra) - 1
            left = jnp.where(jnp.bitwise_and(lane, last) == 0, 0.0, pltpu.roll(here, 1, 1))
            after = jnp.where(jnp.bitwise_and(lane, last) == last, 0.0, pltpu.roll(here, LANES - 1, 1))
            pieces.append(left + after)
        sides = jnp.concatenate(pieces, axis=1)
        residual = residual - (scale[...] * product(c_ref[...], p) + COUPLING * (2.0 * p - sides))
        p = ahead * p + correct * (residual * inverse)
        field = field + p
    right[...] = field

    def prolong(js, g):
        span = cols(g, len(js) * count)
        v = js[0] // packed
        leading = take(right[:, cols(own_tiles + v // pairs, LANES)], front[v, 0:1, :LANES])
        leading_octant = jnp.broadcast_to(front[v, 0:1, LANES:], (8, LANES))
        spread, octants = [], []
        for j in js:
            parent = right[:, cols(j // pairs, LANES)]
            back = (LANES - (j % heads) * HEAD) % LANES
            for h in range(0, count, LANES):
                spot = cols(j, count, h)
                one, octant = take(parent, parent_ref[:, spot]), octant_ref[:, spot]
                if h == 0:
                    one = jnp.where(lane < HEAD, pltpu.roll(leading, back, 1), one)
                    octant = jnp.where(lane < HEAD, pltpu.roll(leading_octant, back, 1)[0:1], octant)
                spread.append(one)
                octants.append(octant)
        high, low = halves(jnp.concatenate(spread, axis=1))
        octant = jnp.concatenate(octants, axis=1)
        parts = []
        for o in range(OCTANTS):
            mine = (octant == o).astype(jnp.float32).astype(jnp.bfloat16)
            parts += [high * mine, low * mine, high * mine]
        p = jnp.dot(up_ref[...], jnp.concatenate(parts, axis=0), preferred_element_type=jnp.float32)
        p_out[:, span] = p
        for i, j in enumerate(js):
            keep_edge(j, of_block(p, i, count), rim_ref, edge, rims)

    over_groups(blocks, prolong)
    for t in range(edge.shape[1] // LANES):
        spot = slice(t * LANES, (t + 1) * LANES)
        rims_out[:, spot] = rim_traces(t_ref, edge[:, spot], face_ref[:, spot])


def spread_kernel(blocks, width, p_ref, t_ref, sub_ref, _, tr_out, subs_out):
    count = p_ref.shape[1] // blocks

    def body(js, g):
        span = cols(g, len(js) * count)
        traces = product(t_ref[...], p_ref[:, span])
        tr_out[:, span] = traces
        for i, j in enumerate(js):
            send_sub(j, trace_tiles(of_block(traces, i, count)), sub_ref, subs_out, width)

    over_groups(blocks, body)


def call(limit, kernel, outs, *args, scratch=(), hbm=False, flops=3 * 10**9):
    args = [pltpu.with_memory_space_constraint(x, pltpu.HBM) for x in args] if hbm else args
    return pl.pallas_call(
        kernel,
        out_shape=[jax.ShapeDtypeStruct(shape, kind) for shape, kind in outs],
        in_specs=[pl.BlockSpec(memory_space=pltpu.HBM if hbm else pltpu.VMEM)] * len(args),
        out_specs=[pl.BlockSpec(memory_space=pltpu.VMEM)] * len(outs),
        scratch_shapes=list(scratch),
        compiler_params=pltpu.CompilerParams(vmem_limit_bytes=limit),
        cost_estimate=pl.CostEstimate(flops=flops, bytes_accessed=1, transcendentals=0),
    )(*args)


def local(
    right_side,
    conductivity,
    material,
    stiffness,
    trace_map,
    face_neighbour,
    sub_sends,
    blk_sends,
    group_sizes,
    coarse_conductivity,
    coarse_stiffness,
    restriction,
):
    f32, i32, bf16 = jnp.float32, jnp.int32, jnp.bfloat16
    modes, count = right_side.shape
    rows = trace_map.shape[0]
    points = rows // FACES
    peers, segments = lax.axis_size("sub"), lax.axis_size("blk")
    blocks = peers // CORES
    parents = group_sizes.shape[1]
    width, rims = sub_sends.shape[1], blk_sends.shape[1]
    total = blocks * count
    limit = (4 << 20) if blocks <= 4 else (40 << 20)
    run = functools.partial(call, limit)

    def pad(size, to):
        return -(-size // to) * to

    rim_width = pad(blocks * rims, LANES)
    near_width = pad(blocks * HEAD, LANES) + blocks * LANES
    field = ((modes, total), f32)
    block = ((modes, count), f32)
    sends = [((rows, total), f32), ((points, blocks * width), f32), ((points, rim_width), f32)]

    def everywhere(partner):
        pairs = []
        for b in range(segments):
            for s in range(peers):
                other_b, other_s = partner(b, s)
                pairs.append((b * peers + s, other_b * peers + other_s))
        return pairs

    def above_or_below(first):
        def partner(b, s):
            other = b + 1 if b % 2 == first else b - 1
            return (other, s) if 0 <= other < segments else (b, s ^ 1)

        return everywhere(partner)

    def crossing(b, s):
        other = b - 1 if s % 2 == 0 else b + 1
        return (other, s ^ 1) if 0 <= other < segments else (b, s ^ 2)

    both = ("blk", "sub")
    cores = [(s, s ^ 1) for s in range(peers)]
    ones, twos, crossings = above_or_below(0), above_or_below(1), everywhere(crossing)

    def over_segments(rim):
        return lax.ppermute(rim, both, ones), lax.ppermute(rim, both, twos)

    map_t = trace_map.T
    t3, tt3, k3 = run(
        prep_kernel,
        [((rows, 3 * modes), bf16), ((modes, 3 * rows), bf16), ((2 * modes, 3 * modes), bf16)],
        map_t, stiffness,
    )
    down3, up3, c3 = run(
        prep_coarse_kernel,
        [((LANES // parents * modes, OCTANTS * parents // LANES * 3 * modes), bf16), ((modes, OCTANTS * 3 * modes), bf16), ((modes, 3 * modes), bf16)],
        restriction, coarse_stiffness,
    )

    height = pad(modes + 11 + pad(width, count) // count, 8)
    inputs = [
        right_side, conductivity.reshape(1, count), material.reshape(1, count), face_neighbour, sub_sends, blk_sends,
        group_sizes, coarse_conductivity.reshape(1, -1),
    ]
    (packed,) = run(
        pack_kernel,
        [((height, count), f32)],
        *inputs,
        scratch=[pltpu.VMEM(x.shape, x.dtype) for x in inputs] + [pltpu.SemaphoreType.DMA((len(inputs),))],
        hbm=True,
    )
    gathered = [packed] + [
        lax.ppermute(packed, "sub", [(s, s ^ (CORES * k)) for s in range(peers)]) for k in range(1, blocks)
    ]
    b, inverse, meta, lane, at, far, edge, subs, rim, sizes, coarse_cond, rim_face, p, rim_out = run(
        functools.partial(start_kernel, blocks, width, rims),
        [
            field, field, ((8, total), f32), *[((8, total), i32)] * 4,
            ((1, blocks * width), i32), ((1, rim_width), i32), ((blocks, LANES), i32), ((blocks, LANES), f32),
            ((1, rim_width), i32), field, sends[2],
        ],
        *gathered, stiffness, map_t, t3, c3,
        scratch=[pltpu.VMEM((blocks, height, count), f32), pltpu.VMEM((modes, rim_width), f32)],
    )
    traces, sub_out = run(functools.partial(spread_kernel, blocks, width), sends[:2], p, t3, subs, rim_out)

    edges, igs = run(
        functools.partial(rim_kernel, blocks, rims), [((8, rim_width), i32), ((modes, rim_width), f32)], rim, edge, inverse
    )
    gather, parent, octant = run(
        functools.partial(layout_kernel, blocks, parents),
        [((OCTANTS * parents // LANES, blocks * LANES), i32), ((1, total), i32), ((1, total), i32)],
        sizes,
        flops=3 * 10**10,
    )
    def apply(kind, coefficients, r, p, traces, sub_out, rim_out, x):
        one, two = over_segments(rim_out)
        swapped = lax.ppermute(sub_out, "sub", cores)
        only_own = kind == "last"
        size = count if only_own else total
        part, col = ((modes, size), f32), ((rows, size), f32)
        jump, own, x = run(
            functools.partial(local_kernel, only_own, blocks, width, x is None),
            [col, part, block],
            p, traces, meta, lane, at, k3, *([] if x is None else [x]),
        )
        goes_on = kind in ("step", "first")
        kernel = functools.partial(ahead_kernel, kind, coefficients, blocks, width, rims)
        args = [r, jump, own, sub_out, swapped, far, tt3] + ([p] if kind == "step" else [])
        if not goes_on:
            (r,) = run(kernel, [part], *args)
            finish = functools.partial(finish_kernel, kind, None, blocks, width, rims)
            args = [r, one, two, edge, tt3]
            if only_own:
                return *run(finish, [block], *args), x
            args += [sizes, coarse_cond]
            (cross,) = run(functools.partial(cross_kernel, blocks, rims), [((modes + 8, LANES), f32)], *args)
            return *run(finish, [field, ((modes + 8, near_width), f32)], *args, cross), cross, x
        r, p, p_edge = run(kernel, [field, field, ((modes, rim_width), f32)], *args, inverse, rim)
        rate = coefficients[1]
        (rim_out,) = run(
            functools.partial(edge_kernel, rate, rims), [((points, rim_width), f32)],
            one, two, edges, igs, p_edge, tt3, t3, rim_face,
        )
        r, p, traces, sub_out = run(
            functools.partial(finish_kernel, kind, rate, blocks, width, rims),
            [field, field, ((rows, total), f32), ((points, blocks * width), f32)],
            r, one, two, edge, tt3, p, inverse, t3, subs, rim_out,
        )
        return r, p, traces, sub_out, rim_out, x

    x = None
    r = b
    pairs = steps(KF)
    for step in range(KF - 1):
        r, p, traces, sub_out, rim_out, x = apply("step", pairs[step], r, p, traces, sub_out, rim_out, x)
    r, near, cross, x = apply("frame", None, r, p, traces, sub_out, rim_out, x)

    cross = lax.ppermute(cross, both, crossings)
    near = lax.ppermute(near, "sub", cores)
    coarse_width = blocks * parents + pad(blocks * LANES // OCTANTS, LANES)
    front = ((blocks * LANES // OCTANTS // parents, 8, 2 * LANES), i32)
    right, scale, leading = run(
        functools.partial(restrict_kernel, blocks, parents),
        [((modes, coarse_width), f32), ((1, coarse_width), f32), front],
        r, near, gather, coarse_cond, down3,
        flops=10**8,
    )
    p, rim_out = run(
        functools.partial(coarse_kernel, blocks, parents, rims),
        [field, sends[2]],
        right, scale, leading, r, cross, gather, parent, octant, coarse_stiffness, down3, up3, c3, t3, rim, rim_face,
        scratch=[
            pltpu.VMEM((modes, coarse_width), f32),
            pltpu.VMEM((1, coarse_width), f32),
            pltpu.VMEM(*front),
            pltpu.VMEM((modes, rim_width), f32),
        ],
    )
    traces, sub_out = run(functools.partial(spread_kernel, blocks, width), sends[:2], p, t3, subs, rim_out)
    r, p, traces, sub_out, rim_out, x = apply("first", (0.0, 1.0 / CENTER), r, p, traces, sub_out, rim_out, x)
    for step in range(KF - 1):
        r, p, traces, sub_out, rim_out, x = apply("step", pairs[step], r, p, traces, sub_out, rim_out, x)
    residual, x = apply("last", None, r, p, traces, sub_out, rim_out, x)
    return x, residual


def solution(mesh):
    in_specs = (
        P(None, ("blk", "sub")),
        P(("blk", "sub")),
        P(("blk", "sub")),
        P(),
        P(),
        P(None, ("blk", "sub")),
        P(("blk", "sub"), None),
        P(("blk", "sub"), None),
        P(("blk", "sub"), None),
        P(("blk", "sub")),
        P(),
        P(),
    )
    out_specs = (P(None, ("blk", "sub")), P(None, ("blk", "sub")))
    return jax.shard_map(local, mesh=mesh, in_specs=in_specs, out_specs=out_specs, check_vma=False)
```

```python
import functools

import jax
import jax.numpy as jnp
from jax import lax
from jax.experimental import pallas as pl
from jax.experimental.pallas import tpu as pltpu
from jax.sharding import PartitionSpec as P

HEAD = 8
KF = 3
KC = 4
FACES = 6
OCTANTS = 8
LANES = 128
CORES = 2

PENALTY = 0.3
COUPLING = 0.5
LOW_EIG = 0.4
HIGH_EIG = 2.5
CENTER = 0.5 * (HIGH_EIG + LOW_EIG)
HALF = 0.5 * (HIGH_EIG - LOW_EIG)


def steps(sweeps):
    sigma = CENTER / HALF
    rho, pairs = 1.0 / sigma, []
    for _ in range(sweeps):
        rho_next = 1.0 / (2.0 * sigma - rho)
        pairs.append((rho_next * rho, 2.0 * rho_next / HALF))
        rho = rho_next
    return pairs


def halves(x):
    high = x.astype(jnp.bfloat16)
    return high, (x - high.astype(jnp.float32)).astype(jnp.bfloat16)


def product(left, x):
    high, low = halves(x)
    right = jnp.concatenate([high, low, high], axis=0)
    return jnp.dot(left, right, preferred_element_type=jnp.float32)


def face_product(left, x):
    high, low = halves(x)
    both = jnp.dot(left, jnp.concatenate([high, low], axis=0), preferred_element_type=jnp.float32)
    modes = both.shape[0] // 2
    return both[:modes] + both[modes:]


def store_left(out, rows, x, base=0):
    high, low = halves(x)
    width = x.shape[1]
    for place, piece in enumerate((high, high, low)):
        out[rows, base + place * width : base + (place + 1) * width] = piece


def take(tile, lane):
    index = jnp.broadcast_to(lane, tile.shape)
    return jnp.take_along_axis(tile, index, axis=1, mode="promise_in_bounds")


def pick(tiles, at, lane):
    out = jnp.zeros(tiles[0].shape, tiles[0].dtype)
    for number, tile in enumerate(tiles):
        out = jnp.where(at == number, take(tile, lane), out)
    return out


def lanes(rows=1):
    return lax.broadcasted_iota(jnp.int32, (rows, LANES), 1)


def cols(j, width, base=None):
    size, start = (width, j * width) if base is None else (LANES, j * width + base)
    return pl.ds(start if isinstance(j, int) else pl.multiple_of(start, LANES), size)


def over(blocks, body):
    if blocks <= 4:
        for j in range(blocks):
            body(j)
    else:
        lax.fori_loop(0, blocks, lambda j, carry: (body(j), carry)[1], 0)


def over_groups(blocks, body):
    size = min(blocks, 4)
    over(blocks // size, lambda g: body([g * size + i for i in range(size)], g))


def own_place():
    me = lax.axis_index("sub")
    return jnp.right_shift(me, 1), jnp.bitwise_and(me, 1)


def trace_tiles(traces):
    points = traces.shape[0] // FACES
    return [
        traces[f * points : (f + 1) * points, h : h + LANES]
        for f in range(FACES)
        for h in range(0, traces.shape[1], LANES)
    ]


def faces(tile_of, js, count):
    return jnp.concatenate(
        [
            jnp.concatenate([tile_of(j, f, h) for j in js for h in range(0, count, LANES)], axis=1)
            for f in range(FACES)
        ],
        axis=0,
    )


def of_block(x, i, count):
    return x[:, i * count : (i + 1) * count]


def send_sub(j, tiles, sub_ref, sub_out, width):
    for h in range(0, width, LANES):
        columns = sub_ref[:, cols(j, width, h)]
        sub_out[:, cols(j, width, h)] = pick(
            tiles, jnp.right_shift(columns, 7), jnp.bitwise_and(columns, LANES - 1)
        )


def send_rim(j, tiles, rim_ref, rim_out, rims):
    group = LANES // rims
    tile = cols(j // group, LANES)
    columns = rim_ref[:, tile]
    rim = pick(tiles, jnp.right_shift(columns, 7), jnp.bitwise_and(columns, LANES - 1))
    mine = lanes() // rims == j % group
    rim_out[:, tile] = jnp.where(mine, rim, rim_out[:, tile])


def prep_kernel(map_ref, stiff_ref, t_out, tt_out, k_out):
    modes, rows = map_ref.shape
    transposed = map_ref[...]
    high, low = halves(PENALTY * transposed)
    tt_out[:modes, :rows] = high
    tt_out[:modes, rows:] = high
    tt_out[modes:, :rows] = low
    tt_out[modes:, rows:] = jnp.zeros((modes, rows), jnp.bfloat16)
    store_left(t_out, slice(0, rows), transposed.T)
    for k in range(2):
        store_left(k_out, slice(k * modes, (k + 1) * modes), stiff_ref[k])


def prep_coarse_kernel(restriction_ref, stiff_ref, down_out, up_out, c_out):
    modes = stiff_ref.shape[0]
    store_left(c_out, slice(0, modes), stiff_ref[...])
    pairs = down_out.shape[0] // modes
    for o in range(OCTANTS):
        rows = slice(o % pairs * modes, (o % pairs + 1) * modes)
        store_left(down_out, rows, restriction_ref[o], o // pairs * 3 * modes)
        store_left(up_out, slice(0, modes), restriction_ref[o].T, o * 3 * modes)


def pack_kernel(
    b_ref, cond_ref, mat_ref, face_ref, sub_ref, rim_ref, size_ref, coarse_ref, out,
    b_in, cond_in, mat_in, face_in, sub_in, rim_in, size_in, coarse_in, done,
):
    sources = (b_ref, cond_ref, mat_ref, face_ref, sub_ref, rim_ref, size_ref, coarse_ref)
    places = (b_in, cond_in, mat_in, face_in, sub_in, rim_in, size_in, coarse_in)
    copies = [
        pltpu.make_async_copy(source, place, done.at[at])
        for at, (source, place) in enumerate(zip(sources, places))
    ]
    for copy in copies:
        copy.start()
    modes, count = b_in.shape
    out[modes:, :] = jnp.zeros((out.shape[0] - modes, count), jnp.float32)
    for copy in copies:
        copy.wait()
    out[:modes, :] = b_in[...]
    out[modes : modes + 1, :] = cond_in[...]
    out[modes + 1 : modes + 2, :] = mat_in[...].astype(jnp.float32)
    out[modes + 2 : modes + 8, :] = face_in[...].astype(jnp.float32)
    out[modes + 8 : modes + 9, : rim_in.shape[1]] = rim_in[...].astype(jnp.float32)
    out[modes + 9 : modes + 10, : size_in.shape[1]] = size_in[...].astype(jnp.float32)
    out[modes + 10 : modes + 11, : coarse_in.shape[1]] = coarse_in[...]
    width = sub_in.shape[1]
    for at, h in enumerate(range(0, width, count)):
        piece = sub_in[:, h : min(h + count, width)].astype(jnp.float32)
        out[modes + 11 + at : modes + 12 + at, : piece.shape[1]] = piece


def start_kernel(blocks, width, rims, *refs):
    gathered, refs = refs[:blocks], refs[blocks:]
    stiff_ref, map_ref, t_ref, _ = refs[:4]
    b_out, ig_out, meta_out, lane_out, at_out, far_out, edge_out, sub_out, rim_out, size_out, coarse_out = refs[4:15]
    face_out, p_out, rims_out, held, edge = refs[15:]
    modes, count = map_ref.shape[0], gathered[0].shape[1]
    chip, core = own_place()
    for k, ref in enumerate(gathered):
        held[jnp.bitwise_xor(chip, k)] = ref[...]
    eye = lax.broadcasted_iota(jnp.int32, (modes, modes), 0) == lax.broadcasted_iota(
        jnp.int32, (modes, modes), 1
    )
    diagonals = [
        jnp.sum(jnp.where(eye, stiff_ref[k], 0.0), axis=1, keepdims=True) for k in range(2)
    ]
    squares = PENALTY * jnp.sum(map_ref[...] * map_ref[...], axis=1, keepdims=True)
    own_tiles = FACES * count // LANES
    sub_tiles = width // LANES
    rim_out[...] = jnp.zeros(rim_out.shape, jnp.int32)
    group = LANES // rims

    def body(j):
        b = held[j, :modes, :]
        cond = held[j, modes : modes + 1, :]
        mat = held[j, modes + 1 : modes + 2, :]
        b_out[:, cols(j, count)] = b
        meta_out[0:1, cols(j, count)] = cond
        meta_out[1:2, cols(j, count)] = mat
        column = held[j, modes + 2 : modes + 8, :].astype(jnp.int32)
        lane = jnp.bitwise_and(column, LANES - 1)
        at = jnp.right_shift(column, 7)
        lane_out[0:FACES, cols(j, count)] = lane
        at_out[0:FACES, cols(j, count)] = at
        rim = jnp.logical_and(at == own_tiles + sub_tiles, lane < rims)
        sub = jnp.logical_and(at >= own_tiles, at < own_tiles + sub_tiles)
        far_out[0:FACES, cols(j, count)] = jnp.where(sub, column - own_tiles * LANES, -1)
        edge_out[0:FACES, cols(j, count)] = jnp.where(
            rim, jnp.bitwise_xor(lane, rims // 2) + (j % group) * rims, -1
        )
        for h in range(0, width, LANES):
            row = modes + 11 + h // count
            piece = held[j, row : row + 1, h % count : h % count + LANES]
            sub_out[:, cols(j, width, h)] = piece.astype(jnp.int32)
        row = jnp.broadcast_to(held[j, modes + 8 : modes + 9, :LANES], (8, LANES))
        row = pltpu.roll(row, (j % group) * rims, 1)[0:1].astype(jnp.int32)
        tile = cols(j // group, LANES)
        rim_out[:, tile] = jnp.where(lanes() // rims == j % group, row, rim_out[:, tile])
        size_out[pl.ds(j, 1), :] = held[j, modes + 9 : modes + 10, :LANES].astype(jnp.int32)
        coarse_out[pl.ds(j, 1), :] = held[j, modes + 10 : modes + 11, :LANES]
        inverse = 1.0 / (cond * jnp.where(mat == 1.0, diagonals[1], diagonals[0]) + squares)
        ig_out[:, cols(j, count)] = inverse
        p_out[:, cols(j, count)] = b * inverse * (1.0 / CENTER)

    over(blocks, body)
    spot = lax.broadcasted_iota(jnp.int32, rim_out.shape, 1)
    face_out[...] = jnp.where(spot < blocks * rims, lax.div(rim_out[...], jnp.int32(count)), -1)
    edge[...] = jnp.zeros(edge.shape, jnp.float32)
    over(blocks, lambda j: keep_edge(j, p_out[:, cols(j, count)], rim_out, edge, rims))
    rims_out[...] = rim_traces(t_ref, edge[...], face_out[...])


def sub_tiles_of(j, sends_refs, core, width, blocks):
    slots = width // (blocks * CORES)
    pairs = LANES // slots // CORES
    lane = lanes()
    mine = lax.axis_index("sub") % CORES
    source = (CORES * (j % pairs) + mine) * slots + lane % slots
    tiles = []
    for t in range(width // LANES):
        tile = None
        for i in range(pairs):
            for ref, sender in zip(sends_refs, (core, 1 - core)):
                there = take(ref[:, cols(j // pairs, LANES, (pairs * t + i) * width)], source)
                tile = there if tile is None else jnp.where(lane // slots == CORES * i + sender, there, tile)
        tiles.append(tile)
    return tiles


def rim_element(columns, count):
    return jnp.bitwise_and(jnp.right_shift(columns, 7), count // LANES - 1), jnp.bitwise_and(columns, LANES - 1)


def local_kernel(only_own, blocks, width, first, *refs):
    p_ref, tr_ref, meta_ref, lane_ref, at_ref, k_ref = refs[:6]
    refs = refs[6:]
    if not first:
        x_ref, refs = refs[0], refs[1:]
    jump_out, own_out, x_out = refs
    modes = p_ref.shape[0]
    chip, core = own_place()
    count = x_out.shape[1]

    def body(js, span, out):
        traces = tr_ref[:, span]
        at_rows, lane_rows = at_ref[:, span], lane_ref[:, span]
        tiles = [
            trace_tiles(of_block(traces, i, count)) for i in range(len(js))
        ]

        def tile(i, f, h):
            row, place = slice(f, f + 1), slice(i * count + h, i * count + h + LANES)
            return pick(tiles[i], at_rows[row, place], lane_rows[row, place])

        jump_out[:, out] = traces - faces(tile, range(len(js)), count)
        both = product(k_ref[...], p_ref[:, span])
        meta = meta_ref[:, span]
        own_out[:, out] = meta[0:1] * jnp.where(meta[1:2] == 1.0, both[modes:], both[:modes])

    if only_own:
        body([chip], cols(chip, count), slice(0, count))
    else:
        over_groups(blocks, lambda js, g: body(js, cols(g, len(js) * count), cols(g, len(js) * count)))
    p = p_ref[:, cols(chip, count)]
    x_out[...] = p if first else x_ref[...] + p


def ahead_kernel(kind, coefficients, blocks, width, rims, *refs):
    r_ref, jump_ref, own_ref, subs_ref, swapped_ref, far_ref, tt_ref = refs[:7]
    refs = list(refs[7:])
    chip, core = own_place()
    count = own_ref.shape[1] // (1 if kind == "last" else blocks)
    group = LANES // rims
    lane = lanes()
    p_ref = refs.pop(0) if kind == "step" else None
    if kind in ("step", "first"):
        ig_ref, rim_ref, r_out, p_out, edge_out = refs
        edge_out[...] = jnp.zeros(edge_out.shape, jnp.float32)
    else:
        r_out = refs[0]

    def body(js, span, here):
        tiles = [sub_tiles_of(j, (subs_ref, swapped_ref), core, width, blocks) for j in js]
        far = far_ref[:, span]

        def tile(i, f, h):
            column = far[f : f + 1, i * count + h : i * count + h + LANES]
            return pick(tiles[i], jnp.right_shift(column, 7), jnp.bitwise_and(column, LANES - 1))

        jump = face_product(tt_ref[...], jump_ref[:, here] - faces(tile, range(len(js)), count))
        residual = r_ref[:, span] - own_ref[:, here] - jump
        r_out[:, here] = residual
        if kind in ("frame", "last"):
            return
        p = coefficients[1] * (residual * ig_ref[:, here])
        if kind == "step":
            p = p + coefficients[0] * p_ref[:, here]
        p_out[:, here] = p
        for i, j in enumerate(js):
            keep_edge(j, of_block(p, i, count), rim_ref, edge_out, rims)

    if kind == "last":
        body([chip], cols(chip, count), slice(0, count))
    else:
        over_groups(blocks, lambda js, g: body(js, cols(g, len(js) * count), cols(g, len(js) * count)))


def rim_tile(one_ref, two_ref, spot, rims):
    segment, segments = lax.axis_index("blk"), lax.axis_size("blk")
    odd = segment % 2 == 1
    low = jnp.where(odd, one_ref[:, spot], two_ref[:, spot])
    high = jnp.where(odd, two_ref[:, spot], one_ref[:, spot])
    low = jnp.where(segment == 0, 0.0, low)
    high = jnp.where(segment == segments - 1, 0.0, high)
    return jnp.where(lanes() % rims < rims // 2, high, low)


def rim_seen(rim, edge, f, h):
    place = edge[f : f + 1, h : h + LANES]
    return jnp.where(place >= 0, take(rim, jnp.bitwise_and(place, LANES - 1)), 0.0)


def keep_edge(j, p, rim_ref, edge_out, rims):
    group = LANES // rims
    spot = cols(j // group, LANES)
    count = p.shape[1]
    at, there = rim_element(rim_ref[:, spot], count)
    edge = pick([p[:, h : h + LANES] for h in range(0, count, LANES)], at, there)
    edge_out[:, spot] = jnp.where(lanes() // rims == j % group, edge, edge_out[:, spot])


def rim_traces(t_ref, p, face):
    traces = product(t_ref[...], p)
    points = traces.shape[0] // FACES
    out = jnp.zeros((points, p.shape[1]), jnp.float32)
    for f in range(FACES):
        out = jnp.where(face == f, traces[f * points : (f + 1) * points], out)
    return out


def edge_kernel(rate, rims, one_ref, two_ref, edges_ref, igs_ref, p_ref, tt_ref, t_ref, face_ref, rims_out):
    for t in range(one_ref.shape[1] // LANES):
        spot = slice(t * LANES, (t + 1) * LANES)
        rim = rim_tile(one_ref, two_ref, spot, rims)
        edge = edges_ref[:, spot]
        added = face_product(tt_ref[...], faces(lambda _, f, h: rim_seen(rim, edge, f, h), [0], LANES))
        p = p_ref[:, spot] + rate * (igs_ref[:, spot] * added)
        rims_out[:, spot] = rim_traces(t_ref, p, face_ref[:, spot])


def cross_kernel(blocks, rims, r_ref, one_ref, two_ref, edge_ref, tt_ref, size_ref, cond_ref, cross_out):
    modes = r_ref.shape[0]
    count = r_ref.shape[1] // blocks
    group = LANES // rims
    chip, core = own_place()
    last = blocks - 1
    first_tile, last_tile = cols(0, count, 0), cols(last, count, count - LANES)
    rim = jnp.where(
        core == 0,
        rim_tile(one_ref, two_ref, cols(0, LANES), rims),
        rim_tile(one_ref, two_ref, cols(last // group, LANES), rims),
    )
    edge = jnp.where(core == 0, edge_ref[:, first_tile], edge_ref[:, last_tile])
    seen = faces(lambda _, f, h: rim_seen(rim, edge, f, h), [0], LANES)
    residual = jnp.where(core == 0, r_ref[:, first_tile], r_ref[:, last_tile])
    cross_out[modes:, :] = jnp.zeros((cross_out.shape[0] - modes, LANES), jnp.float32)
    cross_out[:modes, :] = residual + face_product(tt_ref[...], seen)
    cross_out[modes : modes + 1, :] = size_ref[last : last + 1, :].astype(jnp.float32)
    cross_out[modes + 1 : modes + 2, :] = cond_ref[last : last + 1, :]


def finish_kernel(kind, rate, blocks, width, rims, *refs):
    r_ref, one_ref, two_ref, edge_ref, tt_ref = refs[:5]
    refs = list(refs[5:])
    chip, core = own_place()
    group = LANES // rims
    lane = lanes()
    if kind in ("step", "first"):
        p_ref, ig_ref, t_ref, sub_ref, _, r_out, p_out, tr_out, subs_out = refs
    elif kind == "frame":
        size_ref, cond_ref, _, r_out, near_out = refs
        near_out[...] = jnp.zeros(near_out.shape, jnp.float32)
    else:
        r_out = refs[0]
    count = r_out.shape[1] // (1 if kind == "last" else blocks)
    modes = r_ref.shape[0]

    def body(js, span, here):
        rim = [rim_tile(one_ref, two_ref, cols(j // group, LANES), rims) for j in js]
        edge = edge_ref[:, span]

        def tile(i, f, h):
            return rim_seen(rim[i], edge, f, i * count + h)

        added = face_product(tt_ref[...], faces(tile, range(len(js)), count))
        residual = r_ref[:, here] + added
        r_out[:, here] = residual
        if kind == "frame":
            heads = LANES // HEAD
            for i, j in enumerate(js):
                spot = cols(j // heads, LANES)
                mine = of_block(residual, i, count)
                moved = pltpu.roll(mine[:, :LANES], (j % heads) * HEAD, 1)
                near_out[:modes, spot] = jnp.where(lane // HEAD == j % heads, moved, near_out[:modes, spot])
                tail = cols(j, LANES, near_out.shape[1] - blocks * LANES)
                near_out[:modes, tail] = mine[:, count - LANES :]
                near_out[modes : modes + 1, tail] = size_ref[pl.ds(j, 1), :].astype(jnp.float32)
                near_out[modes + 1 : modes + 2, tail] = cond_ref[pl.ds(j, 1), :]
        if kind in ("frame", "last"):
            return
        p = p_ref[:, here] + rate * (ig_ref[:, here] * added)
        p_out[:, here] = p
        traces = product(t_ref[...], p)
        tr_out[:, here] = traces
        for i, j in enumerate(js):
            send_sub(j, trace_tiles(of_block(traces, i, count)), sub_ref, subs_out, width)

    if kind == "last":
        body([chip], cols(chip, count), slice(0, count))
    else:
        over_groups(blocks, lambda js, g: body(js, cols(g, len(js) * count), cols(g, len(js) * count)))


def layout_kernel(blocks, parents, size_ref, gather_out, parent_out, octant_out):
    lane = lanes()
    pairs = LANES // parents
    half = jnp.right_shift(lane, parents.bit_length() - 1)
    count = parent_out.shape[1] // blocks

    def body(j):
        each, end, size, start = children(size_ref[pl.ds(j, 1), :], parents, jnp.bitwise_and(lanes(parents), parents - 1))
        for i in range(OCTANTS // pairs):
            octant = pairs * i + half
            place = jnp.bitwise_and(start + octant + HEAD, count - 1)
            gather_out[i : i + 1, cols(j, LANES)] = jnp.where(octant < size, place, -1)
        for h in range(0, count, LANES):
            position = jnp.bitwise_and(lanes(parents) + (h - HEAD), count - 1)
            parent, octant = owner(each, end, position)
            parent_out[:, cols(j, count, h)] = parent + parents * (j % pairs)
            octant_out[:, cols(j, count, h)] = octant

    over(blocks, body)


def rim_kernel(blocks, rims, rim_ref, edge_ref, ig_ref, edges_out, igs_out):
    group = LANES // rims
    edges_out[...] = jnp.full(edges_out.shape, -1, jnp.int32)
    igs_out[...] = jnp.zeros(igs_out.shape, jnp.float32)
    count = ig_ref.shape[1] // blocks

    def body(j):
        tile = cols(j // group, LANES)
        mine = lanes() // rims == j % group
        at, there = rim_element(rim_ref[:, tile], count)
        edges = pick([edge_ref[:, cols(j, count, h)] for h in range(0, count, LANES)], at, there)
        igs = pick([ig_ref[:, cols(j, count, h)] for h in range(0, count, LANES)], at, there)
        edges_out[:, tile] = jnp.where(mine, edges, edges_out[:, tile])
        igs_out[:, tile] = jnp.where(mine, igs, igs_out[:, tile])

    over(blocks, body)


def children(sizes, parents, wanted):
    row = lax.broadcasted_iota(jnp.int32, (parents, LANES), 0)
    lane = lanes(parents)
    sizes = jnp.broadcast_to(sizes, (parents, LANES))
    each = jnp.sum(jnp.where(row == lane, sizes, 0), axis=1, keepdims=True)
    end = jnp.sum(jnp.where(lane <= row, sizes, 0), axis=1, keepdims=True)
    size = jnp.sum(jnp.where(row == wanted, each, 0), axis=0, keepdims=True)
    start = jnp.sum(jnp.where(row < wanted, each, 0), axis=0, keepdims=True)
    return each, end, size, start


def owner(each, end, position):
    passed = end <= position
    parent = jnp.sum(passed.astype(jnp.int32), axis=0, keepdims=True)
    return parent, position[0:1] - jnp.sum(jnp.where(passed, each, 0), axis=0, keepdims=True)


def restrict(sources, at, lane_of, down_ref):
    parts = []
    for i in range(len(at[0])):
        picked = [pick(*one) for one in zip(sources, [row[i] for row in at], [row[i] for row in lane_of])]
        high, low = halves(jnp.concatenate(picked, axis=1))
        parts += [high, low, high]
    both = jnp.dot(down_ref[...], jnp.concatenate(parts, axis=0), preferred_element_type=jnp.float32)
    modes = sources[0][0].shape[0]
    pairs = both.shape[0] // modes
    width = LANES // pairs
    totals = []
    for b in range(len(sources)):
        mine = both[:, b * LANES : (b + 1) * LANES]
        total = mine[:modes]
        for k in range(1, pairs):
            total = total + pltpu.roll(mine[k * modes : (k + 1) * modes], LANES - k * width, 1)
        totals.append(jnp.where(lanes() < width, total, 0.0))
    return totals


def last_parents(tail, modes, parents, extra):
    wanted = parents - extra + jnp.bitwise_and(lanes(parents), extra - 1)
    each, end, size, start = children(tail[modes : modes + 1].astype(jnp.int32), parents, wanted)
    rows = jnp.broadcast_to(tail[modes + 1 : modes + 2], (8, LANES))
    conds = take(rows, wanted[0:1])[0:1]
    total = jnp.sum(each, axis=0, keepdims=True)
    position = total - HEAD + jnp.bitwise_and(lanes(parents), HEAD - 1)
    parent, octant = owner(each, end, position)
    return size, start, conds, parent - (parents - extra), octant


def restrict_kernel(
    blocks, parents, r_ref, near_ref, gather_ref, cond_ref, down_ref, right_out, scale_out, front_out
):
    modes = r_ref.shape[0]
    count = r_ref.shape[1] // blocks
    lane = lanes()
    pairs = LANES // parents
    heads = LANES // HEAD
    extra = LANES // OCTANTS
    packed = parents // extra
    chip, core = own_place()
    own_tiles = blocks // pairs
    tails = near_ref.shape[1] - blocks * LANES
    right_out[...] = jnp.zeros(right_out.shape, jnp.float32)
    scale_out[...] = jnp.ones(scale_out.shape, jnp.float32)

    def body(js, g):
        sources, at, there = [], [], []
        for j in js:
            source = j + core
            tile = pl.ds(pl.multiple_of((jnp.minimum(source, blocks - 1) // heads) * LANES, LANES), LANES)
            arriving = pltpu.roll(near_ref[:modes, tile], (LANES - (source % heads) * HEAD) % LANES, 1)
            arriving = jnp.where(source < blocks, arriving, 0.0)
            own = [r_ref[:, cols(j, count, h)] for h in range(0, count, LANES)]
            sources.append([jnp.where(lane < HEAD, arriving, own[0])] + own[1:])
            places = [gather_ref[i : i + 1, cols(j, LANES)] for i in range(OCTANTS // pairs)]
            at.append([jnp.right_shift(place, 7) for place in places])
            there.append([jnp.bitwise_and(place, LANES - 1) for place in places])
            mine = jnp.broadcast_to(cond_ref[pl.ds(j, 1), :], (8, LANES))
            mine = pltpu.roll(mine, (j % pairs) * parents, 1)[0:1]
            spot = cols(j // pairs, LANES)
            scale_out[:, spot] = jnp.where(lane // parents == j % pairs, mine, scale_out[:, spot])
        before(js[0] // packed, sources, at, there)
        totals = restrict(sources, at, there, down_ref)
        for j, total in zip(js, totals):
            spot = cols(j // pairs, LANES)
            right_out[:, spot] = right_out[:, spot] + pltpu.roll(total, (j % pairs) * parents, 1)
        v = js[0] // packed
        spot = cols(v // pairs, LANES, own_tiles * LANES)
        right_out[:, spot] = right_out[:, spot] + pltpu.roll(totals[-1], (v % pairs) * parents, 1)

    def before(v, all_sources, all_at, all_there):
        group = jnp.bitwise_and(lane // extra, packed - 1)
        sources = []
        start = size = head_parent = head_octant = jnp.zeros((1, LANES), jnp.int32)
        conds = jnp.ones((1, LANES), jnp.float32)
        for i in range(packed):
            j = packed * v + i
            at = j - (1 - core)
            tail = near_ref[:, pl.ds(pl.multiple_of(tails + jnp.maximum(at, 0) * LANES, LANES), LANES)]
            sources.append(jnp.where(lane < HEAD, r_ref[:, cols(j, count, 0)], tail[:modes]))
            one_size, one_start, one_cond, parent, octant = last_parents(tail, modes, parents, extra)
            mine = group == i
            size = jnp.where(jnp.logical_and(mine, at >= 0), one_size, size)
            start = jnp.where(mine, one_start, start)
            conds = jnp.where(jnp.logical_and(mine, lane < parents), one_cond, conds)
            here = lane // HEAD == j % heads
            head_parent = jnp.where(here, parent + (v % pairs) * parents + i * extra, head_parent)
            head_octant = jnp.where(here, octant, head_octant)
        octants = [pairs * i + lane // parents for i in range(OCTANTS // pairs)]
        all_sources.append(sources)
        all_at.append([jnp.where(octant < size, group, -1) for octant in octants])
        all_there.append([jnp.bitwise_and(start + octant + HEAD, LANES - 1) for octant in octants])
        spot = cols(v // pairs, LANES, own_tiles * LANES)
        conds = pltpu.roll(jnp.broadcast_to(conds, (8, LANES)), (v % pairs) * parents, 1)[0:1]
        scale_out[:, spot] = jnp.where(lane // parents == v % pairs, conds, scale_out[:, spot])
        front_out[v, 0:1, :LANES] = head_parent
        front_out[v, 0:1, LANES:] = head_octant

    over_groups(blocks, body)


def coarse_kernel(
    blocks, parents, rims, right_ref, scale_ref, front_ref, r_ref, cross_ref, gather_ref, parent_ref, octant_ref,
    stiff_ref, down_ref, up_ref, c_ref, t_ref, rim_ref, face_ref, p_out, rims_out, right, scale, front, edge,
):
    modes = r_ref.shape[0]
    count = r_ref.shape[1] // blocks
    lane = lanes()
    pairs = LANES // parents
    heads = LANES // HEAD
    extra = LANES // OCTANTS
    packed = parents // extra
    chip, core = own_place()
    segment, segments = lax.axis_index("blk"), lax.axis_size("blk")
    own_tiles = blocks // pairs
    edge[...] = jnp.zeros(edge.shape, jnp.float32)
    right[...] = right_ref[...]
    scale[...] = scale_ref[...]
    front[...] = front_ref[...]

    cross = cross_ref[...]
    size, start, conds, parent, octant = last_parents(cross, modes, parents, extra)
    above = jnp.where(jnp.logical_and(lane < HEAD, segment < segments - 1), cross[:modes], 0.0)
    below = jnp.where(lane < HEAD, r_ref[:, :LANES], cross[:modes])
    below = jnp.where(segment == 0, 0.0, below)
    at, there = [], []
    for i in range(OCTANTS // pairs):
        place = gather_ref[i : i + 1, cols(blocks - 1, LANES)]
        one = pairs * i + lane // parents
        inside = jnp.logical_and(place >= 0, place < HEAD)
        mine = jnp.logical_and(jnp.bitwise_and(lane, parents - 1) < extra, one < size)
        at.append(jnp.where(core == 1, jnp.where(inside, 0, -1), jnp.where(mine, 0, -1)))
        there.append(jnp.bitwise_and(jnp.where(core == 1, place, start + one + HEAD), LANES - 1))
    (added,) = restrict([[jnp.where(core == 1, above, below)]], [at], [there], down_ref)
    spot = cols((blocks - 1) // pairs, LANES)
    moved = pltpu.roll(added, ((blocks - 1) % pairs) * parents, 1)
    right[:, spot] = right[:, spot] + jnp.where(core == 1, moved, 0.0)
    spot = cols(0, LANES, own_tiles * LANES)
    right[:, spot] = right[:, spot] + jnp.where(core == 0, added, 0.0)
    scale[:, spot] = jnp.where(jnp.logical_and(core == 0, lane < extra), conds, scale[:, spot])
    first = jnp.logical_and(core == 0, lane < HEAD)
    front[0, 0:1, :LANES] = jnp.where(first, parent, front[0, 0:1, :LANES])
    front[0, 0:1, LANES:] = jnp.where(first, octant, front[0, 0:1, LANES:])

    eye = lax.broadcasted_iota(jnp.int32, (modes, modes), 0) == lax.broadcasted_iota(
        jnp.int32, (modes, modes), 1
    )
    diagonal = jnp.sum(jnp.where(eye, stiff_ref[...], 0.0), axis=1, keepdims=True)
    tiles = right.shape[1] // LANES
    inverse = 1.0 / (scale[...] * diagonal + 2.0 * COUPLING)
    residual = right[...]
    p = residual * inverse * (1.0 / CENTER)
    field = p
    for ahead, correct in steps(KC - 1):
        pieces = []
        for t in range(tiles):
            here = p[:, t * LANES : (t + 1) * LANES]
            last = (parents if t < own_tiles else extra) - 1
            left = jnp.where(jnp.bitwise_and(lane, last) == 0, 0.0, pltpu.roll(here, 1, 1))
            after = jnp.where(jnp.bitwise_and(lane, last) == last, 0.0, pltpu.roll(here, LANES - 1, 1))
            pieces.append(left + after)
        sides = jnp.concatenate(pieces, axis=1)
        residual = residual - (scale[...] * product(c_ref[...], p) + COUPLING * (2.0 * p - sides))
        p = ahead * p + correct * (residual * inverse)
        field = field + p
    right[...] = field

    def prolong(js, g):
        span = cols(g, len(js) * count)
        v = js[0] // packed
        leading = take(right[:, cols(own_tiles + v // pairs, LANES)], front[v, 0:1, :LANES])
        leading_octant = jnp.broadcast_to(front[v, 0:1, LANES:], (8, LANES))
        spread, octants = [], []
        for j in js:
            parent = right[:, cols(j // pairs, LANES)]
            back = (LANES - (j % heads) * HEAD) % LANES
            for h in range(0, count, LANES):
                spot = cols(j, count, h)
                one, octant = take(parent, parent_ref[:, spot]), octant_ref[:, spot]
                if h == 0:
                    one = jnp.where(lane < HEAD, pltpu.roll(leading, back, 1), one)
                    octant = jnp.where(lane < HEAD, pltpu.roll(leading_octant, back, 1)[0:1], octant)
                spread.append(one)
                octants.append(octant)
        high, low = halves(jnp.concatenate(spread, axis=1))
        octant = jnp.concatenate(octants, axis=1)
        parts = []
        for o in range(OCTANTS):
            mine = (octant == o).astype(jnp.float32).astype(jnp.bfloat16)
            parts += [high * mine, low * mine, high * mine]
        p = jnp.dot(up_ref[...], jnp.concatenate(parts, axis=0), preferred_element_type=jnp.float32)
        p_out[:, span] = p
        for i, j in enumerate(js):
            keep_edge(j, of_block(p, i, count), rim_ref, edge, rims)

    over_groups(blocks, prolong)
    for t in range(edge.shape[1] // LANES):
        spot = slice(t * LANES, (t + 1) * LANES)
        rims_out[:, spot] = rim_traces(t_ref, edge[:, spot], face_ref[:, spot])


def spread_kernel(blocks, width, p_ref, t_ref, sub_ref, _, tr_out, subs_out):
    count = p_ref.shape[1] // blocks

    def body(js, g):
        span = cols(g, len(js) * count)
        traces = product(t_ref[...], p_ref[:, span])
        tr_out[:, span] = traces
        for i, j in enumerate(js):
            send_sub(j, trace_tiles(of_block(traces, i, count)), sub_ref, subs_out, width)

    over_groups(blocks, body)


def call(limit, kernel, outs, *args, scratch=(), hbm=False, flops=3 * 10**9):
    args = [pltpu.with_memory_space_constraint(x, pltpu.HBM) for x in args] if hbm else args
    return pl.pallas_call(
        kernel,
        out_shape=[jax.ShapeDtypeStruct(shape, kind) for shape, kind in outs],
        in_specs=[pl.BlockSpec(memory_space=pltpu.HBM if hbm else pltpu.VMEM)] * len(args),
        out_specs=[pl.BlockSpec(memory_space=pltpu.VMEM)] * len(outs),
        scratch_shapes=list(scratch),
        compiler_params=pltpu.CompilerParams(vmem_limit_bytes=limit),
        cost_estimate=pl.CostEstimate(flops=flops, bytes_accessed=1, transcendentals=0),
    )(*args)


def local(
    right_side,
    conductivity,
    material,
    stiffness,
    trace_map,
    face_neighbour,
    sub_sends,
    blk_sends,
    group_sizes,
    coarse_conductivity,
    coarse_stiffness,
    restriction,
):
    f32, i32, bf16 = jnp.float32, jnp.int32, jnp.bfloat16
    modes, count = right_side.shape
    rows = trace_map.shape[0]
    points = rows // FACES
    peers, segments = lax.axis_size("sub"), lax.axis_size("blk")
    blocks = peers // CORES
    parents = group_sizes.shape[1]
    width, rims = sub_sends.shape[1], blk_sends.shape[1]
    total = blocks * count
    limit = (4 << 20) if blocks <= 4 else (40 << 20)
    run = functools.partial(call, limit)

    def pad(size, to):
        return -(-size // to) * to

    rim_width = pad(blocks * rims, LANES)
    near_width = pad(blocks * HEAD, LANES) + blocks * LANES
    field = ((modes, total), f32)
    block = ((modes, count), f32)
    sends = [((rows, total), f32), ((points, blocks * width), f32), ((points, rim_width), f32)]

    def everywhere(partner):
        pairs = []
        for b in range(segments):
            for s in range(peers):
                other_b, other_s = partner(b, s)
                pairs.append((b * peers + s, other_b * peers + other_s))
        return pairs

    def above_or_below(first):
        def partner(b, s):
            other = b + 1 if b % 2 == first else b - 1
            return (other, s) if 0 <= other < segments else (b, s ^ 1)

        return everywhere(partner)

    def crossing(b, s):
        other = b - 1 if s % 2 == 0 else b + 1
        return (other, s ^ 1) if 0 <= other < segments else (b, s ^ 2)

    both = ("blk", "sub")
    cores = [(s, s ^ 1) for s in range(peers)]
    ones, twos, crossings = above_or_below(0), above_or_below(1), everywhere(crossing)

    def over_segments(rim):
        return lax.ppermute(rim, both, ones), lax.ppermute(rim, both, twos)

    map_t = trace_map.T
    t3, tt3, k3 = run(
        prep_kernel,
        [((rows, 3 * modes), bf16), ((2 * modes, 2 * rows), bf16), ((2 * modes, 3 * modes), bf16)],
        map_t, stiffness,
    )
    down3, up3, c3 = run(
        prep_coarse_kernel,
        [((LANES // parents * modes, OCTANTS * parents // LANES * 3 * modes), bf16), ((modes, OCTANTS * 3 * modes), bf16), ((modes, 3 * modes), bf16)],
        restriction, coarse_stiffness,
    )

    height = pad(modes + 11 + pad(width, count) // count, 8)
    inputs = [
        right_side, conductivity.reshape(1, count), material.reshape(1, count), face_neighbour, sub_sends, blk_sends,
        group_sizes, coarse_conductivity.reshape(1, -1),
    ]
    (packed,) = run(
        pack_kernel,
        [((height, count), f32)],
        *inputs,
        scratch=[pltpu.VMEM(x.shape, x.dtype) for x in inputs] + [pltpu.SemaphoreType.DMA((len(inputs),))],
        hbm=True,
    )
    gathered = [packed] + [
        lax.ppermute(packed, "sub", [(s, s ^ (CORES * k)) for s in range(peers)]) for k in range(1, blocks)
    ]
    b, inverse, meta, lane, at, far, edge, subs, rim, sizes, coarse_cond, rim_face, p, rim_out = run(
        functools.partial(start_kernel, blocks, width, rims),
        [
            field, field, ((8, total), f32), *[((8, total), i32)] * 4,
            ((1, blocks * width), i32), ((1, rim_width), i32), ((blocks, LANES), i32), ((blocks, LANES), f32),
            ((1, rim_width), i32), field, sends[2],
        ],
        *gathered, stiffness, map_t, t3, c3,
        scratch=[pltpu.VMEM((blocks, height, count), f32), pltpu.VMEM((modes, rim_width), f32)],
    )
    traces, sub_out = run(functools.partial(spread_kernel, blocks, width), sends[:2], p, t3, subs, rim_out)

    edges, igs = run(
        functools.partial(rim_kernel, blocks, rims), [((8, rim_width), i32), ((modes, rim_width), f32)], rim, edge, inverse
    )
    gather, parent, octant = run(
        functools.partial(layout_kernel, blocks, parents),
        [((OCTANTS * parents // LANES, blocks * LANES), i32), ((1, total), i32), ((1, total), i32)],
        sizes,
        flops=3 * 10**10,
    )
    def apply(kind, coefficients, r, p, traces, sub_out, rim_out, x):
        one, two = over_segments(rim_out)
        swapped = lax.ppermute(sub_out, "sub", cores)
        only_own = kind == "last"
        size = count if only_own else total
        part, col = ((modes, size), f32), ((rows, size), f32)
        jump, own, x = run(
            functools.partial(local_kernel, only_own, blocks, width, x is None),
            [col, part, block],
            p, traces, meta, lane, at, k3, *([] if x is None else [x]),
        )
        goes_on = kind in ("step", "first")
        kernel = functools.partial(ahead_kernel, kind, coefficients, blocks, width, rims)
        args = [r, jump, own, sub_out, swapped, far, tt3] + ([p] if kind == "step" else [])
        if not goes_on:
            (r,) = run(kernel, [part], *args)
            finish = functools.partial(finish_kernel, kind, None, blocks, width, rims)
            args = [r, one, two, edge, tt3]
            if only_own:
                return *run(finish, [block], *args), x
            args += [sizes, coarse_cond]
            (cross,) = run(functools.partial(cross_kernel, blocks, rims), [((modes + 8, LANES), f32)], *args)
            return *run(finish, [field, ((modes + 8, near_width), f32)], *args, cross), cross, x
        r, p, p_edge = run(kernel, [field, field, ((modes, rim_width), f32)], *args, inverse, rim)
        rate = coefficients[1]
        (rim_out,) = run(
            functools.partial(edge_kernel, rate, rims), [((points, rim_width), f32)],
            one, two, edges, igs, p_edge, tt3, t3, rim_face,
        )
        r, p, traces, sub_out = run(
            functools.partial(finish_kernel, kind, rate, blocks, width, rims),
            [field, field, ((rows, total), f32), ((points, blocks * width), f32)],
            r, one, two, edge, tt3, p, inverse, t3, subs, rim_out,
        )
        return r, p, traces, sub_out, rim_out, x

    x = None
    r = b
    pairs = steps(KF)
    for step in range(KF - 1):
        r, p, traces, sub_out, rim_out, x = apply("step", pairs[step], r, p, traces, sub_out, rim_out, x)
    r, near, cross, x = apply("frame", None, r, p, traces, sub_out, rim_out, x)

    cross = lax.ppermute(cross, both, crossings)
    near = lax.ppermute(near, "sub", cores)
    coarse_width = blocks * parents + pad(blocks * LANES // OCTANTS, LANES)
    front = ((blocks * LANES // OCTANTS // parents, 8, 2 * LANES), i32)
    right, scale, leading = run(
        functools.partial(restrict_kernel, blocks, parents),
        [((modes, coarse_width), f32), ((1, coarse_width), f32), front],
        r, near, gather, coarse_cond, down3,
        flops=10**8,
    )
    p, rim_out = run(
        functools.partial(coarse_kernel, blocks, parents, rims),
        [field, sends[2]],
        right, scale, leading, r, cross, gather, parent, octant, coarse_stiffness, down3, up3, c3, t3, rim, rim_face,
        scratch=[
            pltpu.VMEM((modes, coarse_width), f32),
            pltpu.VMEM((1, coarse_width), f32),
            pltpu.VMEM(*front),
            pltpu.VMEM((modes, rim_width), f32),
        ],
    )
    traces, sub_out = run(functools.partial(spread_kernel, blocks, width), sends[:2], p, t3, subs, rim_out)
    r, p, traces, sub_out, rim_out, x = apply("first", (0.0, 1.0 / CENTER), r, p, traces, sub_out, rim_out, x)
    for step in range(KF - 1):
        r, p, traces, sub_out, rim_out, x = apply("step", pairs[step], r, p, traces, sub_out, rim_out, x)
    residual, x = apply("last", None, r, p, traces, sub_out, rim_out, x)
    return x, residual


def solution(mesh):
    in_specs = (
        P(None, ("blk", "sub")),
        P(("blk", "sub")),
        P(("blk", "sub")),
        P(),
        P(),
        P(None, ("blk", "sub")),
        P(("blk", "sub"), None),
        P(("blk", "sub"), None),
        P(("blk", "sub"), None),
        P(("blk", "sub")),
        P(),
        P(),
    )
    out_specs = (P(None, ("blk", "sub")), P(None, ("blk", "sub")))
    return jax.shard_map(local, mesh=mesh, in_specs=in_specs, out_specs=out_specs, check_vma=False)
```

```python
import functools

import jax
import jax.numpy as jnp
from jax import lax
from jax.experimental import pallas as pl
from jax.experimental.pallas import tpu as pltpu
from jax.sharding import PartitionSpec as P

HEAD = 8
KF = 3
KC = 4
FACES = 6
OCTANTS = 8
LANES = 128
CORES = 2

PENALTY = 0.3
COUPLING = 0.5
LOW_EIG = 0.4
HIGH_EIG = 2.5
CENTER = 0.5 * (HIGH_EIG + LOW_EIG)
HALF = 0.5 * (HIGH_EIG - LOW_EIG)


def steps(sweeps):
    sigma = CENTER / HALF
    rho, pairs = 1.0 / sigma, []
    for _ in range(sweeps):
        rho_next = 1.0 / (2.0 * sigma - rho)
        pairs.append((rho_next * rho, 2.0 * rho_next / HALF))
        rho = rho_next
    return pairs


def halves(x):
    high = x.astype(jnp.bfloat16)
    return high, (x - high.astype(jnp.float32)).astype(jnp.bfloat16)


def product(left, x):
    high, low = halves(x)
    right = jnp.concatenate([high, low, high], axis=0)
    return jnp.dot(left, right, preferred_element_type=jnp.float32)


def face_product(left, x):
    high, low = halves(x)
    both = jnp.dot(left, jnp.concatenate([high, low], axis=0), preferred_element_type=jnp.float32)
    modes = both.shape[0] // 2
    return both[:modes] + both[modes:]


def store_left(out, rows, x, base=0):
    high, low = halves(x)
    width = x.shape[1]
    for place, piece in enumerate((high, high, low)):
        out[rows, base + place * width : base + (place + 1) * width] = piece


def take(tile, lane):
    index = jnp.broadcast_to(lane, tile.shape)
    return jnp.take_along_axis(tile, index, axis=1, mode="promise_in_bounds")


def pick(tiles, at, lane):
    out = jnp.zeros(tiles[0].shape, tiles[0].dtype)
    for number, tile in enumerate(tiles):
        out = jnp.where(at == number, take(tile, lane), out)
    return out


def lanes(rows=1):
    return lax.broadcasted_iota(jnp.int32, (rows, LANES), 1)


def cols(j, width, base=None):
    size, start = (width, j * width) if base is None else (LANES, j * width + base)
    return pl.ds(start if isinstance(j, int) else pl.multiple_of(start, LANES), size)


def over(blocks, body):
    if blocks <= 4:
        for j in range(blocks):
            body(j)
    else:
        lax.fori_loop(0, blocks, lambda j, carry: (body(j), carry)[1], 0)


def over_groups(blocks, body):
    size = min(blocks, 4)
    over(blocks // size, lambda g: body([g * size + i for i in range(size)], g))


def own_place():
    me = lax.axis_index("sub")
    return jnp.right_shift(me, 1), jnp.bitwise_and(me, 1)


def trace_tiles(traces):
    points = traces.shape[0] // FACES
    return [
        traces[f * points : (f + 1) * points, h : h + LANES]
        for f in range(FACES)
        for h in range(0, traces.shape[1], LANES)
    ]


def faces(tile_of, js, count):
    return jnp.concatenate(
        [
            jnp.concatenate([tile_of(j, f, h) for j in js for h in range(0, count, LANES)], axis=1)
            for f in range(FACES)
        ],
        axis=0,
    )


def of_block(x, i, count):
    return x[:, i * count : (i + 1) * count]


def send_sub(j, tiles, sub_ref, sub_out, width):
    for h in range(0, width, LANES):
        columns = sub_ref[:, cols(j, width, h)]
        sub_out[:, cols(j, width, h)] = pick(
            tiles, jnp.right_shift(columns, 7), jnp.bitwise_and(columns, LANES - 1)
        )


def send_rim(j, tiles, rim_ref, rim_out, rims):
    group = LANES // rims
    tile = cols(j // group, LANES)
    columns = rim_ref[:, tile]
    rim = pick(tiles, jnp.right_shift(columns, 7), jnp.bitwise_and(columns, LANES - 1))
    mine = lanes() // rims == j % group
    rim_out[:, tile] = jnp.where(mine, rim, rim_out[:, tile])


def prep_kernel(map_ref, stiff_ref, t_out, tt_out, k_out):
    modes, rows = map_ref.shape
    transposed = map_ref[...]
    high, low = halves(PENALTY * transposed)
    tt_out[:modes, :rows] = high
    tt_out[:modes, rows:] = high
    tt_out[modes:, :rows] = low
    tt_out[modes:, rows:] = jnp.zeros((modes, rows), jnp.bfloat16)
    store_left(t_out, slice(0, rows), transposed.T)
    for k in range(2):
        store_left(k_out, slice(k * modes, (k + 1) * modes), stiff_ref[k])


def prep_coarse_kernel(restriction_ref, stiff_ref, down_out, up_out, c_out):
    modes = stiff_ref.shape[0]
    store_left(c_out, slice(0, modes), stiff_ref[...])
    pairs = down_out.shape[0] // modes
    for o in range(OCTANTS):
        rows = slice(o % pairs * modes, (o % pairs + 1) * modes)
        store_left(down_out, rows, restriction_ref[o], o // pairs * 3 * modes)
        store_left(up_out, slice(0, modes), restriction_ref[o].T, o * 3 * modes)


def pack_kernel(
    b_ref, cond_ref, mat_ref, face_ref, sub_ref, rim_ref, size_ref, coarse_ref, out,
    b_in, cond_in, mat_in, face_in, sub_in, rim_in, size_in, coarse_in, done,
):
    sources = (b_ref, cond_ref, mat_ref, face_ref, sub_ref, rim_ref, size_ref, coarse_ref)
    places = (b_in, cond_in, mat_in, face_in, sub_in, rim_in, size_in, coarse_in)
    copies = [
        pltpu.make_async_copy(source, place, done.at[at])
        for at, (source, place) in enumerate(zip(sources, places))
    ]
    for copy in copies:
        copy.start()
    modes, count = b_in.shape
    out[modes:, :] = jnp.zeros((out.shape[0] - modes, count), jnp.float32)
    for copy in copies:
        copy.wait()
    out[:modes, :] = b_in[...]
    out[modes : modes + 1, :] = cond_in[...]
    out[modes + 1 : modes + 2, :] = mat_in[...].astype(jnp.float32)
    out[modes + 2 : modes + 8, :] = face_in[...].astype(jnp.float32)
    out[modes + 8 : modes + 9, : rim_in.shape[1]] = rim_in[...].astype(jnp.float32)
    out[modes + 9 : modes + 10, : size_in.shape[1]] = size_in[...].astype(jnp.float32)
    out[modes + 10 : modes + 11, : coarse_in.shape[1]] = coarse_in[...]
    width = sub_in.shape[1]
    for at, h in enumerate(range(0, width, count)):
        piece = sub_in[:, h : min(h + count, width)].astype(jnp.float32)
        out[modes + 11 + at : modes + 12 + at, : piece.shape[1]] = piece


def start_kernel(blocks, width, rims, *refs):
    gathered, refs = refs[:blocks], refs[blocks:]
    stiff_ref, map_ref, t_ref, _ = refs[:4]
    b_out, ig_out, meta_out, lane_out, at_out, far_out, edge_out, sub_out, rim_out, size_out, coarse_out = refs[4:15]
    face_out, p_out, rims_out, held, edge = refs[15:]
    modes, count = map_ref.shape[0], gathered[0].shape[1]
    chip, core = own_place()
    for k, ref in enumerate(gathered):
        held[jnp.bitwise_xor(chip, (blocks - k) % blocks)] = ref[...]
    eye = lax.broadcasted_iota(jnp.int32, (modes, modes), 0) == lax.broadcasted_iota(
        jnp.int32, (modes, modes), 1
    )
    diagonals = [
        jnp.sum(jnp.where(eye, stiff_ref[k], 0.0), axis=1, keepdims=True) for k in range(2)
    ]
    squares = PENALTY * jnp.sum(map_ref[...] * map_ref[...], axis=1, keepdims=True)
    own_tiles = FACES * count // LANES
    sub_tiles = width // LANES
    rim_out[...] = jnp.zeros(rim_out.shape, jnp.int32)
    group = LANES // rims

    def body(j):
        b = held[j, :modes, :]
        cond = held[j, modes : modes + 1, :]
        mat = held[j, modes + 1 : modes + 2, :]
        b_out[:, cols(j, count)] = b
        meta_out[0:1, cols(j, count)] = cond
        meta_out[1:2, cols(j, count)] = mat
        column = held[j, modes + 2 : modes + 8, :].astype(jnp.int32)
        lane = jnp.bitwise_and(column, LANES - 1)
        at = jnp.right_shift(column, 7)
        lane_out[0:FACES, cols(j, count)] = lane
        at_out[0:FACES, cols(j, count)] = at
        rim = jnp.logical_and(at == own_tiles + sub_tiles, lane < rims)
        sub = jnp.logical_and(at >= own_tiles, at < own_tiles + sub_tiles)
        far_out[0:FACES, cols(j, count)] = jnp.where(sub, column - own_tiles * LANES, -1)
        edge_out[0:FACES, cols(j, count)] = jnp.where(
            rim, jnp.bitwise_xor(lane, rims // 2) + (j % group) * rims, -1
        )
        for h in range(0, width, LANES):
            row = modes + 11 + h // count
            piece = held[j, row : row + 1, h % count : h % count + LANES]
            sub_out[:, cols(j, width, h)] = piece.astype(jnp.int32)
        row = jnp.broadcast_to(held[j, modes + 8 : modes + 9, :LANES], (8, LANES))
        row = pltpu.roll(row, (j % group) * rims, 1)[0:1].astype(jnp.int32)
        tile = cols(j // group, LANES)
        rim_out[:, tile] = jnp.where(lanes() // rims == j % group, row, rim_out[:, tile])
        size_out[pl.ds(j, 1), :] = held[j, modes + 9 : modes + 10, :LANES].astype(jnp.int32)
        coarse_out[pl.ds(j, 1), :] = held[j, modes + 10 : modes + 11, :LANES]
        inverse = 1.0 / (cond * jnp.where(mat == 1.0, diagonals[1], diagonals[0]) + squares)
        ig_out[:, cols(j, count)] = inverse
        p_out[:, cols(j, count)] = b * inverse * (1.0 / CENTER)

    over(blocks, body)
    spot = lax.broadcasted_iota(jnp.int32, rim_out.shape, 1)
    face_out[...] = jnp.where(spot < blocks * rims, lax.div(rim_out[...], jnp.int32(count)), -1)
    edge[...] = jnp.zeros(edge.shape, jnp.float32)
    over(blocks, lambda j: keep_edge(j, p_out[:, cols(j, count)], rim_out, edge, rims))
    rims_out[...] = rim_traces(t_ref, edge[...], face_out[...])


def sub_tiles_of(j, sends_refs, core, width, blocks):
    slots = width // (blocks * CORES)
    pairs = LANES // slots // CORES
    lane = lanes()
    mine = lax.axis_index("sub") % CORES
    source = (CORES * (j % pairs) + mine) * slots + lane % slots
    tiles = []
    for t in range(width // LANES):
        tile = None
        for i in range(pairs):
            for ref, sender in zip(sends_refs, (core, 1 - core)):
                there = take(ref[:, cols(j // pairs, LANES, (pairs * t + i) * width)], source)
                tile = there if tile is None else jnp.where(lane // slots == CORES * i + sender, there, tile)
        tiles.append(tile)
    return tiles


def rim_element(columns, count):
    return jnp.bitwise_and(jnp.right_shift(columns, 7), count // LANES - 1), jnp.bitwise_and(columns, LANES - 1)


def local_kernel(only_own, blocks, width, first, *refs):
    p_ref, tr_ref, meta_ref, lane_ref, at_ref, k_ref = refs[:6]
    refs = refs[6:]
    if not first:
        x_ref, refs = refs[0], refs[1:]
    jump_out, own_out, x_out = refs
    modes = p_ref.shape[0]
    chip, core = own_place()
    count = x_out.shape[1]

    def body(js, span, out):
        traces = tr_ref[:, span]
        at_rows, lane_rows = at_ref[:, span], lane_ref[:, span]
        tiles = [
            trace_tiles(of_block(traces, i, count)) for i in range(len(js))
        ]

        def tile(i, f, h):
            row, place = slice(f, f + 1), slice(i * count + h, i * count + h + LANES)
            return pick(tiles[i], at_rows[row, place], lane_rows[row, place])

        jump_out[:, out] = traces - faces(tile, range(len(js)), count)
        both = product(k_ref[...], p_ref[:, span])
        meta = meta_ref[:, span]
        own_out[:, out] = meta[0:1] * jnp.where(meta[1:2] == 1.0, both[modes:], both[:modes])

    if only_own:
        body([chip], cols(chip, count), slice(0, count))
    else:
        over_groups(blocks, lambda js, g: body(js, cols(g, len(js) * count), cols(g, len(js) * count)))
    p = p_ref[:, cols(chip, count)]
    x_out[...] = p if first else x_ref[...] + p


def ahead_kernel(kind, coefficients, blocks, width, rims, *refs):
    r_ref, jump_ref, own_ref, subs_ref, swapped_ref, far_ref, tt_ref = refs[:7]
    refs = list(refs[7:])
    chip, core = own_place()
    count = own_ref.shape[1] // (1 if kind == "last" else blocks)
    group = LANES // rims
    lane = lanes()
    p_ref = refs.pop(0) if kind == "step" else None
    if kind in ("step", "first"):
        ig_ref, rim_ref, r_out, p_out, edge_out = refs
        edge_out[...] = jnp.zeros(edge_out.shape, jnp.float32)
    else:
        r_out = refs[0]

    def body(js, span, here):
        tiles = [sub_tiles_of(j, (subs_ref, swapped_ref), core, width, blocks) for j in js]
        far = far_ref[:, span]

        def tile(i, f, h):
            column = far[f : f + 1, i * count + h : i * count + h + LANES]
            return pick(tiles[i], jnp.right_shift(column, 7), jnp.bitwise_and(column, LANES - 1))

        jump = face_product(tt_ref[...], jump_ref[:, here] - faces(tile, range(len(js)), count))
        residual = r_ref[:, span] - own_ref[:, here] - jump
        r_out[:, here] = residual
        if kind in ("frame", "last"):
            return
        p = coefficients[1] * (residual * ig_ref[:, here])
        if kind == "step":
            p = p + coefficients[0] * p_ref[:, here]
        p_out[:, here] = p
        for i, j in enumerate(js):
            keep_edge(j, of_block(p, i, count), rim_ref, edge_out, rims)

    if kind == "last":
        body([chip], cols(chip, count), slice(0, count))
    else:
        over_groups(blocks, lambda js, g: body(js, cols(g, len(js) * count), cols(g, len(js) * count)))


def rim_tile(one_ref, two_ref, spot, rims):
    segment, segments = lax.axis_index("blk"), lax.axis_size("blk")
    odd = segment % 2 == 1
    low = jnp.where(odd, one_ref[:, spot], two_ref[:, spot])
    high = jnp.where(odd, two_ref[:, spot], one_ref[:, spot])
    low = jnp.where(segment == 0, 0.0, low)
    high = jnp.where(segment == segments - 1, 0.0, high)
    return jnp.where(lanes() % rims < rims // 2, high, low)


def rim_seen(rim, edge, f, h):
    place = edge[f : f + 1, h : h + LANES]
    return jnp.where(place >= 0, take(rim, jnp.bitwise_and(place, LANES - 1)), 0.0)


def keep_edge(j, p, rim_ref, edge_out, rims):
    group = LANES // rims
    spot = cols(j // group, LANES)
    count = p.shape[1]
    at, there = rim_element(rim_ref[:, spot], count)
    edge = pick([p[:, h : h + LANES] for h in range(0, count, LANES)], at, there)
    edge_out[:, spot] = jnp.where(lanes() // rims == j % group, edge, edge_out[:, spot])


def rim_traces(t_ref, p, face):
    traces = product(t_ref[...], p)
    points = traces.shape[0] // FACES
    out = jnp.zeros((points, p.shape[1]), jnp.float32)
    for f in range(FACES):
        out = jnp.where(face == f, traces[f * points : (f + 1) * points], out)
    return out


def edge_kernel(rate, rims, one_ref, two_ref, edges_ref, igs_ref, p_ref, tt_ref, t_ref, face_ref, rims_out):
    for t in range(one_ref.shape[1] // LANES):
        spot = slice(t * LANES, (t + 1) * LANES)
        rim = rim_tile(one_ref, two_ref, spot, rims)
        edge = edges_ref[:, spot]
        added = face_product(tt_ref[...], faces(lambda _, f, h: rim_seen(rim, edge, f, h), [0], LANES))
        p = p_ref[:, spot] + rate * (igs_ref[:, spot] * added)
        rims_out[:, spot] = rim_traces(t_ref, p, face_ref[:, spot])


def cross_kernel(blocks, rims, r_ref, one_ref, two_ref, edge_ref, tt_ref, size_ref, cond_ref, cross_out):
    modes = r_ref.shape[0]
    count = r_ref.shape[1] // blocks
    group = LANES // rims
    chip, core = own_place()
    last = blocks - 1
    first_tile, last_tile = cols(0, count, 0), cols(last, count, count - LANES)
    rim = jnp.where(
        core == 0,
        rim_tile(one_ref, two_ref, cols(0, LANES), rims),
        rim_tile(one_ref, two_ref, cols(last // group, LANES), rims),
    )
    edge = jnp.where(core == 0, edge_ref[:, first_tile], edge_ref[:, last_tile])
    seen = faces(lambda _, f, h: rim_seen(rim, edge, f, h), [0], LANES)
    residual = jnp.where(core == 0, r_ref[:, first_tile], r_ref[:, last_tile])
    cross_out[modes:, :] = jnp.zeros((cross_out.shape[0] - modes, LANES), jnp.float32)
    cross_out[:modes, :] = residual + face_product(tt_ref[...], seen)
    cross_out[modes : modes + 1, :] = size_ref[last : last + 1, :].astype(jnp.float32)
    cross_out[modes + 1 : modes + 2, :] = cond_ref[last : last + 1, :]


def finish_kernel(kind, rate, blocks, width, rims, *refs):
    r_ref, one_ref, two_ref, edge_ref, tt_ref = refs[:5]
    refs = list(refs[5:])
    chip, core = own_place()
    group = LANES // rims
    lane = lanes()
    if kind in ("step", "first"):
        p_ref, ig_ref, t_ref, sub_ref, _, r_out, p_out, tr_out, subs_out = refs
    elif kind == "frame":
        size_ref, cond_ref, _, r_out, near_out = refs
        near_out[...] = jnp.zeros(near_out.shape, jnp.float32)
    else:
        r_out = refs[0]
    count = r_out.shape[1] // (1 if kind == "last" else blocks)
    modes = r_ref.shape[0]

    def body(js, span, here):
        rim = [rim_tile(one_ref, two_ref, cols(j // group, LANES), rims) for j in js]
        edge = edge_ref[:, span]

        def tile(i, f, h):
            return rim_seen(rim[i], edge, f, i * count + h)

        added = face_product(tt_ref[...], faces(tile, range(len(js)), count))
        residual = r_ref[:, here] + added
        r_out[:, here] = residual
        if kind == "frame":
            heads = LANES // HEAD
            for i, j in enumerate(js):
                spot = cols(j // heads, LANES)
                mine = of_block(residual, i, count)
                moved = pltpu.roll(mine[:, :LANES], (j % heads) * HEAD, 1)
                near_out[:modes, spot] = jnp.where(lane // HEAD == j % heads, moved, near_out[:modes, spot])
                tail = cols(j, LANES, near_out.shape[1] - blocks * LANES)
                near_out[:modes, tail] = mine[:, count - LANES :]
                near_out[modes : modes + 1, tail] = size_ref[pl.ds(j, 1), :].astype(jnp.float32)
                near_out[modes + 1 : modes + 2, tail] = cond_ref[pl.ds(j, 1), :]
        if kind in ("frame", "last"):
            return
        p = p_ref[:, here] + rate * (ig_ref[:, here] * added)
        p_out[:, here] = p
        traces = product(t_ref[...], p)
        tr_out[:, here] = traces
        for i, j in enumerate(js):
            send_sub(j, trace_tiles(of_block(traces, i, count)), sub_ref, subs_out, width)

    if kind == "last":
        body([chip], cols(chip, count), slice(0, count))
    else:
        over_groups(blocks, lambda js, g: body(js, cols(g, len(js) * count), cols(g, len(js) * count)))


def layout_kernel(blocks, parents, size_ref, gather_out, parent_out, octant_out):
    lane = lanes()
    pairs = LANES // parents
    half = jnp.right_shift(lane, parents.bit_length() - 1)
    count = parent_out.shape[1] // blocks

    def body(j):
        each, end, size, start = children(size_ref[pl.ds(j, 1), :], parents, jnp.bitwise_and(lanes(parents), parents - 1))
        for i in range(OCTANTS // pairs):
            octant = pairs * i + half
            place = jnp.bitwise_and(start + octant + HEAD, count - 1)
            gather_out[i : i + 1, cols(j, LANES)] = jnp.where(octant < size, place, -1)
        for h in range(0, count, LANES):
            position = jnp.bitwise_and(lanes(parents) + (h - HEAD), count - 1)
            parent, octant = owner(each, end, position)
            parent_out[:, cols(j, count, h)] = parent + parents * (j % pairs)
            octant_out[:, cols(j, count, h)] = octant

    over(blocks, body)


def rim_kernel(blocks, rims, rim_ref, edge_ref, ig_ref, edges_out, igs_out):
    group = LANES // rims
    edges_out[...] = jnp.full(edges_out.shape, -1, jnp.int32)
    igs_out[...] = jnp.zeros(igs_out.shape, jnp.float32)
    count = ig_ref.shape[1] // blocks

    def body(j):
        tile = cols(j // group, LANES)
        mine = lanes() // rims == j % group
        at, there = rim_element(rim_ref[:, tile], count)
        edges = pick([edge_ref[:, cols(j, count, h)] for h in range(0, count, LANES)], at, there)
        igs = pick([ig_ref[:, cols(j, count, h)] for h in range(0, count, LANES)], at, there)
        edges_out[:, tile] = jnp.where(mine, edges, edges_out[:, tile])
        igs_out[:, tile] = jnp.where(mine, igs, igs_out[:, tile])

    over(blocks, body)


def children(sizes, parents, wanted):
    row = lax.broadcasted_iota(jnp.int32, (parents, LANES), 0)
    lane = lanes(parents)
    sizes = jnp.broadcast_to(sizes, (parents, LANES))
    each = jnp.sum(jnp.where(row == lane, sizes, 0), axis=1, keepdims=True)
    end = jnp.sum(jnp.where(lane <= row, sizes, 0), axis=1, keepdims=True)
    size = jnp.sum(jnp.where(row == wanted, each, 0), axis=0, keepdims=True)
    start = jnp.sum(jnp.where(row < wanted, each, 0), axis=0, keepdims=True)
    return each, end, size, start


def owner(each, end, position):
    passed = end <= position
    parent = jnp.sum(passed.astype(jnp.int32), axis=0, keepdims=True)
    return parent, position[0:1] - jnp.sum(jnp.where(passed, each, 0), axis=0, keepdims=True)


def restrict(sources, at, lane_of, down_ref):
    parts = []
    for i in range(len(at[0])):
        picked = [pick(*one) for one in zip(sources, [row[i] for row in at], [row[i] for row in lane_of])]
        high, low = halves(jnp.concatenate(picked, axis=1))
        parts += [high, low, high]
    both = jnp.dot(down_ref[...], jnp.concatenate(parts, axis=0), preferred_element_type=jnp.float32)
    modes = sources[0][0].shape[0]
    pairs = both.shape[0] // modes
    width = LANES // pairs
    totals = []
    for b in range(len(sources)):
        mine = both[:, b * LANES : (b + 1) * LANES]
        total = mine[:modes]
        for k in range(1, pairs):
            total = total + pltpu.roll(mine[k * modes : (k + 1) * modes], LANES - k * width, 1)
        totals.append(jnp.where(lanes() < width, total, 0.0))
    return totals


def last_parents(tail, modes, parents, extra):
    wanted = parents - extra + jnp.bitwise_and(lanes(parents), extra - 1)
    each, end, size, start = children(tail[modes : modes + 1].astype(jnp.int32), parents, wanted)
    rows = jnp.broadcast_to(tail[modes + 1 : modes + 2], (8, LANES))
    conds = take(rows, wanted[0:1])[0:1]
    total = jnp.sum(each, axis=0, keepdims=True)
    position = total - HEAD + jnp.bitwise_and(lanes(parents), HEAD - 1)
    parent, octant = owner(each, end, position)
    return size, start, conds, parent - (parents - extra), octant


def restrict_kernel(
    blocks, parents, r_ref, near_ref, gather_ref, cond_ref, down_ref, right_out, scale_out, front_out
):
    modes = r_ref.shape[0]
    count = r_ref.shape[1] // blocks
    lane = lanes()
    pairs = LANES // parents
    heads = LANES // HEAD
    extra = LANES // OCTANTS
    packed = parents // extra
    chip, core = own_place()
    own_tiles = blocks // pairs
    tails = near_ref.shape[1] - blocks * LANES
    right_out[...] = jnp.zeros(right_out.shape, jnp.float32)
    scale_out[...] = jnp.ones(scale_out.shape, jnp.float32)

    def body(js, g):
        sources, at, there = [], [], []
        for j in js:
            source = j + core
            tile = pl.ds(pl.multiple_of((jnp.minimum(source, blocks - 1) // heads) * LANES, LANES), LANES)
            arriving = pltpu.roll(near_ref[:modes, tile], (LANES - (source % heads) * HEAD) % LANES, 1)
            arriving = jnp.where(source < blocks, arriving, 0.0)
            own = [r_ref[:, cols(j, count, h)] for h in range(0, count, LANES)]
            sources.append([jnp.where(lane < HEAD, arriving, own[0])] + own[1:])
            places = [gather_ref[i : i + 1, cols(j, LANES)] for i in range(OCTANTS // pairs)]
            at.append([jnp.right_shift(place, 7) for place in places])
            there.append([jnp.bitwise_and(place, LANES - 1) for place in places])
            mine = jnp.broadcast_to(cond_ref[pl.ds(j, 1), :], (8, LANES))
            mine = pltpu.roll(mine, (j % pairs) * parents, 1)[0:1]
            spot = cols(j // pairs, LANES)
            scale_out[:, spot] = jnp.where(lane // parents == j % pairs, mine, scale_out[:, spot])
        before(js[0] // packed, sources, at, there)
        totals = restrict(sources, at, there, down_ref)
        for j, total in zip(js, totals):
            spot = cols(j // pairs, LANES)
            right_out[:, spot] = right_out[:, spot] + pltpu.roll(total, (j % pairs) * parents, 1)
        v = js[0] // packed
        spot = cols(v // pairs, LANES, own_tiles * LANES)
        right_out[:, spot] = right_out[:, spot] + pltpu.roll(totals[-1], (v % pairs) * parents, 1)

    def before(v, all_sources, all_at, all_there):
        group = jnp.bitwise_and(lane // extra, packed - 1)
        sources = []
        start = size = head_parent = head_octant = jnp.zeros((1, LANES), jnp.int32)
        conds = jnp.ones((1, LANES), jnp.float32)
        for i in range(packed):
            j = packed * v + i
            at = j - (1 - core)
            tail = near_ref[:, pl.ds(pl.multiple_of(tails + jnp.maximum(at, 0) * LANES, LANES), LANES)]
            sources.append(jnp.where(lane < HEAD, r_ref[:, cols(j, count, 0)], tail[:modes]))
            one_size, one_start, one_cond, parent, octant = last_parents(tail, modes, parents, extra)
            mine = group == i
            size = jnp.where(jnp.logical_and(mine, at >= 0), one_size, size)
            start = jnp.where(mine, one_start, start)
            conds = jnp.where(jnp.logical_and(mine, lane < parents), one_cond, conds)
            here = lane // HEAD == j % heads
            head_parent = jnp.where(here, parent + (v % pairs) * parents + i * extra, head_parent)
            head_octant = jnp.where(here, octant, head_octant)
        octants = [pairs * i + lane // parents for i in range(OCTANTS // pairs)]
        all_sources.append(sources)
        all_at.append([jnp.where(octant < size, group, -1) for octant in octants])
        all_there.append([jnp.bitwise_and(start + octant + HEAD, LANES - 1) for octant in octants])
        spot = cols(v // pairs, LANES, own_tiles * LANES)
        conds = pltpu.roll(jnp.broadcast_to(conds, (8, LANES)), (v % pairs) * parents, 1)[0:1]
        scale_out[:, spot] = jnp.where(lane // parents == v % pairs, conds, scale_out[:, spot])
        front_out[v, 0:1, :LANES] = head_parent
        front_out[v, 0:1, LANES:] = head_octant

    over_groups(blocks, body)


def coarse_kernel(
    blocks, parents, rims, right_ref, scale_ref, front_ref, r_ref, cross_ref, gather_ref, parent_ref, octant_ref,
    stiff_ref, down_ref, up_ref, c_ref, t_ref, rim_ref, face_ref, p_out, rims_out, right, scale, front, edge,
):
    modes = r_ref.shape[0]
    count = r_ref.shape[1] // blocks
    lane = lanes()
    pairs = LANES // parents
    heads = LANES // HEAD
    extra = LANES // OCTANTS
    packed = parents // extra
    chip, core = own_place()
    segment, segments = lax.axis_index("blk"), lax.axis_size("blk")
    own_tiles = blocks // pairs
    edge[...] = jnp.zeros(edge.shape, jnp.float32)
    right[...] = right_ref[...]
    scale[...] = scale_ref[...]
    front[...] = front_ref[...]

    cross = cross_ref[...]
    size, start, conds, parent, octant = last_parents(cross, modes, parents, extra)
    above = jnp.where(jnp.logical_and(lane < HEAD, segment < segments - 1), cross[:modes], 0.0)
    below = jnp.where(lane < HEAD, r_ref[:, :LANES], cross[:modes])
    below = jnp.where(segment == 0, 0.0, below)
    at, there = [], []
    for i in range(OCTANTS // pairs):
        place = gather_ref[i : i + 1, cols(blocks - 1, LANES)]
        one = pairs * i + lane // parents
        inside = jnp.logical_and(place >= 0, place < HEAD)
        mine = jnp.logical_and(jnp.bitwise_and(lane, parents - 1) < extra, one < size)
        at.append(jnp.where(core == 1, jnp.where(inside, 0, -1), jnp.where(mine, 0, -1)))
        there.append(jnp.bitwise_and(jnp.where(core == 1, place, start + one + HEAD), LANES - 1))
    (added,) = restrict([[jnp.where(core == 1, above, below)]], [at], [there], down_ref)
    spot = cols((blocks - 1) // pairs, LANES)
    moved = pltpu.roll(added, ((blocks - 1) % pairs) * parents, 1)
    right[:, spot] = right[:, spot] + jnp.where(core == 1, moved, 0.0)
    spot = cols(0, LANES, own_tiles * LANES)
    right[:, spot] = right[:, spot] + jnp.where(core == 0, added, 0.0)
    scale[:, spot] = jnp.where(jnp.logical_and(core == 0, lane < extra), conds, scale[:, spot])
    first = jnp.logical_and(core == 0, lane < HEAD)
    front[0, 0:1, :LANES] = jnp.where(first, parent, front[0, 0:1, :LANES])
    front[0, 0:1, LANES:] = jnp.where(first, octant, front[0, 0:1, LANES:])

    eye = lax.broadcasted_iota(jnp.int32, (modes, modes), 0) == lax.broadcasted_iota(
        jnp.int32, (modes, modes), 1
    )
    diagonal = jnp.sum(jnp.where(eye, stiff_ref[...], 0.0), axis=1, keepdims=True)
    tiles = right.shape[1] // LANES
    inverse = 1.0 / (scale[...] * diagonal + 2.0 * COUPLING)
    residual = right[...]
    p = residual * inverse * (1.0 / CENTER)
    field = p
    for ahead, correct in steps(KC - 1):
        pieces = []
        for t in range(tiles):
            here = p[:, t * LANES : (t + 1) * LANES]
            last = (parents if t < own_tiles else extra) - 1
            left = jnp.where(jnp.bitwise_and(lane, last) == 0, 0.0, pltpu.roll(here, 1, 1))
            after = jnp.where(jnp.bitwise_and(lane, last) == last, 0.0, pltpu.roll(here, LANES - 1, 1))
            pieces.append(left + after)
        sides = jnp.concatenate(pieces, axis=1)
        residual = residual - (scale[...] * product(c_ref[...], p) + COUPLING * (2.0 * p - sides))
        p = ahead * p + correct * (residual * inverse)
        field = field + p
    right[...] = field

    def prolong(js, g):
        span = cols(g, len(js) * count)
        v = js[0] // packed
        leading = take(right[:, cols(own_tiles + v // pairs, LANES)], front[v, 0:1, :LANES])
        leading_octant = jnp.broadcast_to(front[v, 0:1, LANES:], (8, LANES))
        spread, octants = [], []
        for j in js:
            parent = right[:, cols(j // pairs, LANES)]
            back = (LANES - (j % heads) * HEAD) % LANES
            for h in range(0, count, LANES):
                spot = cols(j, count, h)
                one, octant = take(parent, parent_ref[:, spot]), octant_ref[:, spot]
                if h == 0:
                    one = jnp.where(lane < HEAD, pltpu.roll(leading, back, 1), one)
                    octant = jnp.where(lane < HEAD, pltpu.roll(leading_octant, back, 1)[0:1], octant)
                spread.append(one)
                octants.append(octant)
        high, low = halves(jnp.concatenate(spread, axis=1))
        octant = jnp.concatenate(octants, axis=1)
        parts = []
        for o in range(OCTANTS):
            mine = (octant == o).astype(jnp.float32).astype(jnp.bfloat16)
            parts += [high * mine, low * mine, high * mine]
        p = jnp.dot(up_ref[...], jnp.concatenate(parts, axis=0), preferred_element_type=jnp.float32)
        p_out[:, span] = p
        for i, j in enumerate(js):
            keep_edge(j, of_block(p, i, count), rim_ref, edge, rims)

    over_groups(blocks, prolong)
    for t in range(edge.shape[1] // LANES):
        spot = slice(t * LANES, (t + 1) * LANES)
        rims_out[:, spot] = rim_traces(t_ref, edge[:, spot], face_ref[:, spot])


def spread_kernel(blocks, width, p_ref, t_ref, sub_ref, _, tr_out, subs_out):
    count = p_ref.shape[1] // blocks

    def body(js, g):
        span = cols(g, len(js) * count)
        traces = product(t_ref[...], p_ref[:, span])
        tr_out[:, span] = traces
        for i, j in enumerate(js):
            send_sub(j, trace_tiles(of_block(traces, i, count)), sub_ref, subs_out, width)

    over_groups(blocks, body)


def call(limit, kernel, outs, *args, scratch=(), hbm=False, flops=3 * 10**9):
    args = [pltpu.with_memory_space_constraint(x, pltpu.HBM) for x in args] if hbm else args
    return pl.pallas_call(
        kernel,
        out_shape=[jax.ShapeDtypeStruct(shape, kind) for shape, kind in outs],
        in_specs=[pl.BlockSpec(memory_space=pltpu.HBM if hbm else pltpu.VMEM)] * len(args),
        out_specs=[pl.BlockSpec(memory_space=pltpu.VMEM)] * len(outs),
        scratch_shapes=list(scratch),
        compiler_params=pltpu.CompilerParams(vmem_limit_bytes=limit),
        cost_estimate=pl.CostEstimate(flops=flops, bytes_accessed=1, transcendentals=0),
    )(*args)


def local(
    right_side,
    conductivity,
    material,
    stiffness,
    trace_map,
    face_neighbour,
    sub_sends,
    blk_sends,
    group_sizes,
    coarse_conductivity,
    coarse_stiffness,
    restriction,
):
    f32, i32, bf16 = jnp.float32, jnp.int32, jnp.bfloat16
    modes, count = right_side.shape
    rows = trace_map.shape[0]
    points = rows // FACES
    peers, segments = lax.axis_size("sub"), lax.axis_size("blk")
    blocks = peers // CORES
    parents = group_sizes.shape[1]
    width, rims = sub_sends.shape[1], blk_sends.shape[1]
    total = blocks * count
    limit = (4 << 20) if blocks <= 4 else (40 << 20)
    run = functools.partial(call, limit)

    def pad(size, to):
        return -(-size // to) * to

    rim_width = pad(blocks * rims, LANES)
    near_width = pad(blocks * HEAD, LANES) + blocks * LANES
    field = ((modes, total), f32)
    block = ((modes, count), f32)
    sends = [((rows, total), f32), ((points, blocks * width), f32), ((points, rim_width), f32)]

    def everywhere(partner):
        pairs = []
        for b in range(segments):
            for s in range(peers):
                other_b, other_s = partner(b, s)
                pairs.append((b * peers + s, other_b * peers + other_s))
        return pairs

    def above_or_below(first):
        def partner(b, s):
            other = b + 1 if b % 2 == first else b - 1
            return (other, s) if 0 <= other < segments else (b, s ^ 1)

        return everywhere(partner)

    def crossing(b, s):
        other = b - 1 if s % 2 == 0 else b + 1
        return (other, s ^ 1) if 0 <= other < segments else (b, s ^ 2)

    both = ("blk", "sub")
    cores = [(s, s ^ 1) for s in range(peers)]
    ones, twos, crossings = above_or_below(0), above_or_below(1), everywhere(crossing)

    def over_segments(rim):
        return lax.ppermute(rim, both, ones), lax.ppermute(rim, both, twos)

    map_t = trace_map.T
    t3, tt3, k3 = run(
        prep_kernel,
        [((rows, 3 * modes), bf16), ((2 * modes, 2 * rows), bf16), ((2 * modes, 3 * modes), bf16)],
        map_t, stiffness,
    )
    down3, up3, c3 = run(
        prep_coarse_kernel,
        [((LANES // parents * modes, OCTANTS * parents // LANES * 3 * modes), bf16), ((modes, OCTANTS * 3 * modes), bf16), ((modes, 3 * modes), bf16)],
        restriction, coarse_stiffness,
    )

    height = pad(modes + 11 + pad(width, count) // count, 8)
    inputs = [
        right_side, conductivity.reshape(1, count), material.reshape(1, count), face_neighbour, sub_sends, blk_sends,
        group_sizes, coarse_conductivity.reshape(1, -1),
    ]
    (packed,) = run(
        pack_kernel,
        [((height, count), f32)],
        *inputs,
        scratch=[pltpu.VMEM(x.shape, x.dtype) for x in inputs] + [pltpu.SemaphoreType.DMA((len(inputs),))],
        hbm=True,
    )
    gathered = [packed] + [
        lax.ppermute(packed, "sub", [(s, s ^ (CORES * k)) for s in range(peers)]) for k in range(blocks - 1, 0, -1)
    ]
    b, inverse, meta, lane, at, far, edge, subs, rim, sizes, coarse_cond, rim_face, p, rim_out = run(
        functools.partial(start_kernel, blocks, width, rims),
        [
            field, field, ((8, total), f32), *[((8, total), i32)] * 4,
            ((1, blocks * width), i32), ((1, rim_width), i32), ((blocks, LANES), i32), ((blocks, LANES), f32),
            ((1, rim_width), i32), field, sends[2],
        ],
        *gathered, stiffness, map_t, t3, c3,
        scratch=[pltpu.VMEM((blocks, height, count), f32), pltpu.VMEM((modes, rim_width), f32)],
    )
    traces, sub_out = run(functools.partial(spread_kernel, blocks, width), sends[:2], p, t3, subs, rim_out)

    edges, igs = run(
        functools.partial(rim_kernel, blocks, rims), [((8, rim_width), i32), ((modes, rim_width), f32)], rim, edge, inverse
    )
    gather, parent, octant = run(
        functools.partial(layout_kernel, blocks, parents),
        [((OCTANTS * parents // LANES, blocks * LANES), i32), ((1, total), i32), ((1, total), i32)],
        sizes,
        flops=3 * 10**10,
    )
    def apply(kind, coefficients, r, p, traces, sub_out, rim_out, x):
        one, two = over_segments(rim_out)
        swapped = lax.ppermute(sub_out, "sub", cores)
        only_own = kind == "last"
        size = count if only_own else total
        part, col = ((modes, size), f32), ((rows, size), f32)
        jump, own, x = run(
            functools.partial(local_kernel, only_own, blocks, width, x is None),
            [col, part, block],
            p, traces, meta, lane, at, k3, *([] if x is None else [x]),
        )
        goes_on = kind in ("step", "first")
        kernel = functools.partial(ahead_kernel, kind, coefficients, blocks, width, rims)
        args = [r, jump, own, sub_out, swapped, far, tt3] + ([p] if kind == "step" else [])
        if not goes_on:
            (r,) = run(kernel, [part], *args)
            finish = functools.partial(finish_kernel, kind, None, blocks, width, rims)
            args = [r, one, two, edge, tt3]
            if only_own:
                return *run(finish, [block], *args), x
            args += [sizes, coarse_cond]
            (cross,) = run(functools.partial(cross_kernel, blocks, rims), [((modes + 8, LANES), f32)], *args)
            return *run(finish, [field, ((modes + 8, near_width), f32)], *args, cross), cross, x
        r, p, p_edge = run(kernel, [field, field, ((modes, rim_width), f32)], *args, inverse, rim)
        rate = coefficients[1]
        (rim_out,) = run(
            functools.partial(edge_kernel, rate, rims), [((points, rim_width), f32)],
            one, two, edges, igs, p_edge, tt3, t3, rim_face,
        )
        r, p, traces, sub_out = run(
            functools.partial(finish_kernel, kind, rate, blocks, width, rims),
            [field, field, ((rows, total), f32), ((points, blocks * width), f32)],
            r, one, two, edge, tt3, p, inverse, t3, subs, rim_out,
        )
        return r, p, traces, sub_out, rim_out, x

    x = None
    r = b
    pairs = steps(KF)
    for step in range(KF - 1):
        r, p, traces, sub_out, rim_out, x = apply("step", pairs[step], r, p, traces, sub_out, rim_out, x)
    r, near, cross, x = apply("frame", None, r, p, traces, sub_out, rim_out, x)

    cross = lax.ppermute(cross, both, crossings)
    near = lax.ppermute(near, "sub", cores)
    coarse_width = blocks * parents + pad(blocks * LANES // OCTANTS, LANES)
    front = ((blocks * LANES // OCTANTS // parents, 8, 2 * LANES), i32)
    right, scale, leading = run(
        functools.partial(restrict_kernel, blocks, parents),
        [((modes, coarse_width), f32), ((1, coarse_width), f32), front],
        r, near, gather, coarse_cond, down3,
        flops=10**8,
    )
    p, rim_out = run(
        functools.partial(coarse_kernel, blocks, parents, rims),
        [field, sends[2]],
        right, scale, leading, r, cross, gather, parent, octant, coarse_stiffness, down3, up3, c3, t3, rim, rim_face,
        scratch=[
            pltpu.VMEM((modes, coarse_width), f32),
            pltpu.VMEM((1, coarse_width), f32),
            pltpu.VMEM(*front),
            pltpu.VMEM((modes, rim_width), f32),
        ],
    )
    traces, sub_out = run(functools.partial(spread_kernel, blocks, width), sends[:2], p, t3, subs, rim_out)
    r, p, traces, sub_out, rim_out, x = apply("first", (0.0, 1.0 / CENTER), r, p, traces, sub_out, rim_out, x)
    for step in range(KF - 1):
        r, p, traces, sub_out, rim_out, x = apply("step", pairs[step], r, p, traces, sub_out, rim_out, x)
    residual, x = apply("last", None, r, p, traces, sub_out, rim_out, x)
    return x, residual


def solution(mesh):
    in_specs = (
        P(None, ("blk", "sub")),
        P(("blk", "sub")),
        P(("blk", "sub")),
        P(),
        P(),
        P(None, ("blk", "sub")),
        P(("blk", "sub"), None),
        P(("blk", "sub"), None),
        P(("blk", "sub"), None),
        P(("blk", "sub")),
        P(),
        P(),
    )
    out_specs = (P(None, ("blk", "sub")), P(None, ("blk", "sub")))
    return jax.shard_map(local, mesh=mesh, in_specs=in_specs, out_specs=out_specs, check_vma=False)
```

```python
import functools

import jax
import jax.numpy as jnp
from jax import lax
from jax.experimental import pallas as pl
from jax.experimental.pallas import tpu as pltpu
from jax.sharding import PartitionSpec as P

HEAD = 8
KF = 3
KC = 4
FACES = 6
OCTANTS = 8
LANES = 128
CORES = 2

PENALTY = 0.3
COUPLING = 0.5
LOW_EIG = 0.4
HIGH_EIG = 2.5
CENTER = 0.5 * (HIGH_EIG + LOW_EIG)
HALF = 0.5 * (HIGH_EIG - LOW_EIG)


def steps(sweeps):
    sigma = CENTER / HALF
    rho, pairs = 1.0 / sigma, []
    for _ in range(sweeps):
        rho_next = 1.0 / (2.0 * sigma - rho)
        pairs.append((rho_next * rho, 2.0 * rho_next / HALF))
        rho = rho_next
    return pairs


def halves(x):
    high = x.astype(jnp.bfloat16)
    return high, (x - high.astype(jnp.float32)).astype(jnp.bfloat16)


def product(left, x):
    high, low = halves(x)
    right = jnp.concatenate([high, low, high], axis=0)
    return jnp.dot(left, right, preferred_element_type=jnp.float32)


def face_product(left, x):
    high, low = halves(x)
    both = jnp.dot(left, jnp.concatenate([high, low], axis=0), preferred_element_type=jnp.float32)
    modes = both.shape[0] // 2
    return both[:modes] + both[modes:]


def store_left(out, rows, x, base=0):
    high, low = halves(x)
    width = x.shape[1]
    for place, piece in enumerate((high, high, low)):
        out[rows, base + place * width : base + (place + 1) * width] = piece


def take(tile, lane):
    index = jnp.broadcast_to(lane, tile.shape)
    return jnp.take_along_axis(tile, index, axis=1, mode="promise_in_bounds")


def pick(tiles, at, lane):
    out = jnp.zeros(tiles[0].shape, tiles[0].dtype)
    for number, tile in enumerate(tiles):
        out = jnp.where(at == number, take(tile, lane), out)
    return out


def lanes(rows=1):
    return lax.broadcasted_iota(jnp.int32, (rows, LANES), 1)


def cols(j, width, base=None):
    size, start = (width, j * width) if base is None else (LANES, j * width + base)
    return pl.ds(start if isinstance(j, int) else pl.multiple_of(start, LANES), size)


def over(blocks, body):
    if blocks <= 4:
        for j in range(blocks):
            body(j)
    else:
        lax.fori_loop(0, blocks, lambda j, carry: (body(j), carry)[1], 0)


def over_groups(blocks, body):
    size = min(blocks, 4)
    over(blocks // size, lambda g: body([g * size + i for i in range(size)], g))


def own_place():
    me = lax.axis_index("sub")
    return jnp.right_shift(me, 1), jnp.bitwise_and(me, 1)


def trace_tiles(traces):
    points = traces.shape[0] // FACES
    return [
        traces[f * points : (f + 1) * points, h : h + LANES]
        for f in range(FACES)
        for h in range(0, traces.shape[1], LANES)
    ]


def faces(tile_of, js, count):
    return jnp.concatenate(
        [
            jnp.concatenate([tile_of(j, f, h) for j in js for h in range(0, count, LANES)], axis=1)
            for f in range(FACES)
        ],
        axis=0,
    )


def of_block(x, i, count):
    return x[:, i * count : (i + 1) * count]


def send_sub(j, tiles, sub_ref, sub_out, width):
    for h in range(0, width, LANES):
        columns = sub_ref[:, cols(j, width, h)]
        sub_out[:, cols(j, width, h)] = pick(
            tiles, jnp.right_shift(columns, 7), jnp.bitwise_and(columns, LANES - 1)
        )


def send_rim(j, tiles, rim_ref, rim_out, rims):
    group = LANES // rims
    tile = cols(j // group, LANES)
    columns = rim_ref[:, tile]
    rim = pick(tiles, jnp.right_shift(columns, 7), jnp.bitwise_and(columns, LANES - 1))
    mine = lanes() // rims == j % group
    rim_out[:, tile] = jnp.where(mine, rim, rim_out[:, tile])


def prep_kernel(map_ref, stiff_ref, t_out, tt_out, k_out):
    modes, rows = map_ref.shape
    transposed = map_ref[...]
    high, low = halves(PENALTY * transposed)
    tt_out[:modes, :rows] = high
    tt_out[:modes, rows:] = high
    tt_out[modes:, :rows] = low
    tt_out[modes:, rows:] = jnp.zeros((modes, rows), jnp.bfloat16)
    store_left(t_out, slice(0, rows), transposed.T)
    for k in range(2):
        store_left(k_out, slice(k * modes, (k + 1) * modes), stiff_ref[k])


def prep_coarse_kernel(restriction_ref, stiff_ref, down_out, up_out, c_out):
    modes = stiff_ref.shape[0]
    store_left(c_out, slice(0, modes), stiff_ref[...])
    pairs = down_out.shape[0] // modes
    for o in range(OCTANTS):
        rows = slice(o % pairs * modes, (o % pairs + 1) * modes)
        store_left(down_out, rows, restriction_ref[o], o // pairs * 3 * modes)
        high, low = halves(restriction_ref[o].T)
        base = o * 2 * modes
        up_out[:modes, base : base + modes] = high
        up_out[:modes, base + modes : base + 2 * modes] = high
        up_out[modes:, base : base + modes] = low
        up_out[modes:, base + modes : base + 2 * modes] = jnp.zeros((modes, modes), jnp.bfloat16)


def pack_kernel(
    b_ref, cond_ref, mat_ref, face_ref, sub_ref, rim_ref, size_ref, coarse_ref, out,
    b_in, cond_in, mat_in, face_in, sub_in, rim_in, size_in, coarse_in, done,
):
    sources = (b_ref, cond_ref, mat_ref, face_ref, sub_ref, rim_ref, size_ref, coarse_ref)
    places = (b_in, cond_in, mat_in, face_in, sub_in, rim_in, size_in, coarse_in)
    copies = [
        pltpu.make_async_copy(source, place, done.at[at])
        for at, (source, place) in enumerate(zip(sources, places))
    ]
    for copy in copies:
        copy.start()
    modes, count = b_in.shape
    out[modes:, :] = jnp.zeros((out.shape[0] - modes, count), jnp.float32)
    for copy in copies:
        copy.wait()
    out[:modes, :] = b_in[...]
    out[modes : modes + 1, :] = cond_in[...]
    out[modes + 1 : modes + 2, :] = mat_in[...].astype(jnp.float32)
    out[modes + 2 : modes + 8, :] = face_in[...].astype(jnp.float32)
    out[modes + 8 : modes + 9, : rim_in.shape[1]] = rim_in[...].astype(jnp.float32)
    out[modes + 9 : modes + 10, : size_in.shape[1]] = size_in[...].astype(jnp.float32)
    out[modes + 10 : modes + 11, : coarse_in.shape[1]] = coarse_in[...]
    width = sub_in.shape[1]
    for at, h in enumerate(range(0, width, count)):
        piece = sub_in[:, h : min(h + count, width)].astype(jnp.float32)
        out[modes + 11 + at : modes + 12 + at, : piece.shape[1]] = piece


def start_kernel(blocks, width, rims, *refs):
    gathered, refs = refs[:blocks], refs[blocks:]
    stiff_ref, map_ref, t_ref, _ = refs[:4]
    b_out, ig_out, meta_out, lane_out, at_out, far_out, edge_out, sub_out, rim_out, size_out, coarse_out = refs[4:15]
    face_out, p_out, rims_out, held, edge = refs[15:]
    modes, count = map_ref.shape[0], gathered[0].shape[1]
    chip, core = own_place()
    for k, ref in enumerate(gathered):
        held[jnp.bitwise_xor(chip, (blocks - k) % blocks)] = ref[...]
    eye = lax.broadcasted_iota(jnp.int32, (modes, modes), 0) == lax.broadcasted_iota(
        jnp.int32, (modes, modes), 1
    )
    diagonals = [
        jnp.sum(jnp.where(eye, stiff_ref[k], 0.0), axis=1, keepdims=True) for k in range(2)
    ]
    squares = PENALTY * jnp.sum(map_ref[...] * map_ref[...], axis=1, keepdims=True)
    own_tiles = FACES * count // LANES
    sub_tiles = width // LANES
    rim_out[...] = jnp.zeros(rim_out.shape, jnp.int32)
    group = LANES // rims

    def body(j):
        b = held[j, :modes, :]
        cond = held[j, modes : modes + 1, :]
        mat = held[j, modes + 1 : modes + 2, :]
        b_out[:, cols(j, count)] = b
        meta_out[0:1, cols(j, count)] = cond
        meta_out[1:2, cols(j, count)] = mat
        column = held[j, modes + 2 : modes + 8, :].astype(jnp.int32)
        lane = jnp.bitwise_and(column, LANES - 1)
        at = jnp.right_shift(column, 7)
        lane_out[0:FACES, cols(j, count)] = lane
        at_out[0:FACES, cols(j, count)] = at
        rim = jnp.logical_and(at == own_tiles + sub_tiles, lane < rims)
        sub = jnp.logical_and(at >= own_tiles, at < own_tiles + sub_tiles)
        far_out[0:FACES, cols(j, count)] = jnp.where(sub, column - own_tiles * LANES, -1)
        edge_out[0:FACES, cols(j, count)] = jnp.where(
            rim, jnp.bitwise_xor(lane, rims // 2) + (j % group) * rims, -1
        )
        for h in range(0, width, LANES):
            row = modes + 11 + h // count
            piece = held[j, row : row + 1, h % count : h % count + LANES]
            sub_out[:, cols(j, width, h)] = piece.astype(jnp.int32)
        row = jnp.broadcast_to(held[j, modes + 8 : modes + 9, :LANES], (8, LANES))
        row = pltpu.roll(row, (j % group) * rims, 1)[0:1].astype(jnp.int32)
        tile = cols(j // group, LANES)
        rim_out[:, tile] = jnp.where(lanes() // rims == j % group, row, rim_out[:, tile])
        size_out[pl.ds(j, 1), :] = held[j, modes + 9 : modes + 10, :LANES].astype(jnp.int32)
        coarse_out[pl.ds(j, 1), :] = held[j, modes + 10 : modes + 11, :LANES]
        inverse = 1.0 / (cond * jnp.where(mat == 1.0, diagonals[1], diagonals[0]) + squares)
        ig_out[:, cols(j, count)] = inverse
        p_out[:, cols(j, count)] = b * inverse * (1.0 / CENTER)

    over(blocks, body)
    spot = lax.broadcasted_iota(jnp.int32, rim_out.shape, 1)
    face_out[...] = jnp.where(spot < blocks * rims, lax.div(rim_out[...], jnp.int32(count)), -1)
    edge[...] = jnp.zeros(edge.shape, jnp.float32)
    over(blocks, lambda j: keep_edge(j, p_out[:, cols(j, count)], rim_out, edge, rims))
    rims_out[...] = rim_traces(t_ref, edge[...], face_out[...])


def sub_tiles_of(j, sends_refs, core, width, blocks):
    slots = width // (blocks * CORES)
    pairs = LANES // slots // CORES
    lane = lanes()
    mine = lax.axis_index("sub") % CORES
    source = (CORES * (j % pairs) + mine) * slots + lane % slots
    tiles = []
    for t in range(width // LANES):
        tile = None
        for i in range(pairs):
            for ref, sender in zip(sends_refs, (core, 1 - core)):
                there = take(ref[:, cols(j // pairs, LANES, (pairs * t + i) * width)], source)
                tile = there if tile is None else jnp.where(lane // slots == CORES * i + sender, there, tile)
        tiles.append(tile)
    return tiles


def rim_element(columns, count):
    return jnp.bitwise_and(jnp.right_shift(columns, 7), count // LANES - 1), jnp.bitwise_and(columns, LANES - 1)


def local_kernel(only_own, blocks, width, first, *refs):
    p_ref, tr_ref, meta_ref, lane_ref, at_ref, k_ref = refs[:6]
    refs = refs[6:]
    if not first:
        x_ref, refs = refs[0], refs[1:]
    jump_out, own_out, x_out = refs
    modes = p_ref.shape[0]
    chip, core = own_place()
    count = x_out.shape[1]

    def body(js, span, out):
        traces = tr_ref[:, span]
        at_rows, lane_rows = at_ref[:, span], lane_ref[:, span]
        tiles = [
            trace_tiles(of_block(traces, i, count)) for i in range(len(js))
        ]

        def tile(i, f, h):
            row, place = slice(f, f + 1), slice(i * count + h, i * count + h + LANES)
            return pick(tiles[i], at_rows[row, place], lane_rows[row, place])

        jump_out[:, out] = traces - faces(tile, range(len(js)), count)
        both = product(k_ref[...], p_ref[:, span])
        meta = meta_ref[:, span]
        own_out[:, out] = meta[0:1] * jnp.where(meta[1:2] == 1.0, both[modes:], both[:modes])

    if only_own:
        body([chip], cols(chip, count), slice(0, count))
    else:
        over_groups(blocks, lambda js, g: body(js, cols(g, len(js) * count), cols(g, len(js) * count)))
    p = p_ref[:, cols(chip, count)]
    x_out[...] = p if first else x_ref[...] + p


def ahead_kernel(kind, coefficients, blocks, width, rims, *refs):
    r_ref, jump_ref, own_ref, subs_ref, swapped_ref, far_ref, tt_ref = refs[:7]
    refs = list(refs[7:])
    chip, core = own_place()
    count = own_ref.shape[1] // (1 if kind == "last" else blocks)
    group = LANES // rims
    lane = lanes()
    p_ref = refs.pop(0) if kind == "step" else None
    if kind in ("step", "first"):
        ig_ref, rim_ref, r_out, p_out, edge_out = refs
        edge_out[...] = jnp.zeros(edge_out.shape, jnp.float32)
    else:
        r_out = refs[0]

    def body(js, span, here):
        tiles = [sub_tiles_of(j, (subs_ref, swapped_ref), core, width, blocks) for j in js]
        far = far_ref[:, span]

        def tile(i, f, h):
            column = far[f : f + 1, i * count + h : i * count + h + LANES]
            return pick(tiles[i], jnp.right_shift(column, 7), jnp.bitwise_and(column, LANES - 1))

        jump = face_product(tt_ref[...], jump_ref[:, here] - faces(tile, range(len(js)), count))
        residual = r_ref[:, span] - own_ref[:, here] - jump
        r_out[:, here] = residual
        if kind in ("frame", "last"):
            return
        p = coefficients[1] * (residual * ig_ref[:, here])
        if kind == "step":
            p = p + coefficients[0] * p_ref[:, here]
        p_out[:, here] = p
        for i, j in enumerate(js):
            keep_edge(j, of_block(p, i, count), rim_ref, edge_out, rims)

    if kind == "last":
        body([chip], cols(chip, count), slice(0, count))
    else:
        over_groups(blocks, lambda js, g: body(js, cols(g, len(js) * count), cols(g, len(js) * count)))


def rim_tile(one_ref, two_ref, spot, rims):
    segment, segments = lax.axis_index("blk"), lax.axis_size("blk")
    odd = segment % 2 == 1
    low = jnp.where(odd, one_ref[:, spot], two_ref[:, spot])
    high = jnp.where(odd, two_ref[:, spot], one_ref[:, spot])
    low = jnp.where(segment == 0, 0.0, low)
    high = jnp.where(segment == segments - 1, 0.0, high)
    return jnp.where(lanes() % rims < rims // 2, high, low)


def rim_seen(rim, edge, f, h):
    place = edge[f : f + 1, h : h + LANES]
    return jnp.where(place >= 0, take(rim, jnp.bitwise_and(place, LANES - 1)), 0.0)


def keep_edge(j, p, rim_ref, edge_out, rims):
    group = LANES // rims
    spot = cols(j // group, LANES)
    count = p.shape[1]
    at, there = rim_element(rim_ref[:, spot], count)
    edge = pick([p[:, h : h + LANES] for h in range(0, count, LANES)], at, there)
    edge_out[:, spot] = jnp.where(lanes() // rims == j % group, edge, edge_out[:, spot])


def rim_traces(t_ref, p, face):
    traces = product(t_ref[...], p)
    points = traces.shape[0] // FACES
    out = jnp.zeros((points, p.shape[1]), jnp.float32)
    for f in range(FACES):
        out = jnp.where(face == f, traces[f * points : (f + 1) * points], out)
    return out


def edge_kernel(rate, rims, one_ref, two_ref, edges_ref, igs_ref, p_ref, tt_ref, t_ref, face_ref, rims_out):
    for t in range(one_ref.shape[1] // LANES):
        spot = slice(t * LANES, (t + 1) * LANES)
        rim = rim_tile(one_ref, two_ref, spot, rims)
        edge = edges_ref[:, spot]
        added = face_product(tt_ref[...], faces(lambda _, f, h: rim_seen(rim, edge, f, h), [0], LANES))
        p = p_ref[:, spot] + rate * (igs_ref[:, spot] * added)
        rims_out[:, spot] = rim_traces(t_ref, p, face_ref[:, spot])


def cross_kernel(blocks, rims, r_ref, one_ref, two_ref, edge_ref, tt_ref, size_ref, cond_ref, cross_out):
    modes = r_ref.shape[0]
    count = r_ref.shape[1] // blocks
    group = LANES // rims
    chip, core = own_place()
    last = blocks - 1
    first_tile, last_tile = cols(0, count, 0), cols(last, count, count - LANES)
    rim = jnp.where(
        core == 0,
        rim_tile(one_ref, two_ref, cols(0, LANES), rims),
        rim_tile(one_ref, two_ref, cols(last // group, LANES), rims),
    )
    edge = jnp.where(core == 0, edge_ref[:, first_tile], edge_ref[:, last_tile])
    seen = faces(lambda _, f, h: rim_seen(rim, edge, f, h), [0], LANES)
    residual = jnp.where(core == 0, r_ref[:, first_tile], r_ref[:, last_tile])
    cross_out[modes:, :] = jnp.zeros((cross_out.shape[0] - modes, LANES), jnp.float32)
    cross_out[:modes, :] = residual + face_product(tt_ref[...], seen)
    cross_out[modes : modes + 1, :] = size_ref[last : last + 1, :].astype(jnp.float32)
    cross_out[modes + 1 : modes + 2, :] = cond_ref[last : last + 1, :]


def finish_kernel(kind, rate, blocks, width, rims, *refs):
    r_ref, one_ref, two_ref, edge_ref, tt_ref = refs[:5]
    refs = list(refs[5:])
    chip, core = own_place()
    group = LANES // rims
    lane = lanes()
    if kind in ("step", "first"):
        p_ref, ig_ref, t_ref, sub_ref, _, r_out, p_out, tr_out, subs_out = refs
    elif kind == "frame":
        size_ref, cond_ref, _, r_out, near_out = refs
        near_out[...] = jnp.zeros(near_out.shape, jnp.float32)
    else:
        r_out = refs[0]
    count = r_out.shape[1] // (1 if kind == "last" else blocks)
    modes = r_ref.shape[0]

    def body(js, span, here):
        rim = [rim_tile(one_ref, two_ref, cols(j // group, LANES), rims) for j in js]
        edge = edge_ref[:, span]

        def tile(i, f, h):
            return rim_seen(rim[i], edge, f, i * count + h)

        added = face_product(tt_ref[...], faces(tile, range(len(js)), count))
        residual = r_ref[:, here] + added
        r_out[:, here] = residual
        if kind == "frame":
            heads = LANES // HEAD
            for i, j in enumerate(js):
                spot = cols(j // heads, LANES)
                mine = of_block(residual, i, count)
                moved = pltpu.roll(mine[:, :LANES], (j % heads) * HEAD, 1)
                near_out[:modes, spot] = jnp.where(lane // HEAD == j % heads, moved, near_out[:modes, spot])
                tail = cols(j, LANES, near_out.shape[1] - blocks * LANES)
                near_out[:modes, tail] = mine[:, count - LANES :]
                near_out[modes : modes + 1, tail] = size_ref[pl.ds(j, 1), :].astype(jnp.float32)
                near_out[modes + 1 : modes + 2, tail] = cond_ref[pl.ds(j, 1), :]
        if kind in ("frame", "last"):
            return
        p = p_ref[:, here] + rate * (ig_ref[:, here] * added)
        p_out[:, here] = p
        traces = product(t_ref[...], p)
        tr_out[:, here] = traces
        for i, j in enumerate(js):
            send_sub(j, trace_tiles(of_block(traces, i, count)), sub_ref, subs_out, width)

    if kind == "last":
        body([chip], cols(chip, count), slice(0, count))
    else:
        over_groups(blocks, lambda js, g: body(js, cols(g, len(js) * count), cols(g, len(js) * count)))


def layout_kernel(blocks, parents, size_ref, gather_out, parent_out, octant_out):
    lane = lanes()
    pairs = LANES // parents
    half = jnp.right_shift(lane, parents.bit_length() - 1)
    count = parent_out.shape[1] // blocks

    def body(j):
        each, end, size, start = children(size_ref[pl.ds(j, 1), :], parents, jnp.bitwise_and(lanes(parents), parents - 1))
        for i in range(OCTANTS // pairs):
            octant = pairs * i + half
            place = jnp.bitwise_and(start + octant + HEAD, count - 1)
            gather_out[i : i + 1, cols(j, LANES)] = jnp.where(octant < size, place, -1)
        for h in range(0, count, LANES):
            position = jnp.bitwise_and(lanes(parents) + (h - HEAD), count - 1)
            parent, octant = owner(each, end, position)
            parent_out[:, cols(j, count, h)] = parent + parents * (j % pairs)
            octant_out[:, cols(j, count, h)] = octant

    over(blocks, body)


def rim_kernel(blocks, rims, rim_ref, edge_ref, ig_ref, edges_out, igs_out):
    group = LANES // rims
    edges_out[...] = jnp.full(edges_out.shape, -1, jnp.int32)
    igs_out[...] = jnp.zeros(igs_out.shape, jnp.float32)
    count = ig_ref.shape[1] // blocks

    def body(j):
        tile = cols(j // group, LANES)
        mine = lanes() // rims == j % group
        at, there = rim_element(rim_ref[:, tile], count)
        edges = pick([edge_ref[:, cols(j, count, h)] for h in range(0, count, LANES)], at, there)
        igs = pick([ig_ref[:, cols(j, count, h)] for h in range(0, count, LANES)], at, there)
        edges_out[:, tile] = jnp.where(mine, edges, edges_out[:, tile])
        igs_out[:, tile] = jnp.where(mine, igs, igs_out[:, tile])

    over(blocks, body)


def children(sizes, parents, wanted):
    row = lax.broadcasted_iota(jnp.int32, (parents, LANES), 0)
    lane = lanes(parents)
    sizes = jnp.broadcast_to(sizes, (parents, LANES))
    each = jnp.sum(jnp.where(row == lane, sizes, 0), axis=1, keepdims=True)
    end = jnp.sum(jnp.where(lane <= row, sizes, 0), axis=1, keepdims=True)
    size = jnp.sum(jnp.where(row == wanted, each, 0), axis=0, keepdims=True)
    start = jnp.sum(jnp.where(row < wanted, each, 0), axis=0, keepdims=True)
    return each, end, size, start


def owner(each, end, position):
    passed = end <= position
    parent = jnp.sum(passed.astype(jnp.int32), axis=0, keepdims=True)
    return parent, position[0:1] - jnp.sum(jnp.where(passed, each, 0), axis=0, keepdims=True)


def restrict(sources, at, lane_of, down_ref):
    parts = []
    for i in range(len(at[0])):
        picked = [pick(*one) for one in zip(sources, [row[i] for row in at], [row[i] for row in lane_of])]
        high, low = halves(jnp.concatenate(picked, axis=1))
        parts += [high, low, high]
    both = jnp.dot(down_ref[...], jnp.concatenate(parts, axis=0), preferred_element_type=jnp.float32)
    modes = sources[0][0].shape[0]
    pairs = both.shape[0] // modes
    width = LANES // pairs
    totals = []
    for b in range(len(sources)):
        mine = both[:, b * LANES : (b + 1) * LANES]
        total = mine[:modes]
        for k in range(1, pairs):
            total = total + pltpu.roll(mine[k * modes : (k + 1) * modes], LANES - k * width, 1)
        totals.append(jnp.where(lanes() < width, total, 0.0))
    return totals


def last_parents(tail, modes, parents, extra):
    wanted = parents - extra + jnp.bitwise_and(lanes(parents), extra - 1)
    each, end, size, start = children(tail[modes : modes + 1].astype(jnp.int32), parents, wanted)
    rows = jnp.broadcast_to(tail[modes + 1 : modes + 2], (8, LANES))
    conds = take(rows, wanted[0:1])[0:1]
    total = jnp.sum(each, axis=0, keepdims=True)
    position = total - HEAD + jnp.bitwise_and(lanes(parents), HEAD - 1)
    parent, octant = owner(each, end, position)
    return size, start, conds, parent - (parents - extra), octant


def restrict_kernel(
    blocks, parents, r_ref, near_ref, gather_ref, cond_ref, down_ref, right_out, scale_out, front_out
):
    modes = r_ref.shape[0]
    count = r_ref.shape[1] // blocks
    lane = lanes()
    pairs = LANES // parents
    heads = LANES // HEAD
    extra = LANES // OCTANTS
    packed = parents // extra
    chip, core = own_place()
    own_tiles = blocks // pairs
    tails = near_ref.shape[1] - blocks * LANES
    right_out[...] = jnp.zeros(right_out.shape, jnp.float32)
    scale_out[...] = jnp.ones(scale_out.shape, jnp.float32)

    def body(js, g):
        sources, at, there = [], [], []
        for j in js:
            source = j + core
            tile = pl.ds(pl.multiple_of((jnp.minimum(source, blocks - 1) // heads) * LANES, LANES), LANES)
            arriving = pltpu.roll(near_ref[:modes, tile], (LANES - (source % heads) * HEAD) % LANES, 1)
            arriving = jnp.where(source < blocks, arriving, 0.0)
            own = [r_ref[:, cols(j, count, h)] for h in range(0, count, LANES)]
            sources.append([jnp.where(lane < HEAD, arriving, own[0])] + own[1:])
            places = [gather_ref[i : i + 1, cols(j, LANES)] for i in range(OCTANTS // pairs)]
            at.append([jnp.right_shift(place, 7) for place in places])
            there.append([jnp.bitwise_and(place, LANES - 1) for place in places])
            mine = jnp.broadcast_to(cond_ref[pl.ds(j, 1), :], (8, LANES))
            mine = pltpu.roll(mine, (j % pairs) * parents, 1)[0:1]
            spot = cols(j // pairs, LANES)
            scale_out[:, spot] = jnp.where(lane // parents == j % pairs, mine, scale_out[:, spot])
        before(js[0] // packed, sources, at, there)
        totals = restrict(sources, at, there, down_ref)
        for j, total in zip(js, totals):
            spot = cols(j // pairs, LANES)
            right_out[:, spot] = right_out[:, spot] + pltpu.roll(total, (j % pairs) * parents, 1)
        v = js[0] // packed
        spot = cols(v // pairs, LANES, own_tiles * LANES)
        right_out[:, spot] = right_out[:, spot] + pltpu.roll(totals[-1], (v % pairs) * parents, 1)

    def before(v, all_sources, all_at, all_there):
        group = jnp.bitwise_and(lane // extra, packed - 1)
        sources = []
        start = size = head_parent = head_octant = jnp.zeros((1, LANES), jnp.int32)
        conds = jnp.ones((1, LANES), jnp.float32)
        for i in range(packed):
            j = packed * v + i
            at = j - (1 - core)
            tail = near_ref[:, pl.ds(pl.multiple_of(tails + jnp.maximum(at, 0) * LANES, LANES), LANES)]
            sources.append(jnp.where(lane < HEAD, r_ref[:, cols(j, count, 0)], tail[:modes]))
            one_size, one_start, one_cond, parent, octant = last_parents(tail, modes, parents, extra)
            mine = group == i
            size = jnp.where(jnp.logical_and(mine, at >= 0), one_size, size)
            start = jnp.where(mine, one_start, start)
            conds = jnp.where(jnp.logical_and(mine, lane < parents), one_cond, conds)
            here = lane // HEAD == j % heads
            head_parent = jnp.where(here, parent + (v % pairs) * parents + i * extra, head_parent)
            head_octant = jnp.where(here, octant, head_octant)
        octants = [pairs * i + lane // parents for i in range(OCTANTS // pairs)]
        all_sources.append(sources)
        all_at.append([jnp.where(octant < size, group, -1) for octant in octants])
        all_there.append([jnp.bitwise_and(start + octant + HEAD, LANES - 1) for octant in octants])
        spot = cols(v // pairs, LANES, own_tiles * LANES)
        conds = pltpu.roll(jnp.broadcast_to(conds, (8, LANES)), (v % pairs) * parents, 1)[0:1]
        scale_out[:, spot] = jnp.where(lane // parents == v % pairs, conds, scale_out[:, spot])
        front_out[v, 0:1, :LANES] = head_parent
        front_out[v, 0:1, LANES:] = head_octant

    over_groups(blocks, body)


def coarse_kernel(
    blocks, parents, rims, right_ref, scale_ref, front_ref, r_ref, cross_ref, gather_ref, parent_ref, octant_ref,
    stiff_ref, down_ref, up_ref, c_ref, t_ref, rim_ref, face_ref, p_out, rims_out, right, scale, front, edge,
):
    modes = r_ref.shape[0]
    count = r_ref.shape[1] // blocks
    lane = lanes()
    pairs = LANES // parents
    heads = LANES // HEAD
    extra = LANES // OCTANTS
    packed = parents // extra
    chip, core = own_place()
    segment, segments = lax.axis_index("blk"), lax.axis_size("blk")
    own_tiles = blocks // pairs
    edge[...] = jnp.zeros(edge.shape, jnp.float32)
    right[...] = right_ref[...]
    scale[...] = scale_ref[...]
    front[...] = front_ref[...]

    cross = cross_ref[...]
    size, start, conds, parent, octant = last_parents(cross, modes, parents, extra)
    above = jnp.where(jnp.logical_and(lane < HEAD, segment < segments - 1), cross[:modes], 0.0)
    below = jnp.where(lane < HEAD, r_ref[:, :LANES], cross[:modes])
    below = jnp.where(segment == 0, 0.0, below)
    at, there = [], []
    for i in range(OCTANTS // pairs):
        place = gather_ref[i : i + 1, cols(blocks - 1, LANES)]
        one = pairs * i + lane // parents
        inside = jnp.logical_and(place >= 0, place < HEAD)
        mine = jnp.logical_and(jnp.bitwise_and(lane, parents - 1) < extra, one < size)
        at.append(jnp.where(core == 1, jnp.where(inside, 0, -1), jnp.where(mine, 0, -1)))
        there.append(jnp.bitwise_and(jnp.where(core == 1, place, start + one + HEAD), LANES - 1))
    (added,) = restrict([[jnp.where(core == 1, above, below)]], [at], [there], down_ref)
    spot = cols((blocks - 1) // pairs, LANES)
    moved = pltpu.roll(added, ((blocks - 1) % pairs) * parents, 1)
    right[:, spot] = right[:, spot] + jnp.where(core == 1, moved, 0.0)
    spot = cols(0, LANES, own_tiles * LANES)
    right[:, spot] = right[:, spot] + jnp.where(core == 0, added, 0.0)
    scale[:, spot] = jnp.where(jnp.logical_and(core == 0, lane < extra), conds, scale[:, spot])
    first = jnp.logical_and(core == 0, lane < HEAD)
    front[0, 0:1, :LANES] = jnp.where(first, parent, front[0, 0:1, :LANES])
    front[0, 0:1, LANES:] = jnp.where(first, octant, front[0, 0:1, LANES:])

    eye = lax.broadcasted_iota(jnp.int32, (modes, modes), 0) == lax.broadcasted_iota(
        jnp.int32, (modes, modes), 1
    )
    diagonal = jnp.sum(jnp.where(eye, stiff_ref[...], 0.0), axis=1, keepdims=True)
    tiles = right.shape[1] // LANES
    inverse = 1.0 / (scale[...] * diagonal + 2.0 * COUPLING)
    residual = right[...]
    p = residual * inverse * (1.0 / CENTER)
    field = p
    for ahead, correct in steps(KC - 1):
        pieces = []
        for t in range(tiles):
            here = p[:, t * LANES : (t + 1) * LANES]
            last = (parents if t < own_tiles else extra) - 1
            left = jnp.where(jnp.bitwise_and(lane, last) == 0, 0.0, pltpu.roll(here, 1, 1))
            after = jnp.where(jnp.bitwise_and(lane, last) == last, 0.0, pltpu.roll(here, LANES - 1, 1))
            pieces.append(left + after)
        sides = jnp.concatenate(pieces, axis=1)
        residual = residual - (scale[...] * product(c_ref[...], p) + COUPLING * (2.0 * p - sides))
        p = ahead * p + correct * (residual * inverse)
        field = field + p
    right[...] = field

    def prolong(js, g):
        span = cols(g, len(js) * count)
        v = js[0] // packed
        leading = take(right[:, cols(own_tiles + v // pairs, LANES)], front[v, 0:1, :LANES])
        leading_octant = jnp.broadcast_to(front[v, 0:1, LANES:], (8, LANES))
        spread, octants = [], []
        for j in js:
            parent = right[:, cols(j // pairs, LANES)]
            back = (LANES - (j % heads) * HEAD) % LANES
            for h in range(0, count, LANES):
                spot = cols(j, count, h)
                one, octant = take(parent, parent_ref[:, spot]), octant_ref[:, spot]
                if h == 0:
                    one = jnp.where(lane < HEAD, pltpu.roll(leading, back, 1), one)
                    octant = jnp.where(lane < HEAD, pltpu.roll(leading_octant, back, 1)[0:1], octant)
                spread.append(one)
                octants.append(octant)
        high, low = halves(jnp.concatenate(spread, axis=1))
        octant = jnp.concatenate(octants, axis=1)
        parts = []
        for o in range(OCTANTS):
            mine = (octant == o).astype(jnp.float32).astype(jnp.bfloat16)
            parts += [high * mine, low * mine]
        both = jnp.dot(up_ref[...], jnp.concatenate(parts, axis=0), preferred_element_type=jnp.float32)
        p = both[:modes] + both[modes:]
        p_out[:, span] = p
        for i, j in enumerate(js):
            keep_edge(j, of_block(p, i, count), rim_ref, edge, rims)

    over_groups(blocks, prolong)
    for t in range(edge.shape[1] // LANES):
        spot = slice(t * LANES, (t + 1) * LANES)
        rims_out[:, spot] = rim_traces(t_ref, edge[:, spot], face_ref[:, spot])


def spread_kernel(blocks, width, p_ref, t_ref, sub_ref, _, tr_out, subs_out):
    count = p_ref.shape[1] // blocks

    def body(js, g):
        span = cols(g, len(js) * count)
        traces = product(t_ref[...], p_ref[:, span])
        tr_out[:, span] = traces
        for i, j in enumerate(js):
            send_sub(j, trace_tiles(of_block(traces, i, count)), sub_ref, subs_out, width)

    over_groups(blocks, body)


def call(limit, kernel, outs, *args, scratch=(), hbm=False, flops=3 * 10**9):
    args = [pltpu.with_memory_space_constraint(x, pltpu.HBM) for x in args] if hbm else args
    return pl.pallas_call(
        kernel,
        out_shape=[jax.ShapeDtypeStruct(shape, kind) for shape, kind in outs],
        in_specs=[pl.BlockSpec(memory_space=pltpu.HBM if hbm else pltpu.VMEM)] * len(args),
        out_specs=[pl.BlockSpec(memory_space=pltpu.VMEM)] * len(outs),
        scratch_shapes=list(scratch),
        compiler_params=pltpu.CompilerParams(vmem_limit_bytes=limit),
        cost_estimate=pl.CostEstimate(flops=flops, bytes_accessed=1, transcendentals=0),
    )(*args)


def local(
    right_side,
    conductivity,
    material,
    stiffness,
    trace_map,
    face_neighbour,
    sub_sends,
    blk_sends,
    group_sizes,
    coarse_conductivity,
    coarse_stiffness,
    restriction,
):
    f32, i32, bf16 = jnp.float32, jnp.int32, jnp.bfloat16
    modes, count = right_side.shape
    rows = trace_map.shape[0]
    points = rows // FACES
    peers, segments = lax.axis_size("sub"), lax.axis_size("blk")
    blocks = peers // CORES
    parents = group_sizes.shape[1]
    width, rims = sub_sends.shape[1], blk_sends.shape[1]
    total = blocks * count
    limit = (4 << 20) if blocks <= 4 else (40 << 20)
    run = functools.partial(call, limit)

    def pad(size, to):
        return -(-size // to) * to

    rim_width = pad(blocks * rims, LANES)
    near_width = pad(blocks * HEAD, LANES) + blocks * LANES
    field = ((modes, total), f32)
    block = ((modes, count), f32)
    sends = [((rows, total), f32), ((points, blocks * width), f32), ((points, rim_width), f32)]

    def everywhere(partner):
        pairs = []
        for b in range(segments):
            for s in range(peers):
                other_b, other_s = partner(b, s)
                pairs.append((b * peers + s, other_b * peers + other_s))
        return pairs

    def above_or_below(first):
        def partner(b, s):
            other = b + 1 if b % 2 == first else b - 1
            return (other, s) if 0 <= other < segments else (b, s ^ 1)

        return everywhere(partner)

    def crossing(b, s):
        other = b - 1 if s % 2 == 0 else b + 1
        return (other, s ^ 1) if 0 <= other < segments else (b, s ^ 2)

    both = ("blk", "sub")
    cores = [(s, s ^ 1) for s in range(peers)]
    ones, twos, crossings = above_or_below(0), above_or_below(1), everywhere(crossing)

    def over_segments(rim):
        return lax.ppermute(rim, both, ones), lax.ppermute(rim, both, twos)

    map_t = trace_map.T
    t3, tt3, k3 = run(
        prep_kernel,
        [((rows, 3 * modes), bf16), ((2 * modes, 2 * rows), bf16), ((2 * modes, 3 * modes), bf16)],
        map_t, stiffness,
    )
    down3, up3, c3 = run(
        prep_coarse_kernel,
        [((LANES // parents * modes, OCTANTS * parents // LANES * 3 * modes), bf16), ((2 * modes, OCTANTS * 2 * modes), bf16), ((modes, 3 * modes), bf16)],
        restriction, coarse_stiffness,
    )

    height = pad(modes + 11 + pad(width, count) // count, 8)
    inputs = [
        right_side, conductivity.reshape(1, count), material.reshape(1, count), face_neighbour, sub_sends, blk_sends,
        group_sizes, coarse_conductivity.reshape(1, -1),
    ]
    (packed,) = run(
        pack_kernel,
        [((height, count), f32)],
        *inputs,
        scratch=[pltpu.VMEM(x.shape, x.dtype) for x in inputs] + [pltpu.SemaphoreType.DMA((len(inputs),))],
        hbm=True,
    )
    gathered = [packed] + [
        lax.ppermute(packed, "sub", [(s, s ^ (CORES * k)) for s in range(peers)]) for k in range(blocks - 1, 0, -1)
    ]
    b, inverse, meta, lane, at, far, edge, subs, rim, sizes, coarse_cond, rim_face, p, rim_out = run(
        functools.partial(start_kernel, blocks, width, rims),
        [
            field, field, ((8, total), f32), *[((8, total), i32)] * 4,
            ((1, blocks * width), i32), ((1, rim_width), i32), ((blocks, LANES), i32), ((blocks, LANES), f32),
            ((1, rim_width), i32), field, sends[2],
        ],
        *gathered, stiffness, map_t, t3, c3,
        scratch=[pltpu.VMEM((blocks, height, count), f32), pltpu.VMEM((modes, rim_width), f32)],
    )
    traces, sub_out = run(functools.partial(spread_kernel, blocks, width), sends[:2], p, t3, subs, rim_out)

    edges, igs = run(
        functools.partial(rim_kernel, blocks, rims), [((8, rim_width), i32), ((modes, rim_width), f32)], rim, edge, inverse
    )
    gather, parent, octant = run(
        functools.partial(layout_kernel, blocks, parents),
        [((OCTANTS * parents // LANES, blocks * LANES), i32), ((1, total), i32), ((1, total), i32)],
        sizes,
        flops=3 * 10**10,
    )
    def apply(kind, coefficients, r, p, traces, sub_out, rim_out, x):
        one, two = over_segments(rim_out)
        swapped = lax.ppermute(sub_out, "sub", cores)
        only_own = kind == "last"
        size = count if only_own else total
        part, col = ((modes, size), f32), ((rows, size), f32)
        jump, own, x = run(
            functools.partial(local_kernel, only_own, blocks, width, x is None),
            [col, part, block],
            p, traces, meta, lane, at, k3, *([] if x is None else [x]),
        )
        goes_on = kind in ("step", "first")
        kernel = functools.partial(ahead_kernel, kind, coefficients, blocks, width, rims)
        args = [r, jump, own, sub_out, swapped, far, tt3] + ([p] if kind == "step" else [])
        if not goes_on:
            (r,) = run(kernel, [part], *args)
            finish = functools.partial(finish_kernel, kind, None, blocks, width, rims)
            args = [r, one, two, edge, tt3]
            if only_own:
                return *run(finish, [block], *args), x
            args += [sizes, coarse_cond]
            (cross,) = run(functools.partial(cross_kernel, blocks, rims), [((modes + 8, LANES), f32)], *args)
            return *run(finish, [field, ((modes + 8, near_width), f32)], *args, cross), cross, x
        r, p, p_edge = run(kernel, [field, field, ((modes, rim_width), f32)], *args, inverse, rim)
        rate = coefficients[1]
        (rim_out,) = run(
            functools.partial(edge_kernel, rate, rims), [((points, rim_width), f32)],
            one, two, edges, igs, p_edge, tt3, t3, rim_face,
        )
        r, p, traces, sub_out = run(
            functools.partial(finish_kernel, kind, rate, blocks, width, rims),
            [field, field, ((rows, total), f32), ((points, blocks * width), f32)],
            r, one, two, edge, tt3, p, inverse, t3, subs, rim_out,
        )
        return r, p, traces, sub_out, rim_out, x

    x = None
    r = b
    pairs = steps(KF)
    for step in range(KF - 1):
        r, p, traces, sub_out, rim_out, x = apply("step", pairs[step], r, p, traces, sub_out, rim_out, x)
    r, near, cross, x = apply("frame", None, r, p, traces, sub_out, rim_out, x)

    cross = lax.ppermute(cross, both, crossings)
    near = lax.ppermute(near, "sub", cores)
    coarse_width = blocks * parents + pad(blocks * LANES // OCTANTS, LANES)
    front = ((blocks * LANES // OCTANTS // parents, 8, 2 * LANES), i32)
    right, scale, leading = run(
        functools.partial(restrict_kernel, blocks, parents),
        [((modes, coarse_width), f32), ((1, coarse_width), f32), front],
        r, near, gather, coarse_cond, down3,
        flops=10**8,
    )
    p, rim_out = run(
        functools.partial(coarse_kernel, blocks, parents, rims),
        [field, sends[2]],
        right, scale, leading, r, cross, gather, parent, octant, coarse_stiffness, down3, up3, c3, t3, rim, rim_face,
        scratch=[
            pltpu.VMEM((modes, coarse_width), f32),
            pltpu.VMEM((1, coarse_width), f32),
            pltpu.VMEM(*front),
            pltpu.VMEM((modes, rim_width), f32),
        ],
    )
    traces, sub_out = run(functools.partial(spread_kernel, blocks, width), sends[:2], p, t3, subs, rim_out)
    r, p, traces, sub_out, rim_out, x = apply("first", (0.0, 1.0 / CENTER), r, p, traces, sub_out, rim_out, x)
    for step in range(KF - 1):
        r, p, traces, sub_out, rim_out, x = apply("step", pairs[step], r, p, traces, sub_out, rim_out, x)
    residual, x = apply("last", None, r, p, traces, sub_out, rim_out, x)
    return x, residual


def solution(mesh):
    in_specs = (
        P(None, ("blk", "sub")),
        P(("blk", "sub")),
        P(("blk", "sub")),
        P(),
        P(),
        P(None, ("blk", "sub")),
        P(("blk", "sub"), None),
        P(("blk", "sub"), None),
        P(("blk", "sub"), None),
        P(("blk", "sub")),
        P(),
        P(),
    )
    out_specs = (P(None, ("blk", "sub")), P(None, ("blk", "sub")))
    return jax.shard_map(local, mesh=mesh, in_specs=in_specs, out_specs=out_specs, check_vma=False)
```
